32 devices in a mesh: samp: 8 (over z, y), cell: 4 (over x, core).
Axes of the slice: x: 2, y: 2, z: 4, core: 2. Of those that a mesh axis runs over, the one named last changes fastest.
Arguments:
- points: float32 [24, 16384], P(None, 'samp'), may hold values from -1 to 1
- yields: bfloat16 [16384, 1024], P('samp', 'cell'), may hold values from -6 to 6
- term_index: int32 [512, 2], replicated, may hold values from 0 to 95, as said below
- block_group: int32 [8], replicated, may hold values from 0 to 7
Outputs:
- coefficients: float32 [512, 1024], P('cell')
- sobol: float32 [8, 1024], P(None, 'cell')
The draws below stay inside these ranges and needn't reach their ends.
Inputs may be any that keep to these rules, and one draw needn't show every extreme that they name: `term_index`: row 0 is 0, 0 (the constant term); every other row names one parameter with degree 1 to 3 and column 0, or two different parameters with degrees 1 to 3 each, the lower column first; no two rows are the same.
All inputs are finite; a program needn't handle non-finite values.
Results may differ from the reference program's by a relative error of at most 0.0037.
Values sent between devices are 32-bit elements; how exact they have to be, the bound alone decides.
No kernel may reach another device: no remote copies, remote signals or barrier semaphores. Data moves between devices by JAX's collectives and lax.ppermute only.
A program may use at most 64 MiB of HBM per device.

```python
import jax
import jax.numpy as jnp
import numpy as np
from jax import lax

PARAMS = 24
TERMS = 512
BLOCK = 64
GROUPS = 8
SAMP_DEV = 2048
BLOCKS = 8
CELLS = 1024
SAMPLES = 16384
N_SAMP = 8


def candidate_table():
    rows = []
    for param in range(23):
        for degree in range(1, 4):
            rows.append((4 * param + degree, 0))
    for degree in range(1, 3):
        rows.append((4 * 23 + degree, 0))
    for low in range(24):
        for high in range(low + 1, 24):
            for deg_low in range(1, 4):
                for deg_high in range(1, 4):
                    rows.append((4 * low + deg_low, 4 * high + deg_high))
    return np.array(rows, dtype=np.int32)


def draw_term_index(key, part):
    table = jnp.asarray(candidate_table())
    order = jax.random.permutation(jax.random.fold_in(key, 11), table.shape[0])
    chosen = table[order[:TERMS - 2]]
    head = jnp.array([[0, 0], [4 * PARAMS - 1, 0]], dtype=jnp.int32)
    return jnp.concatenate([head, chosen], axis=0).astype(jnp.int32)


def set_ends(values, key, smallest, high):
    extent = values.shape
    place = [jax.random.randint(jax.random.fold_in(key, axis), (), 0, extent[axis]) for axis in range(len(extent))]
    values = values.at[tuple(place)].set(smallest)
    longest = extent.index(max(extent))
    place[longest] = (place[longest] + 1) % extent[longest]
    return values.at[tuple(place)].set(high)


def block_levels(own_key, extent, cuts, smallest, high):
    gain = 1.0
    for position, blocks in cuts:
        steps = jax.random.uniform(jax.random.fold_in(jax.random.fold_in(own_key, 6), position), (blocks,), jnp.float32, smallest / len(cuts), high / len(cuts))
        gain = gain * jnp.repeat(jnp.exp(steps), extent[position] // blocks).reshape((-1,) + (1,) * (len(extent) - 1 - position))
    return gain


def scatter_about(stream_key, extent, scale, limit, cuts=(), kind=jnp.bfloat16):
    factor_of = block_levels(stream_key, extent, cuts, -0.22, 0.18) if cuts else 1.0
    values = jax.random.normal(stream_key, extent, jnp.float32) * scale * factor_of
    return jnp.minimum(jnp.maximum(values, -limit), limit).astype(kind)


def setup_inputs(seed: int = 0) -> dict:
    splits = jax.random.split(jax.random.key(seed), 5)
    points = jnp.clip(jax.random.uniform(splits[0], (PARAMS, SAMPLES), jnp.float32, -1.0, 1.0) * block_levels(splits[0], (PARAMS, SAMPLES), ((1, 8),), -0.4, 0.0), -1.0, 1.0)
    yields = scatter_about(splits[1], (SAMPLES, CELLS), 1.0, 6.0, ((0, 8), (1, 4)))
    term_index = draw_term_index(jax.random.fold_in(splits[4], 71), 0)
    block_group = set_ends(jax.random.randint(splits[3], (BLOCKS,), 0, GROUPS), jax.random.fold_in(splits[3], 1), 0, GROUPS - 1).astype(jnp.int32)
    return {"points": points, "yields": yields, "term_index": term_index, "block_group": block_group}


def basis_rows(xs):
    ones = jnp.ones_like(xs)
    first = 1.7320508075688772 * xs
    second = 2.23606797749979 * (1.5 * xs * xs - 0.5)
    third = 2.6457513110645907 * (2.5 * xs * xs * xs - 1.5 * xs)
    stacked = jnp.stack([ones, first, second, third], axis=1)
    return stacked.reshape(4 * xs.shape[0], xs.shape[1])

def design(xs, term_index):
    table = basis_rows(xs)
    columns = jnp.arange(table.shape[0], dtype=jnp.int32)
    pick_a = (term_index[:, 0:1] == columns[None, :]).astype(table.dtype)
    pick_b = (term_index[:, 1:2] == columns[None, :]).astype(table.dtype)
    left = jnp.dot(pick_a, table, precision=lax.Precision.HIGHEST)
    right = jnp.dot(pick_b, table, precision=lax.Precision.HIGHEST)
    return (left * right).astype(jnp.bfloat16)

def reference(points, yields, term_index, block_group):
    xb = points.reshape(PARAMS, N_SAMP, SAMP_DEV).transpose(1, 0, 2)
    yb = yields.reshape(N_SAMP, SAMP_DEV, CELLS)

    def accumulate(carry, item):
        gram, cross = carry
        xs, ys = item
        psi = design(xs, term_index)
        gram = gram + jnp.dot(psi.astype(jnp.float32), psi.T.astype(jnp.float32), preferred_element_type=jnp.float32)
        cross = cross + jnp.dot(psi.astype(jnp.float32), ys.astype(jnp.float32), preferred_element_type=jnp.float32)
        return ((gram, cross), None)
    start = (jnp.zeros((TERMS, TERMS), jnp.float32), jnp.zeros((TERMS, CELLS), jnp.float32))
    (gram, cross), unused = lax.scan(accumulate, start, (xb, yb))
    lower = jnp.linalg.cholesky(gram)
    inner = lax.linalg.triangular_solve(lower, cross, left_side=True, lower=True)
    coef = lax.linalg.triangular_solve(lower, inner, left_side=True, lower=True, transpose_a=True)
    coefficients = coef * jnp.sqrt(jnp.float32(SAMPLES))
    keep = (jnp.arange(TERMS) >= 1).astype(jnp.float32)
    squares = coef * coef * keep[:, None]
    groups = jnp.repeat(block_group, BLOCK)
    member = (groups[None, :] == jnp.arange(GROUPS, dtype=jnp.int32)[:, None]).astype(jnp.float32)
    part = jnp.dot(member, squares, precision=lax.Precision.HIGHEST)
    total = lax.optimization_barrier(jnp.sum(squares, axis=0))
    return (coefficients, part / total[None, :])
```

```python
import functools

import jax
import jax.numpy as jnp
from jax import lax
from jax.experimental import pallas as pl
from jax.experimental.pallas import tpu as pltpu
from jax.sharding import PartitionSpec as P

BLOCK = 64
GROUPS = 8
TILE = 128
HIGH = lax.Precision.HIGHEST


def split3(values):
    top = values.astype(jnp.bfloat16).astype(jnp.float32)
    rest = values - top
    middle = rest.astype(jnp.bfloat16).astype(jnp.float32)
    return top, middle, rest - middle


def picks(column, params, width):
    span = 3 * params
    degree = column % 4
    place = (degree - 1) * params + column // 4
    lanes = lax.broadcasted_iota(jnp.int32, (column.shape[0], width), 1)
    hit = (lanes == place) | (lanes == place + span) | (lanes == place + 2 * span)
    hit = (hit & (degree > 0)) | ((lanes == 3 * span) & (degree == 0))
    return hit.astype(jnp.float32).astype(jnp.bfloat16)


def design_kernel(chunk, cell_ref, index_ref, points_ref, psi_ref, fold_ref, table_ref):
    params, samples = points_ref.shape
    terms = index_ref.shape[0]
    width = table_ref.shape[0]
    span = 3 * params
    xs = points_ref[...]
    first = 1.7320508075688772 * xs
    second = 2.23606797749979 * (1.5 * xs * xs - 0.5)
    third = 2.6457513110645907 * (2.5 * xs * xs * xs - 1.5 * xs)
    for at, rows in enumerate((first, second, third)):
        for part, values in enumerate(split3(rows)):
            table_ref[pl.ds(part * span + at * params, params), :] = values
    table_ref[pl.ds(3 * span, width - 3 * span), :] = jnp.ones((width - 3 * span, samples), jnp.float32)
    pick_a = picks(index_ref[:, 0:1], params, width)
    pick_b = picks(index_ref[:, 1:2], params, width)
    for start in range(0, samples, chunk):
        table = table_ref[:, start:start + chunk].astype(jnp.bfloat16)
        left = jnp.dot(pick_a, table, preferred_element_type=jnp.float32)
        right = jnp.dot(pick_b, table, preferred_element_type=jnp.float32)
        psi_ref[:, start:start + chunk] = (left * right).astype(jnp.bfloat16)
    blocks = terms // TILE
    part_rows = fold_ref.shape[0] // 2
    cell = cell_ref[0]
    for block in range(blocks):
        rows = psi_ref[pl.ds(pl.multiple_of(block * TILE + cell * part_rows, part_rows), part_rows), :]
        reach = (block + 1) * TILE
        value = lax.dot_general(
            rows, psi_ref[0:reach, :], (((1,), (1,)), ((), ())), preferred_element_type=jnp.float32
        )
        half, at = fold_place(block, blocks)
        fold_ref[half * part_rows:(half + 1) * part_rows, at:at + reach] = value


def fold_place(block, blocks):
    low = min(block, blocks - 1 - block)
    return low, 0 if block == low else (low + 1) * TILE


def design(points, term_index, cell, n_cell):
    params, samples = points.shape
    terms = term_index.shape[0]
    blocks = terms // TILE
    rows = 2 * TILE // n_cell
    return pl.pallas_call(
        functools.partial(design_kernel, 512),
        out_shape=(
            jax.ShapeDtypeStruct((terms, samples), jnp.bfloat16),
            jax.ShapeDtypeStruct((rows, (blocks + 1) * TILE), jnp.float32),
        ),
        in_specs=[
            pl.BlockSpec(memory_space=pltpu.SMEM),
            pl.BlockSpec(memory_space=pltpu.VMEM),
            pl.BlockSpec(memory_space=pltpu.VMEM),
        ],
        out_specs=(pl.BlockSpec(memory_space=pltpu.VMEM),) * 2,
        scratch_shapes=[pltpu.VMEM((256, samples), jnp.float32)],
        compiler_params=pltpu.CompilerParams(vmem_limit_bytes=32 * 2**20),
        name="design",
    )(cell.reshape(1), term_index, points)


def sweep_tile(tile):
    size = tile.shape[0]
    rows = lax.broadcasted_iota(jnp.int32, tile.shape, 0)
    columns = lax.broadcasted_iota(jnp.int32, tile.shape, 1)

    def step(at, now):
        column = jnp.take_along_axis(now, jnp.full(now.shape, at, jnp.int32), axis=1)
        row = jnp.sum(jnp.where(rows == at, now, 0.0), axis=0, keepdims=True)
        pivot = jnp.sum(jnp.where(columns[0:1] == at, row, 0.0), axis=1, keepdims=True)
        inverse = 1.0 / pivot
        scaled = row * inverse
        kept = now - column * scaled
        kept = jnp.where(columns == at, column * inverse, kept)
        kept = jnp.where(rows == at, jnp.where(columns == at, -inverse, scaled), kept)
        return kept

    return lax.fori_loop(0, size, step, tile)


def inverse_kernel(parts, fold_ref, out_ref):
    terms = out_ref.shape[0]
    blocks = terms // TILE
    piece = TILE // parts
    for block in range(blocks):
        half, at = fold_place(block, blocks)
        reach = (block + 1) * TILE
        for part in range(parts):
            start = part * 2 * piece + half * piece
            out_ref[block * TILE + part * piece:block * TILE + (part + 1) * piece, 0:reach] = (
                fold_ref[start:start + piece, at:at + reach]
            )
    for block in range(blocks):
        for other in range(block):
            tile = out_ref[block * TILE:(block + 1) * TILE, other * TILE:(other + 1) * TILE]
            out_ref[other * TILE:(other + 1) * TILE, block * TILE:(block + 1) * TILE] = tile.T

    def block_step(block, carry):
        start = pl.multiple_of(block * TILE, TILE)
        band = pl.ds(start, TILE)
        minus = sweep_tile(out_ref[band, band])
        old = out_ref[band, :]
        columns = out_ref[:, band]
        fresh = -jnp.dot(minus, old, precision=HIGH, preferred_element_type=jnp.float32)
        out_ref[...] -= jnp.dot(columns, fresh, precision=HIGH, preferred_element_type=jnp.float32)
        out_ref[band, :] = fresh
        out_ref[:, band] = fresh.T
        out_ref[band, band] = minus
        return carry

    lax.fori_loop(0, blocks, block_step, 0)


def minus_inverse(fold, parts):
    terms = (fold.shape[1] // TILE - 1) * TILE
    return pl.pallas_call(
        functools.partial(inverse_kernel, parts),
        out_shape=jax.ShapeDtypeStruct((terms, terms), jnp.float32),
        in_specs=[pl.BlockSpec(memory_space=pltpu.VMEM)],
        out_specs=pl.BlockSpec(memory_space=pltpu.VMEM),
        compiler_params=pltpu.CompilerParams(vmem_limit_bytes=32 * 2**20),
        cost_estimate=pl.CostEstimate(flops=30 * 10**9, bytes_accessed=3 * 2**20, transcendentals=512),
        name="minus_inverse",
    )(fold)


def finish_kernel(samples, group_ref, inverse_ref, cross_ref, coef_ref, sobol_ref):
    terms, cells = cross_ref.shape
    coef = -jnp.dot(inverse_ref[...], cross_ref[...], precision=HIGH, preferred_element_type=jnp.float32)
    coef_ref[...] = coef * jnp.sqrt(jnp.float32(samples))
    squares = coef * coef
    keep = lax.broadcasted_iota(jnp.int32, squares.shape, 0) >= 1
    squares = jnp.where(keep, squares, 0.0)
    sums = [
        jnp.sum(squares[at:at + BLOCK], axis=0, keepdims=True) for at in range(0, terms, BLOCK)
    ]
    total = functools.reduce(jnp.add, sums)
    for group in range(GROUPS):
        part = jnp.zeros_like(total)
        for at, value in enumerate(sums):
            part = part + jnp.where(group_ref[at] == group, value, 0.0)
        sobol_ref[group:group + 1, :] = part / total


def finish(inverse, cross, block_group, samples):
    terms, cells = cross.shape
    return pl.pallas_call(
        functools.partial(finish_kernel, samples),
        out_shape=(
            jax.ShapeDtypeStruct((terms, cells), jnp.float32),
            jax.ShapeDtypeStruct((GROUPS, cells), jnp.float32),
        ),
        in_specs=[
            pl.BlockSpec(memory_space=pltpu.SMEM),
            pl.BlockSpec(memory_space=pltpu.VMEM),
            pl.BlockSpec(memory_space=pltpu.VMEM),
        ],
        out_specs=(pl.BlockSpec(memory_space=pltpu.VMEM),) * 2,
        compiler_params=pltpu.CompilerParams(vmem_limit_bytes=32 * 2**20),
        name="finish",
    )(block_group, inverse, cross)


def gather_cells(piece, n_cell):
    me = lax.axis_index("cell")
    held = piece[None]
    step = 1
    while step < n_cell:
        came = lax.ppermute(held, "cell", [(at, at ^ step) for at in range(n_cell)])
        upper = (me & step) != 0
        held = jnp.concatenate([jnp.where(upper, came, held), jnp.where(upper, held, came)], axis=0)
        step *= 2
    return held


def on_device(points, yields, term_index, block_group):
    n_samp = lax.axis_size("samp")
    n_cell = lax.axis_size("cell")
    psi, fold = design(points, term_index, lax.axis_index("cell"), n_cell)
    pieces = fold.reshape(n_samp, 8, -1)
    came = lax.all_to_all(pieces, "samp", split_axis=0, concat_axis=0)
    piece = jnp.sum(came, axis=0)
    gathered = lax.all_to_all(
        jnp.broadcast_to(piece[None], pieces.shape), "samp", split_axis=0, concat_axis=0
    )
    fold = gather_cells(gathered.reshape(fold.shape), n_cell)
    inverse = minus_inverse(fold.reshape(-1, fold.shape[-1]), n_cell)
    cross = jnp.dot(psi, yields, preferred_element_type=jnp.float32)
    cross = lax.psum(cross, "samp")
    scaled, sobol = finish(inverse, cross, block_group, points.shape[1] * n_samp)
    coefficients = lax.all_to_all(scaled, "cell", split_axis=0, concat_axis=1, tiled=True)
    return (coefficients, sobol)


def solution(mesh):
    placed = (P(None, "samp"), P("samp", "cell"), P(), P())
    return jax.shard_map(
        on_device,
        mesh=mesh,
        in_specs=placed,
        out_specs=(P("cell", None), P(None, "cell")),
        check_vma=False,
    )
```

```python
import functools

import jax
import jax.numpy as jnp
from jax import lax
from jax.experimental import pallas as pl
from jax.experimental.pallas import tpu as pltpu
from jax.sharding import PartitionSpec as P

BLOCK = 64
GROUPS = 8
TILE = 128
HIGH = lax.Precision.HIGHEST


def split3(values):
    top = values.astype(jnp.bfloat16).astype(jnp.float32)
    rest = values - top
    middle = rest.astype(jnp.bfloat16).astype(jnp.float32)
    return top, middle, rest - middle


def picks(column, params, width):
    span = 3 * params
    degree = column % 4
    place = (degree - 1) * params + column // 4
    lanes = lax.broadcasted_iota(jnp.int32, (column.shape[0], width), 1)
    hit = (lanes == place) | (lanes == place + span) | (lanes == place + 2 * span)
    hit = (hit & (degree > 0)) | ((lanes == 3 * span) & (degree == 0))
    return hit.astype(jnp.float32).astype(jnp.bfloat16)


def design_kernel(chunk, cell_ref, index_ref, points_ref, psi_ref, fold_ref, table_ref):
    params, samples = points_ref.shape
    terms = index_ref.shape[0]
    width = table_ref.shape[0]
    span = 3 * params
    xs = points_ref[...]
    first = 1.7320508075688772 * xs
    second = 2.23606797749979 * (1.5 * xs * xs - 0.5)
    third = 2.6457513110645907 * (2.5 * xs * xs * xs - 1.5 * xs)
    for at, rows in enumerate((first, second, third)):
        for part, values in enumerate(split3(rows)):
            table_ref[pl.ds(part * span + at * params, params), :] = values
    table_ref[pl.ds(3 * span, width - 3 * span), :] = jnp.ones((width - 3 * span, samples), jnp.float32)
    pick_a = picks(index_ref[:, 0:1], params, width)
    pick_b = picks(index_ref[:, 1:2], params, width)
    for start in range(0, samples, chunk):
        table = table_ref[:, start:start + chunk].astype(jnp.bfloat16)
        left = jnp.dot(pick_a, table, preferred_element_type=jnp.float32)
        right = jnp.dot(pick_b, table, preferred_element_type=jnp.float32)
        psi_ref[:, start:start + chunk] = (left * right).astype(jnp.bfloat16)
    blocks = terms // TILE
    part_rows = fold_ref.shape[0] // 2
    cell = cell_ref[0]
    for block in range(blocks):
        rows = psi_ref[pl.ds(pl.multiple_of(block * TILE + cell * part_rows, part_rows), part_rows), :]
        reach = (block + 1) * TILE
        value = lax.dot_general(
            rows, psi_ref[0:reach, :], (((1,), (1,)), ((), ())), preferred_element_type=jnp.float32
        )
        half, at = fold_place(block, blocks)
        fold_ref[half * part_rows:(half + 1) * part_rows, at:at + reach] = value


def fold_place(block, blocks):
    low = min(block, blocks - 1 - block)
    return low, 0 if block == low else (low + 1) * TILE


def design(points, term_index, cell, n_cell):
    params, samples = points.shape
    terms = term_index.shape[0]
    blocks = terms // TILE
    rows = 2 * TILE // n_cell
    return pl.pallas_call(
        functools.partial(design_kernel, 512),
        out_shape=(
            jax.ShapeDtypeStruct((terms, samples), jnp.bfloat16),
            jax.ShapeDtypeStruct((rows, (blocks + 1) * TILE), jnp.float32),
        ),
        in_specs=[
            pl.BlockSpec(memory_space=pltpu.SMEM),
            pl.BlockSpec(memory_space=pltpu.VMEM),
            pl.BlockSpec(memory_space=pltpu.VMEM),
        ],
        out_specs=(pl.BlockSpec(memory_space=pltpu.VMEM),) * 2,
        scratch_shapes=[pltpu.VMEM((256, samples), jnp.float32)],
        compiler_params=pltpu.CompilerParams(vmem_limit_bytes=32 * 2**20),
        name="design",
    )(cell.reshape(1), term_index, points)


def lane_of(values, at):
    return jnp.take_along_axis(values, jnp.full(values.shape, at, jnp.int32), axis=1)


def row_of(values, at):
    return jnp.broadcast_to(values[at:at + 1, :], values.shape)


def sweep_tile(bands):
    bands = list(bands)
    shape = bands[0].shape
    subs = lax.broadcasted_iota(jnp.int32, shape, 0)
    lanes = lax.broadcasted_iota(jnp.int32, shape, 1)
    for at in range(len(bands)):
        base = 8 * at
        own = bands[at]
        inside = (lanes >= base) & (lanes < base + 8)
        columns = [lane_of(own, base + k) for k in range(8)]
        pivot = [[row_of(columns[k], i) if k <= i else None for k in range(8)] for i in range(8)]
        edged = jnp.where(inside, jnp.where(lanes == subs + base, -1.0, 0.0), own)
        rows = [row_of(edged, i) for i in range(8)]
        factor = [[None] * 8 for _ in range(8)]
        inverse = []
        for p in range(8):
            inverse.append(1.0 / pivot[p][p])
            for i in range(p + 1, 8):
                factor[i][p] = pivot[i][p] * inverse[p]
                for k in range(p + 1, i + 1):
                    pivot[i][k] = pivot[i][k] - factor[i][p] * pivot[k][p]
                rows[i] = rows[i] - factor[i][p] * rows[p]
        rows = [rows[i] * inverse[i] for i in range(8)]
        for p in range(7, 0, -1):
            for i in range(p):
                rows[i] = rows[i] - factor[p][i] * rows[p]
        for step in range(1, len(bands)):
            other = (at + step) % len(bands)
            value = jnp.where(inside, 0.0, bands[other])
            for k in range(8):
                value = value - lane_of(bands[other], base + k) * rows[k]
            bands[other] = value
        fresh = rows[0]
        for i in range(1, 8):
            fresh = jnp.where(subs == i, rows[i], fresh)
        bands[at] = fresh
    return bands


def sweep_block(gram_ref, block):
    band = slice(block * TILE, (block + 1) * TILE)
    bands = sweep_tile(gram_ref[block * TILE + at:block * TILE + at + 8, band] for at in range(0, TILE, 8))
    minus = jnp.concatenate(bands, axis=0)
    old = gram_ref[band, :]
    columns = gram_ref[:, band]
    fresh = -jnp.dot(minus, old, precision=HIGH, preferred_element_type=jnp.float32)
    gram_ref[...] -= jnp.dot(columns, fresh, precision=HIGH, preferred_element_type=jnp.float32)
    gram_ref[band, :] = fresh
    gram_ref[:, band] = fresh.T
    gram_ref[band, band] = minus


def first_kernel(where_ref, *refs):
    out_ref = refs[-1]
    terms = out_ref.shape[0]
    blocks = terms // TILE
    at = 0
    for half_step in range(2):
        for cell_step in range(len(refs[:-1]) // 2):
            ref = refs[at]
            at += 1
            piece = ref.shape[0]
            start = pl.multiple_of((where_ref[1] ^ cell_step) * piece, piece)
            for half in range(2):
                @pl.when((where_ref[0] ^ half_step) == half)
                def _():
                    for block in (half, blocks - 1 - half):
                        reach = (block + 1) * TILE
                        lane = fold_place(block, blocks)[1]
                        out_ref[pl.ds(start + block * TILE, piece), 0:reach] = ref[:, lane:lane + reach]
    for block in range(blocks):
        for other in range(block):
            tile = out_ref[block * TILE:(block + 1) * TILE, other * TILE:(other + 1) * TILE]
            out_ref[other * TILE:(other + 1) * TILE, block * TILE:(block + 1) * TILE] = tile.T
    sweep_block(out_ref, 0)


def next_kernel(block, in_ref, out_ref):
    out_ref[...] = in_ref[...]
    sweep_block(out_ref, block)


STEP_COST = pl.CostEstimate(flops=5 * 10**9, bytes_accessed=2 * 2**20, transcendentals=512)
VMEM = pl.BlockSpec(memory_space=pltpu.VMEM)
SMEM = pl.BlockSpec(memory_space=pltpu.SMEM)
BIG = pltpu.CompilerParams(vmem_limit_bytes=32 * 2**20)


def first_block(where, pieces, terms):
    return pl.pallas_call(
        first_kernel,
        out_shape=jax.ShapeDtypeStruct((terms, terms), jnp.float32),
        in_specs=[SMEM] + [VMEM] * len(pieces),
        out_specs=VMEM,
        compiler_params=BIG,
        cost_estimate=STEP_COST,
        name="block_0",
    )(where, *pieces)


def next_block(gram, block):
    return pl.pallas_call(
        functools.partial(next_kernel, block),
        out_shape=jax.ShapeDtypeStruct(gram.shape, jnp.float32),
        in_specs=[VMEM],
        out_specs=VMEM,
        input_output_aliases={0: 0},
        compiler_params=BIG,
        cost_estimate=STEP_COST,
        name="block_%d" % block,
    )(gram)


def place_kernel(where_ref, *refs):
    out_ref = refs[-1]
    for step, ref in enumerate(refs[:-1]):
        rows = ref.shape[0]
        out_ref[pl.ds(pl.multiple_of((where_ref[0] ^ step) * rows, rows), rows), :] = ref[...]


def place_rows(where, pieces):
    rows, lanes = pieces[0].shape
    return pl.pallas_call(
        place_kernel,
        out_shape=jax.ShapeDtypeStruct((rows * len(pieces), lanes), jnp.float32),
        in_specs=[SMEM] + [VMEM] * len(pieces),
        out_specs=VMEM,
        name="place_rows",
    )(where, *pieces)


def finish_kernel(samples, n_cell, where_ref, group_ref, inverse_ref, *refs):
    pieces = refs[:-(n_cell + 3)]
    coef_refs = refs[-(n_cell + 3):-3]
    sobol_ref, cross_ref, hold_ref = refs[-3:]
    for step, ref in enumerate(pieces):
        rows = ref.shape[0]
        cross_ref[pl.ds(pl.multiple_of((where_ref[0] ^ step) * rows, rows), rows), :] = ref[...]
    terms, cells = cross_ref.shape
    coef = -jnp.dot(inverse_ref[...], cross_ref[...], precision=HIGH, preferred_element_type=jnp.float32)
    hold_ref[...] = coef * jnp.sqrt(jnp.float32(samples))
    share = terms // n_cell
    for step, ref in enumerate(coef_refs):
        ref[...] = hold_ref[pl.ds(pl.multiple_of((where_ref[1] ^ step) * share, share), share), :]
    squares = coef * coef
    keep = lax.broadcasted_iota(jnp.int32, squares.shape, 0) >= 1
    squares = jnp.where(keep, squares, 0.0)
    sums = [
        jnp.sum(squares[at:at + BLOCK], axis=0, keepdims=True) for at in range(0, terms, BLOCK)
    ]
    total = functools.reduce(jnp.add, sums)
    for group in range(GROUPS):
        part = jnp.zeros_like(total)
        for at, value in enumerate(sums):
            part = part + jnp.where(group_ref[at] == group, value, 0.0)
        sobol_ref[group:group + 1, :] = part / total


def finish(where, inverse, pieces, block_group, samples, n_cell):
    terms = inverse.shape[0]
    cells = pieces[0].shape[1]
    share = jax.ShapeDtypeStruct((terms // n_cell, cells), jnp.float32)
    *shares, sobol = pl.pallas_call(
        functools.partial(finish_kernel, samples, n_cell),
        out_shape=(share,) * n_cell + (jax.ShapeDtypeStruct((GROUPS, cells), jnp.float32),),
        in_specs=[SMEM, SMEM] + [VMEM] * (1 + len(pieces)),
        out_specs=(VMEM,) * (n_cell + 1),
        scratch_shapes=[pltpu.VMEM((terms, cells), jnp.float32)] * 2,
        compiler_params=BIG,
        name="finish",
    )(where, block_group, inverse, *pieces)
    return shares, sobol


def join_kernel(where_ref, *refs):
    out_ref, sems = refs[-2:]
    copies = []
    for step, ref in enumerate(refs[:-2]):
        wide = ref.shape[1]
        to = out_ref.at[:, pl.ds(pl.multiple_of((where_ref[0] ^ step) * wide, wide), wide)]
        copies.append(pltpu.make_async_copy(ref, to, sems.at[step]))
        copies[-1].start()
    for copy in copies:
        copy.wait()


def join_columns(where, shares):
    rows, wide = shares[0].shape
    anywhere = pl.BlockSpec(memory_space=pl.ANY)
    return pl.pallas_call(
        join_kernel,
        out_shape=jax.ShapeDtypeStruct((rows, wide * len(shares)), jnp.float32),
        in_specs=[SMEM] + [anywhere] * len(shares),
        out_specs=anywhere,
        scratch_shapes=[pltpu.SemaphoreType.DMA((len(shares),))],
        name="join_columns",
    )(where, *shares)


def swap(values, axis, step):
    size = lax.axis_size(axis)
    return lax.ppermute(values, axis, [(at, at ^ step) for at in range(size)])


def pick(values, at):
    return lax.dynamic_index_in_dim(values, at, axis=0, keepdims=False)


def sum_over_samples(values, me, gathered):
    rows, lanes = values.shape
    low, high = me & 1, me >> 1
    halves = values.reshape(2, rows // 2, lanes)
    half = pick(halves, low) + swap(pick(halves, low ^ 1), "samp", 1)
    quarters = half.reshape(4, rows // 8, lanes)
    piece = pick(quarters, high)
    for came in [swap(pick(quarters, high ^ step), "samp", 2 * step) for step in range(1, 4)]:
        piece = piece + came
    pieces = [piece] + [swap(piece, "samp", 2 * step) for step in range(1, 4)]
    if gathered:
        half = place_rows(high.reshape(1), pieces)
        return [half, swap(half, "samp", 1)]
    return pieces


def on_device(points, yields, term_index, block_group):
    n_samp = lax.axis_size("samp")
    n_cell = lax.axis_size("cell")
    me, cell = lax.axis_index("samp"), lax.axis_index("cell")
    psi, fold = design(points, term_index, cell, n_cell)
    cross = jnp.dot(psi, yields, preferred_element_type=jnp.float32)
    if n_samp == 8:
        halves = sum_over_samples(fold, me, True)
        first_half = me & 1
    else:
        fold = lax.psum(fold, "samp")
        halves = [fold[:fold.shape[0] // 2], fold[fold.shape[0] // 2:]]
        first_half = jnp.zeros_like(me)
    eighths = []
    for half in halves:
        held = [half]
        step = n_cell // 2
        while step:
            held = held + [swap(value, "cell", step) for value in held]
            step //= 2
        order = [0]
        step = n_cell // 2
        while step:
            order = order + [value ^ step for value in order]
            step //= 2
        eighths += [held[order.index(value)] for value in range(n_cell)]
    gram = first_block(jnp.stack([first_half, cell]), eighths, term_index.shape[0])
    if n_samp == 8:
        quarters = sum_over_samples(cross, me, False)
        other = [swap(value, "samp", 1) for value in quarters]
        pieces = [None] * 8
        for step in range(4):
            pieces[step] = quarters[step]
            pieces[4 + step] = other[step]
        spot = (me & 1) * 4 + (me >> 1)
    else:
        pieces = [lax.psum(cross, "samp")]
        spot = jnp.zeros_like(me)
    for block in range(1, term_index.shape[0] // TILE):
        gram = next_block(gram, block)
    where = jnp.stack([spot, cell])
    shares, sobol = finish(where, gram, pieces, block_group, points.shape[1] * n_samp, n_cell)
    shares = [shares[0]] + [swap(shares[step], "cell", step) for step in range(1, n_cell)]
    return (join_columns(cell.reshape(1), shares), sobol)


def solution(mesh):
    placed = (P(None, "samp"), P("samp", "cell"), P(), P())
    return jax.shard_map(
        on_device,
        mesh=mesh,
        in_specs=placed,
        out_specs=(P("cell", None), P(None, "cell")),
        check_vma=False,
    )
```

```python
import functools

import jax
import jax.numpy as jnp
from jax import lax
from jax.experimental import pallas as pl
from jax.experimental.pallas import tpu as pltpu
from jax.sharding import PartitionSpec as P

BLOCK = 64
GROUPS = 8
TILE = 128
HIGH = lax.Precision.HIGHEST


def split3(values):
    top = values.astype(jnp.bfloat16).astype(jnp.float32)
    rest = values - top
    middle = rest.astype(jnp.bfloat16).astype(jnp.float32)
    return top, middle, rest - middle


def picks(column, params, width):
    span = 3 * params
    degree = column % 4
    place = (degree - 1) * params + column // 4
    lanes = lax.broadcasted_iota(jnp.int32, (column.shape[0], width), 1)
    hit = (lanes == place) | (lanes == place + span) | (lanes == place + 2 * span)
    hit = (hit & (degree > 0)) | ((lanes == 3 * span) & (degree == 0))
    return hit.astype(jnp.float32).astype(jnp.bfloat16)


def design_kernel(chunk, cell_ref, index_ref, points_ref, psi_ref, fold_ref, table_ref):
    params, samples = points_ref.shape
    terms = index_ref.shape[0]
    width = table_ref.shape[0]
    span = 3 * params
    xs = points_ref[...]
    first = 1.7320508075688772 * xs
    second = 2.23606797749979 * (1.5 * xs * xs - 0.5)
    third = 2.6457513110645907 * (2.5 * xs * xs * xs - 1.5 * xs)
    for at, rows in enumerate((first, second, third)):
        for part, values in enumerate(split3(rows)):
            table_ref[pl.ds(part * span + at * params, params), :] = values
    table_ref[pl.ds(3 * span, width - 3 * span), :] = jnp.ones((width - 3 * span, samples), jnp.float32)
    pick_a = picks(index_ref[:, 0:1], params, width)
    pick_b = picks(index_ref[:, 1:2], params, width)
    for start in range(0, samples, chunk):
        table = table_ref[:, start:start + chunk].astype(jnp.bfloat16)
        left = jnp.dot(pick_a, table, preferred_element_type=jnp.float32)
        right = jnp.dot(pick_b, table, preferred_element_type=jnp.float32)
        psi_ref[:, start:start + chunk] = (left * right).astype(jnp.bfloat16)
    blocks = terms // TILE
    part_rows = fold_ref.shape[0] // 2
    cell = cell_ref[0]
    for block in range(blocks):
        rows = psi_ref[pl.ds(pl.multiple_of(block * TILE + cell * part_rows, part_rows), part_rows), :]
        reach = (block + 1) * TILE
        value = lax.dot_general(
            rows, psi_ref[0:reach, :], (((1,), (1,)), ((), ())), preferred_element_type=jnp.float32
        )
        half, at = fold_place(block, blocks)
        fold_ref[half * part_rows:(half + 1) * part_rows, at:at + reach] = value


def fold_place(block, blocks):
    low = min(block, blocks - 1 - block)
    return low, 0 if block == low else (low + 1) * TILE


def design(points, term_index, cell, n_cell):
    params, samples = points.shape
    terms = term_index.shape[0]
    blocks = terms // TILE
    rows = 2 * TILE // n_cell
    return pl.pallas_call(
        functools.partial(design_kernel, 512),
        out_shape=(
            jax.ShapeDtypeStruct((terms, samples), jnp.bfloat16),
            jax.ShapeDtypeStruct((rows, (blocks + 1) * TILE), jnp.float32),
        ),
        in_specs=[
            pl.BlockSpec(memory_space=pltpu.SMEM),
            pl.BlockSpec(memory_space=pltpu.VMEM),
            pl.BlockSpec(memory_space=pltpu.VMEM),
        ],
        out_specs=(pl.BlockSpec(memory_space=pltpu.VMEM),) * 2,
        scratch_shapes=[pltpu.VMEM((256, samples), jnp.float32)],
        compiler_params=pltpu.CompilerParams(vmem_limit_bytes=32 * 2**20),
        name="design",
    )(cell.reshape(1), term_index, points)


def lane_of(values, at):
    return jnp.take_along_axis(values, jnp.full(values.shape, at, jnp.int32), axis=1)


def row_of(values, at):
    return jnp.broadcast_to(values[at:at + 1, :], values.shape)


def sweep_tile(bands):
    bands = list(bands)
    shape = bands[0].shape
    subs = lax.broadcasted_iota(jnp.int32, shape, 0)
    lanes = lax.broadcasted_iota(jnp.int32, shape, 1)
    for at in range(len(bands)):
        base = 8 * at
        own = bands[at]
        inside = (lanes >= base) & (lanes < base + 8)
        columns = [lane_of(own, base + k) for k in range(8)]
        pivot = [[row_of(columns[k], i) if k <= i else None for k in range(8)] for i in range(8)]
        edged = jnp.where(inside, jnp.where(lanes == subs + base, -1.0, 0.0), own)
        rows = [row_of(edged, i) for i in range(8)]
        factor = [[None] * 8 for _ in range(8)]
        inverse = []
        for p in range(8):
            inverse.append(1.0 / pivot[p][p])
            for i in range(p + 1, 8):
                factor[i][p] = pivot[i][p] * inverse[p]
                for k in range(p + 1, i + 1):
                    pivot[i][k] = pivot[i][k] - factor[i][p] * pivot[k][p]
                rows[i] = rows[i] - factor[i][p] * rows[p]
        rows = [rows[i] * inverse[i] for i in range(8)]
        for p in range(7, 0, -1):
            for i in range(p):
                rows[i] = rows[i] - factor[p][i] * rows[p]
        for step in range(1, len(bands)):
            other = (at + step) % len(bands)
            value = jnp.where(inside, 0.0, bands[other])
            for k in range(8):
                value = value - lane_of(bands[other], base + k) * rows[k]
            bands[other] = value
        fresh = rows[0]
        for i in range(1, 8):
            fresh = jnp.where(subs == i, rows[i], fresh)
        bands[at] = fresh
    return bands


def sweep_block(gram_ref, block):
    band = slice(block * TILE, (block + 1) * TILE)
    bands = sweep_tile(gram_ref[block * TILE + at:block * TILE + at + 8, band] for at in range(0, TILE, 8))
    minus = jnp.concatenate(bands, axis=0)
    old = gram_ref[band, :]
    columns = gram_ref[:, band]
    fresh = -jnp.dot(minus, old, precision=HIGH, preferred_element_type=jnp.float32)
    gram_ref[...] -= jnp.dot(columns, fresh, precision=HIGH, preferred_element_type=jnp.float32)
    gram_ref[band, :] = fresh
    gram_ref[:, band] = fresh.T
    gram_ref[band, band] = minus


def first_kernel(where_ref, *refs):
    out_ref = refs[-1]
    terms = out_ref.shape[0]
    blocks = terms // TILE
    for step, ref in enumerate(refs[:-1]):
        piece = ref.shape[0] // 2
        start = pl.multiple_of((where_ref[0] ^ step) * piece, piece)
        for block in range(blocks):
            half, lane = fold_place(block, blocks)
            reach = (block + 1) * TILE
            out_ref[pl.ds(start + block * TILE, piece), 0:reach] = (
                ref[half * piece:(half + 1) * piece, lane:lane + reach]
            )
    for block in range(blocks):
        for other in range(block):
            tile = out_ref[block * TILE:(block + 1) * TILE, other * TILE:(other + 1) * TILE]
            out_ref[other * TILE:(other + 1) * TILE, block * TILE:(block + 1) * TILE] = tile.T
    sweep_block(out_ref, 0)


def next_kernel(block, in_ref, out_ref):
    out_ref[...] = in_ref[...]
    sweep_block(out_ref, block)


STEP_COST = pl.CostEstimate(flops=5 * 10**9, bytes_accessed=2 * 2**20, transcendentals=512)
VMEM = pl.BlockSpec(memory_space=pltpu.VMEM)
SMEM = pl.BlockSpec(memory_space=pltpu.SMEM)
BIG = pltpu.CompilerParams(vmem_limit_bytes=32 * 2**20)


def first_block(where, pieces, terms):
    return pl.pallas_call(
        first_kernel,
        out_shape=jax.ShapeDtypeStruct((terms, terms), jnp.float32),
        in_specs=[SMEM] + [VMEM] * len(pieces),
        out_specs=VMEM,
        compiler_params=BIG,
        cost_estimate=STEP_COST,
        name="block_0",
    )(where, *pieces)


def next_block(gram, block):
    return pl.pallas_call(
        functools.partial(next_kernel, block),
        out_shape=jax.ShapeDtypeStruct(gram.shape, jnp.float32),
        in_specs=[VMEM],
        out_specs=VMEM,
        input_output_aliases={0: 0},
        compiler_params=BIG,
        cost_estimate=STEP_COST,
        name="block_%d" % block,
    )(gram)


def finish_kernel(samples, n_cell, where_ref, group_ref, inverse_ref, *refs):
    pieces = refs[:-(n_cell + 3)]
    coef_refs = refs[-(n_cell + 3):-3]
    sobol_ref, cross_ref, hold_ref = refs[-3:]
    for step, ref in enumerate(pieces):
        rows = ref.shape[0]
        cross_ref[pl.ds(pl.multiple_of((where_ref[0] ^ step) * rows, rows), rows), :] = ref[...]
    terms, cells = cross_ref.shape
    coef = -jnp.dot(inverse_ref[...], cross_ref[...], precision=HIGH, preferred_element_type=jnp.float32)
    hold_ref[...] = coef * jnp.sqrt(jnp.float32(samples))
    share = terms // n_cell
    for step, ref in enumerate(coef_refs):
        ref[...] = hold_ref[pl.ds(pl.multiple_of((where_ref[1] ^ step) * share, share), share), :]
    squares = coef * coef
    keep = lax.broadcasted_iota(jnp.int32, squares.shape, 0) >= 1
    squares = jnp.where(keep, squares, 0.0)
    sums = [
        jnp.sum(squares[at:at + BLOCK], axis=0, keepdims=True) for at in range(0, terms, BLOCK)
    ]
    total = functools.reduce(jnp.add, sums)
    for group in range(GROUPS):
        part = jnp.zeros_like(total)
        for at, value in enumerate(sums):
            part = part + jnp.where(group_ref[at] == group, value, 0.0)
        sobol_ref[group:group + 1, :] = part / total


def finish(where, inverse, pieces, block_group, samples, n_cell):
    terms = inverse.shape[0]
    cells = pieces[0].shape[1]
    share = jax.ShapeDtypeStruct((terms // n_cell, cells), jnp.float32)
    *shares, sobol = pl.pallas_call(
        functools.partial(finish_kernel, samples, n_cell),
        out_shape=(share,) * n_cell + (jax.ShapeDtypeStruct((GROUPS, cells), jnp.float32),),
        in_specs=[SMEM, SMEM] + [VMEM] * (1 + len(pieces)),
        out_specs=(VMEM,) * (n_cell + 1),
        scratch_shapes=[pltpu.VMEM((terms, cells), jnp.float32)] * 2,
        compiler_params=BIG,
        name="finish",
    )(where, block_group, inverse, *pieces)
    return shares, sobol


def join_kernel(where_ref, *refs):
    out_ref = refs[-1]
    for step, ref in enumerate(refs[:-1]):
        wide = ref.shape[1]
        out_ref[:, pl.ds(pl.multiple_of((where_ref[0] ^ step) * wide, wide), wide)] = ref[...]


def join_columns(where, shares):
    rows, wide = shares[0].shape
    return pl.pallas_call(
        join_kernel,
        out_shape=jax.ShapeDtypeStruct((rows, wide * len(shares)), jnp.float32),
        in_specs=[SMEM] + [VMEM] * len(shares),
        out_specs=VMEM,
        name="join_columns",
    )(where, *shares)


def swap(values, axis, step):
    size = lax.axis_size(axis)
    return lax.ppermute(values, axis, [(at, at ^ step) for at in range(size)])


def sum_over_samples(fold):
    n_samp = lax.axis_size("samp")
    pieces = fold.reshape(n_samp, 8, -1)
    piece = jnp.sum(lax.all_to_all(pieces, "samp", split_axis=0, concat_axis=0), axis=0)
    spread = jnp.broadcast_to(piece[None], pieces.shape)
    return lax.all_to_all(spread, "samp", split_axis=0, concat_axis=0).reshape(fold.shape)


def sum_in_groups(values):
    size = lax.axis_size("samp")
    pairs = [[at, at + 1] for at in range(0, size, 2)]
    rest = [list(range(start, size, 2)) for start in range(2)]
    values = lax.psum(values, "samp", axis_index_groups=pairs)
    return lax.psum(values, "samp", axis_index_groups=rest)


def on_device(points, yields, term_index, block_group):
    n_samp = lax.axis_size("samp")
    n_cell = lax.axis_size("cell")
    cell = lax.axis_index("cell")
    psi, fold = design(points, term_index, cell, n_cell)
    cross = sum_in_groups(jnp.dot(psi, yields, preferred_element_type=jnp.float32))
    held, order = [sum_over_samples(fold)], [0]
    step = n_cell // 2
    while step:
        held = held + [swap(value, "cell", step) for value in held]
        order = order + [value ^ step for value in order]
        step //= 2
    gram = first_block(cell.reshape(1), [held[order.index(at)] for at in range(n_cell)], term_index.shape[0])
    for block in range(1, term_index.shape[0] // TILE):
        gram = next_block(gram, block)
    where = jnp.stack([jnp.zeros_like(cell), cell])
    shares, sobol = finish(where, gram, [cross], block_group, points.shape[1] * n_samp, n_cell)
    shares = [shares[0]] + [swap(shares[step], "cell", step) for step in range(1, n_cell)]
    return (join_columns(cell.reshape(1), shares), sobol)


def solution(mesh):
    placed = (P(None, "samp"), P("samp", "cell"), P(), P())
    return jax.shard_map(
        on_device,
        mesh=mesh,
        in_specs=placed,
        out_specs=(P("cell", None), P(None, "cell")),
        check_vma=False,
    )
```

```python
import functools

import jax
import jax.numpy as jnp
from jax import lax
from jax.experimental import pallas as pl
from jax.experimental.pallas import tpu as pltpu
from jax.sharding import PartitionSpec as P

BLOCK = 64
GROUPS = 8
TILE = 128
HIGH = lax.Precision.HIGHEST


def split3(values):
    top = values.astype(jnp.bfloat16).astype(jnp.float32)
    rest = values - top
    middle = rest.astype(jnp.bfloat16).astype(jnp.float32)
    return top, middle, rest - middle


def picks(column, params, width):
    span = 3 * params
    degree = column % 4
    place = (degree - 1) * params + column // 4
    lanes = lax.broadcasted_iota(jnp.int32, (column.shape[0], width), 1)
    hit = (lanes == place) | (lanes == place + span) | (lanes == place + 2 * span)
    hit = (hit & (degree > 0)) | ((lanes == 3 * span) & (degree == 0))
    return hit.astype(jnp.float32).astype(jnp.bfloat16)


def design_kernel(chunk, cell_ref, index_ref, points_ref, psi_ref, fold_ref, table_ref):
    params, samples = points_ref.shape
    terms = index_ref.shape[0]
    width = table_ref.shape[0]
    span = 3 * params
    xs = points_ref[...]
    first = 1.7320508075688772 * xs
    second = 2.23606797749979 * (1.5 * xs * xs - 0.5)
    third = 2.6457513110645907 * (2.5 * xs * xs * xs - 1.5 * xs)
    for at, rows in enumerate((first, second, third)):
        for part, values in enumerate(split3(rows)):
            table_ref[pl.ds(part * span + at * params, params), :] = values
    table_ref[pl.ds(3 * span, width - 3 * span), :] = jnp.ones((width - 3 * span, samples), jnp.float32)
    pick_a = picks(index_ref[:, 0:1], params, width)
    pick_b = picks(index_ref[:, 1:2], params, width)
    for start in range(0, samples, chunk):
        table = table_ref[:, start:start + chunk].astype(jnp.bfloat16)
        left = jnp.dot(pick_a, table, preferred_element_type=jnp.float32)
        right = jnp.dot(pick_b, table, preferred_element_type=jnp.float32)
        psi_ref[:, start:start + chunk] = (left * right).astype(jnp.bfloat16)
    blocks = terms // TILE
    part_rows = fold_ref.shape[0] // 2
    cell = cell_ref[0]
    for block in range(blocks):
        rows = psi_ref[pl.ds(pl.multiple_of(block * TILE + cell * part_rows, part_rows), part_rows), :]
        reach = (block + 1) * TILE
        value = lax.dot_general(
            rows, psi_ref[0:reach, :], (((1,), (1,)), ((), ())), preferred_element_type=jnp.float32
        )
        half, at = fold_place(block, blocks)
        fold_ref[half * part_rows:(half + 1) * part_rows, at:at + reach] = value


def fold_place(block, blocks):
    low = min(block, blocks - 1 - block)
    return low, 0 if block == low else (low + 1) * TILE


def design(points, term_index, cell, n_cell):
    params, samples = points.shape
    terms = term_index.shape[0]
    blocks = terms // TILE
    rows = 2 * TILE // n_cell
    return pl.pallas_call(
        functools.partial(design_kernel, 512),
        out_shape=(
            jax.ShapeDtypeStruct((terms, samples), jnp.bfloat16),
            jax.ShapeDtypeStruct((rows, (blocks + 1) * TILE), jnp.float32),
        ),
        in_specs=[
            pl.BlockSpec(memory_space=pltpu.SMEM),
            pl.BlockSpec(memory_space=pltpu.VMEM),
            pl.BlockSpec(memory_space=pltpu.VMEM),
        ],
        out_specs=(pl.BlockSpec(memory_space=pltpu.VMEM),) * 2,
        scratch_shapes=[pltpu.VMEM((256, samples), jnp.float32)],
        compiler_params=pltpu.CompilerParams(vmem_limit_bytes=32 * 2**20),
        name="design",
    )(cell.reshape(1), term_index, points)


def lane_of(values, at):
    return jnp.take_along_axis(values, jnp.full(values.shape, at, jnp.int32), axis=1)


def row_of(values, at):
    return jnp.broadcast_to(values[at:at + 1, :], values.shape)


def sweep_tile(bands):
    bands = list(bands)
    shape = bands[0].shape
    subs = lax.broadcasted_iota(jnp.int32, shape, 0)
    lanes = lax.broadcasted_iota(jnp.int32, shape, 1)
    for at in range(len(bands)):
        base = 8 * at
        own = bands[at]
        inside = (lanes >= base) & (lanes < base + 8)
        columns = [lane_of(own, base + k) for k in range(8)]
        pivot = [[row_of(columns[k], i) if k <= i else None for k in range(8)] for i in range(8)]
        edged = jnp.where(inside, jnp.where(lanes == subs + base, -1.0, 0.0), own)
        rows = [row_of(edged, i) for i in range(8)]
        factor = [[None] * 8 for _ in range(8)]
        inverse = []
        for p in range(8):
            inverse.append(1.0 / pivot[p][p])
            for i in range(p + 1, 8):
                factor[i][p] = pivot[i][p] * inverse[p]
                for k in range(p + 1, i + 1):
                    pivot[i][k] = pivot[i][k] - factor[i][p] * pivot[k][p]
                rows[i] = rows[i] - factor[i][p] * rows[p]
        rows = [rows[i] * inverse[i] for i in range(8)]
        for p in range(7, 0, -1):
            for i in range(p):
                rows[i] = rows[i] - factor[p][i] * rows[p]
        for step in range(1, len(bands)):
            other = (at + step) % len(bands)
            value = jnp.where(inside, 0.0, bands[other])
            for k in range(7, -1, -1):
                value = value - lane_of(bands[other], base + k) * rows[k]
            bands[other] = value
        fresh = rows[0]
        for i in range(1, 8):
            fresh = jnp.where(subs == i, rows[i], fresh)
        bands[at] = fresh
    return bands


def sweep_block(gram_ref, block):
    band = slice(block * TILE, (block + 1) * TILE)
    bands = sweep_tile(gram_ref[block * TILE + at:block * TILE + at + 8, band] for at in range(0, TILE, 8))
    minus = jnp.concatenate(bands, axis=0)
    old = gram_ref[band, :]
    columns = gram_ref[:, band]
    fresh = -jnp.dot(minus, old, precision=HIGH, preferred_element_type=jnp.float32)
    gram_ref[...] -= jnp.dot(columns, fresh, precision=HIGH, preferred_element_type=jnp.float32)
    gram_ref[band, :] = fresh
    gram_ref[:, band] = fresh.T
    gram_ref[band, band] = minus


def first_kernel(where_ref, *refs):
    out_ref = refs[-1]
    terms = out_ref.shape[0]
    blocks = terms // TILE
    for step, ref in enumerate(refs[:-1]):
        piece = ref.shape[0] // 2
        start = pl.multiple_of((where_ref[0] ^ step) * piece, piece)
        for block in range(blocks):
            half, lane = fold_place(block, blocks)
            reach = (block + 1) * TILE
            out_ref[pl.ds(start + block * TILE, piece), 0:reach] = (
                ref[half * piece:(half + 1) * piece, lane:lane + reach]
            )
    for block in range(blocks):
        for other in range(block):
            tile = out_ref[block * TILE:(block + 1) * TILE, other * TILE:(other + 1) * TILE]
            out_ref[other * TILE:(other + 1) * TILE, block * TILE:(block + 1) * TILE] = tile.T
    sweep_block(out_ref, 0)


def next_kernel(block, in_ref, out_ref):
    out_ref[...] = in_ref[...]
    sweep_block(out_ref, block)


STEP_COST = pl.CostEstimate(flops=5 * 10**9, bytes_accessed=2 * 2**20, transcendentals=512)
VMEM = pl.BlockSpec(memory_space=pltpu.VMEM)
SMEM = pl.BlockSpec(memory_space=pltpu.SMEM)
BIG = pltpu.CompilerParams(vmem_limit_bytes=32 * 2**20)


def first_block(where, pieces, terms):
    return pl.pallas_call(
        first_kernel,
        out_shape=jax.ShapeDtypeStruct((terms, terms), jnp.float32),
        in_specs=[SMEM] + [VMEM] * len(pieces),
        out_specs=VMEM,
        compiler_params=BIG,
        cost_estimate=STEP_COST,
        name="block_0",
    )(where, *pieces)


def next_block(gram, block):
    return pl.pallas_call(
        functools.partial(next_kernel, block),
        out_shape=jax.ShapeDtypeStruct(gram.shape, jnp.float32),
        in_specs=[VMEM],
        out_specs=VMEM,
        input_output_aliases={0: 0},
        compiler_params=BIG,
        cost_estimate=STEP_COST,
        name="block_%d" % block,
    )(gram)


def finish_kernel(samples, n_cell, where_ref, group_ref, inverse_ref, *refs):
    pieces = refs[:-(n_cell + 3)]
    coef_refs = refs[-(n_cell + 3):-3]
    sobol_ref, cross_ref, hold_ref = refs[-3:]
    for step, ref in enumerate(pieces):
        rows = ref.shape[0]
        cross_ref[pl.ds(pl.multiple_of((where_ref[0] ^ step) * rows, rows), rows), :] = ref[...]
    terms, cells = cross_ref.shape
    coef = -jnp.dot(inverse_ref[...], cross_ref[...], precision=HIGH, preferred_element_type=jnp.float32)
    hold_ref[...] = coef * jnp.sqrt(jnp.float32(samples))
    share = terms // n_cell
    for step, ref in enumerate(coef_refs):
        ref[...] = hold_ref[pl.ds(pl.multiple_of((where_ref[1] ^ step) * share, share), share), :]
    squares = coef * coef
    keep = lax.broadcasted_iota(jnp.int32, squares.shape, 0) >= 1
    squares = jnp.where(keep, squares, 0.0)
    sums = [
        jnp.sum(squares[at:at + BLOCK], axis=0, keepdims=True) for at in range(0, terms, BLOCK)
    ]
    total = functools.reduce(jnp.add, sums)
    for group in range(GROUPS):
        part = jnp.zeros_like(total)
        for at, value in enumerate(sums):
            part = part + jnp.where(group_ref[at] == group, value, 0.0)
        sobol_ref[group:group + 1, :] = part / total


def finish(where, inverse, pieces, block_group, samples, n_cell):
    terms = inverse.shape[0]
    cells = pieces[0].shape[1]
    share = jax.ShapeDtypeStruct((terms // n_cell, cells), jnp.float32)
    *shares, sobol = pl.pallas_call(
        functools.partial(finish_kernel, samples, n_cell),
        out_shape=(share,) * n_cell + (jax.ShapeDtypeStruct((GROUPS, cells), jnp.float32),),
        in_specs=[SMEM, SMEM] + [VMEM] * (1 + len(pieces)),
        out_specs=(VMEM,) * (n_cell + 1),
        scratch_shapes=[pltpu.VMEM((terms, cells), jnp.float32)] * 2,
        compiler_params=BIG,
        name="finish",
    )(where, block_group, inverse, *pieces)
    return shares, sobol


def join_kernel(where_ref, *refs):
    out_ref = refs[-1]
    for step, ref in enumerate(refs[:-1]):
        wide = ref.shape[1]
        out_ref[:, pl.ds(pl.multiple_of((where_ref[0] ^ step) * wide, wide), wide)] = ref[...]


def join_columns(where, shares):
    rows, wide = shares[0].shape
    return pl.pallas_call(
        join_kernel,
        out_shape=jax.ShapeDtypeStruct((rows, wide * len(shares)), jnp.float32),
        in_specs=[SMEM] + [VMEM] * len(shares),
        out_specs=VMEM,
        name="join_columns",
    )(where, *shares)


def swap(values, axis, step):
    size = lax.axis_size(axis)
    return lax.ppermute(values, axis, [(at, at ^ step) for at in range(size)])


def exchange(pieces):
    return lax.all_to_all(pieces, "samp", split_axis=0, concat_axis=0)


def spread(piece):
    copies = jnp.broadcast_to(piece[None], (lax.axis_size("samp"),) + piece.shape)
    return exchange(copies)


def on_device(points, yields, term_index, block_group):
    n_samp = lax.axis_size("samp")
    n_cell = lax.axis_size("cell")
    cell = lax.axis_index("cell")
    psi, fold = design(points, term_index, cell, n_cell)
    pieces = fold.reshape((n_samp, 8, -1) if fold.shape[0] % (8 * n_samp) else (n_samp, -1, fold.shape[1]))
    piece = jnp.sum(exchange(pieces), axis=0)
    cross = jnp.dot(psi, yields, preferred_element_type=jnp.float32)
    fold = spread(piece).reshape(fold.shape)
    fold, cross = lax.optimization_barrier((fold, cross))
    parts = exchange(cross.reshape(n_samp, -1, cross.shape[1]))
    held, order = [fold], [0]
    step = n_cell // 2
    while step:
        held = held + [swap(value, "cell", step) for value in held]
        order = order + [value ^ step for value in order]
        step //= 2
    gram = first_block(cell.reshape(1), [held[order.index(at)] for at in range(n_cell)], term_index.shape[0])
    blocks = term_index.shape[0] // TILE
    for block in range(1, blocks):
        if block == blocks // 2:
            gram, parts = lax.optimization_barrier((gram, parts))
            summed = spread(jnp.sum(parts, axis=0))
        gram = next_block(gram, block)
    gram, summed = lax.optimization_barrier((gram, summed))
    cross = summed.reshape(cross.shape)
    where = jnp.stack([jnp.zeros_like(cell), cell])
    shares, sobol = finish(where, gram, [cross], block_group, points.shape[1] * n_samp, n_cell)
    shares = [shares[0]] + [swap(shares[step], "cell", step) for step in range(1, n_cell)]
    return (join_columns(cell.reshape(1), shares), sobol)


def solution(mesh):
    placed = (P(None, "samp"), P("samp", "cell"), P(), P())
    return jax.shard_map(
        on_device,
        mesh=mesh,
        in_specs=placed,
        out_specs=(P("cell", None), P(None, "cell")),
        check_vma=False,
    )
```

```python
import functools

import jax
import jax.numpy as jnp
from jax import lax
from jax.experimental import pallas as pl
from jax.experimental.pallas import tpu as pltpu
from jax.sharding import PartitionSpec as P

BLOCK = 64
GROUPS = 8
TILE = 128
HIGH = lax.Precision.HIGHEST


def split3(values):
    top = values.astype(jnp.bfloat16).astype(jnp.float32)
    rest = values - top
    middle = rest.astype(jnp.bfloat16).astype(jnp.float32)
    return top, middle, rest - middle


def picks(column, params, width):
    span = 3 * params
    degree = column % 4
    place = (degree - 1) * params + column // 4
    lanes = lax.broadcasted_iota(jnp.int32, (column.shape[0], width), 1)
    hit = (lanes == place) | (lanes == place + span) | (lanes == place + 2 * span)
    hit = (hit & (degree > 0)) | ((lanes == 3 * span) & (degree == 0))
    return hit.astype(jnp.float32).astype(jnp.bfloat16)


def design_kernel(chunk, cell_ref, index_ref, points_ref, psi_ref, fold_ref, table_ref):
    params, samples = points_ref.shape
    terms = index_ref.shape[0]
    width = table_ref.shape[0]
    span = 3 * params
    xs = points_ref[...]
    first = 1.7320508075688772 * xs
    second = 2.23606797749979 * (1.5 * xs * xs - 0.5)
    third = 2.6457513110645907 * (2.5 * xs * xs * xs - 1.5 * xs)
    for at, rows in enumerate((first, second, third)):
        for part, values in enumerate(split3(rows)):
            table_ref[pl.ds(part * span + at * params, params), :] = values
    table_ref[pl.ds(3 * span, width - 3 * span), :] = jnp.ones((width - 3 * span, samples), jnp.float32)
    pick_a = picks(index_ref[:, 0:1], params, width)
    pick_b = picks(index_ref[:, 1:2], params, width)
    for start in range(0, samples, chunk):
        table = table_ref[:, start:start + chunk].astype(jnp.bfloat16)
        left = jnp.dot(pick_a, table, preferred_element_type=jnp.float32)
        right = jnp.dot(pick_b, table, preferred_element_type=jnp.float32)
        psi_ref[:, start:start + chunk] = (left * right).astype(jnp.bfloat16)
    blocks = terms // TILE
    part_rows = fold_ref.shape[0] // 2
    cell = cell_ref[0]
    for block in range(blocks):
        rows = psi_ref[pl.ds(pl.multiple_of(block * TILE + cell * part_rows, part_rows), part_rows), :]
        reach = (block + 1) * TILE
        value = lax.dot_general(
            rows, psi_ref[0:reach, :], (((1,), (1,)), ((), ())), preferred_element_type=jnp.float32
        )
        half, at = fold_place(block, blocks)
        fold_ref[half * part_rows:(half + 1) * part_rows, at:at + reach] = value


def fold_place(block, blocks):
    low = min(block, blocks - 1 - block)
    return low, 0 if block == low else (low + 1) * TILE


def design(points, term_index, cell, n_cell):
    params, samples = points.shape
    terms = term_index.shape[0]
    blocks = terms // TILE
    rows = 2 * TILE // n_cell
    return pl.pallas_call(
        functools.partial(design_kernel, 512),
        out_shape=(
            jax.ShapeDtypeStruct((terms, samples), jnp.bfloat16),
            jax.ShapeDtypeStruct((rows, (blocks + 1) * TILE), jnp.float32),
        ),
        in_specs=[
            pl.BlockSpec(memory_space=pltpu.SMEM),
            pl.BlockSpec(memory_space=pltpu.VMEM),
            pl.BlockSpec(memory_space=pltpu.VMEM),
        ],
        out_specs=(pl.BlockSpec(memory_space=pltpu.VMEM),) * 2,
        scratch_shapes=[pltpu.VMEM((256, samples), jnp.float32)],
        compiler_params=pltpu.CompilerParams(vmem_limit_bytes=32 * 2**20),
        name="design",
    )(cell.reshape(1), term_index, points)


def lane_of(values, at):
    return jnp.take_along_axis(values, jnp.full(values.shape, at, jnp.int32), axis=1)


def row_of(values, at):
    return jnp.broadcast_to(values[at:at + 1, :], values.shape)


def sweep_tile(bands):
    bands = list(bands)
    shape = bands[0].shape
    subs = lax.broadcasted_iota(jnp.int32, shape, 0)
    lanes = lax.broadcasted_iota(jnp.int32, shape, 1)
    for at in range(len(bands)):
        base = 8 * at
        own = bands[at]
        inside = (lanes >= base) & (lanes < base + 8)
        columns = [lane_of(own, base + k) for k in range(8)]
        pivot = [[row_of(columns[k], i) if k <= i else None for k in range(8)] for i in range(8)]
        edged = jnp.where(inside, jnp.where(lanes == subs + base, -1.0, 0.0), own)
        rows = [row_of(edged, i) for i in range(8)]
        factor = [[None] * 8 for _ in range(8)]
        inverse = []
        for p in range(8):
            inverse.append(1.0 / pivot[p][p])
            for i in range(p + 1, 8):
                factor[i][p] = pivot[i][p] * inverse[p]
                for k in range(p + 1, i + 1):
                    pivot[i][k] = pivot[i][k] - factor[i][p] * pivot[k][p]
                rows[i] = rows[i] - factor[i][p] * rows[p]
        rows = [rows[i] * inverse[i] for i in range(8)]
        for p in range(7, 0, -1):
            for i in range(p):
                rows[i] = rows[i] - factor[p][i] * rows[p]
        for step in range(1, len(bands)):
            other = (at + step) % len(bands)
            value = jnp.where(inside, 0.0, bands[other])
            for k in range(7, -1, -1):
                value = value - lane_of(bands[other], base + k) * rows[k]
            bands[other] = value
        fresh = rows[0]
        for i in range(1, 8):
            fresh = jnp.where(subs == i, rows[i], fresh)
        bands[at] = fresh
    return bands


def stacked_dot(left, right):
    a = [part.astype(jnp.bfloat16) for part in split3(left)]
    b = [part.astype(jnp.bfloat16) for part in split3(right)]
    left = jnp.concatenate([a[0], a[0], a[1], a[1], a[0], a[2]], axis=1)
    right = jnp.concatenate([b[0], b[1], b[0], b[1], b[2], b[0]], axis=0)
    return jnp.dot(left, right, preferred_element_type=jnp.float32)


def sweep_block(gram_ref, block):
    band = slice(block * TILE, (block + 1) * TILE)
    bands = sweep_tile(gram_ref[block * TILE + at:block * TILE + at + 8, band] for at in range(0, TILE, 8))
    minus = jnp.concatenate(bands, axis=0)
    old = gram_ref[band, :]
    columns = gram_ref[:, band]
    fresh = -stacked_dot(minus, old)
    gram_ref[...] -= stacked_dot(columns, fresh)
    gram_ref[band, :] = fresh
    gram_ref[:, band] = fresh.T
    gram_ref[band, band] = minus


def first_kernel(where_ref, *refs):
    out_ref = refs[-1]
    terms = out_ref.shape[0]
    blocks = terms // TILE
    for step, ref in enumerate(refs[:-1]):
        piece = ref.shape[0] // 2
        start = pl.multiple_of((where_ref[0] ^ step) * piece, piece)
        for block in range(blocks):
            half, lane = fold_place(block, blocks)
            reach = (block + 1) * TILE
            out_ref[pl.ds(start + block * TILE, piece), 0:reach] = (
                ref[half * piece:(half + 1) * piece, lane:lane + reach]
            )
    for block in range(blocks):
        for other in range(block):
            tile = out_ref[block * TILE:(block + 1) * TILE, other * TILE:(other + 1) * TILE]
            out_ref[other * TILE:(other + 1) * TILE, block * TILE:(block + 1) * TILE] = tile.T
    sweep_block(out_ref, 0)


def next_kernel(block, in_ref, out_ref):
    out_ref[...] = in_ref[...]
    sweep_block(out_ref, block)


STEP_COST = pl.CostEstimate(flops=5 * 10**9, bytes_accessed=2 * 2**20, transcendentals=512)
VMEM = pl.BlockSpec(memory_space=pltpu.VMEM)
SMEM = pl.BlockSpec(memory_space=pltpu.SMEM)
BIG = pltpu.CompilerParams(vmem_limit_bytes=32 * 2**20)


def first_block(where, pieces, terms):
    return pl.pallas_call(
        first_kernel,
        out_shape=jax.ShapeDtypeStruct((terms, terms), jnp.float32),
        in_specs=[SMEM] + [VMEM] * len(pieces),
        out_specs=VMEM,
        compiler_params=BIG,
        cost_estimate=STEP_COST,
        name="block_0",
    )(where, *pieces)


def next_block(gram, block):
    return pl.pallas_call(
        functools.partial(next_kernel, block),
        out_shape=jax.ShapeDtypeStruct(gram.shape, jnp.float32),
        in_specs=[VMEM],
        out_specs=VMEM,
        input_output_aliases={0: 0},
        compiler_params=BIG,
        cost_estimate=STEP_COST,
        name="block_%d" % block,
    )(gram)


def finish_kernel(samples, n_cell, where_ref, group_ref, inverse_ref, *refs):
    pieces = refs[:-(n_cell + 3)]
    coef_refs = refs[-(n_cell + 3):-3]
    sobol_ref, cross_ref, hold_ref = refs[-3:]
    for step, ref in enumerate(pieces):
        rows = ref.shape[0]
        cross_ref[pl.ds(pl.multiple_of((where_ref[0] ^ step) * rows, rows), rows), :] = ref[...]
    terms, cells = cross_ref.shape
    coef = -jnp.dot(inverse_ref[...], cross_ref[...], precision=HIGH, preferred_element_type=jnp.float32)
    hold_ref[...] = coef * jnp.sqrt(jnp.float32(samples))
    share = terms // n_cell
    for step, ref in enumerate(coef_refs):
        ref[...] = hold_ref[pl.ds(pl.multiple_of((where_ref[1] ^ step) * share, share), share), :]
    squares = coef * coef
    keep = lax.broadcasted_iota(jnp.int32, squares.shape, 0) >= 1
    squares = jnp.where(keep, squares, 0.0)
    sums = [
        jnp.sum(squares[at:at + BLOCK], axis=0, keepdims=True) for at in range(0, terms, BLOCK)
    ]
    total = functools.reduce(jnp.add, sums)
    for group in range(GROUPS):
        part = jnp.zeros_like(total)
        for at, value in enumerate(sums):
            part = part + jnp.where(group_ref[at] == group, value, 0.0)
        sobol_ref[group:group + 1, :] = part / total


def finish(where, inverse, pieces, block_group, samples, n_cell):
    terms = inverse.shape[0]
    cells = pieces[0].shape[1]
    share = jax.ShapeDtypeStruct((terms // n_cell, cells), jnp.float32)
    *shares, sobol = pl.pallas_call(
        functools.partial(finish_kernel, samples, n_cell),
        out_shape=(share,) * n_cell + (jax.ShapeDtypeStruct((GROUPS, cells), jnp.float32),),
        in_specs=[SMEM, SMEM] + [VMEM] * (1 + len(pieces)),
        out_specs=(VMEM,) * (n_cell + 1),
        scratch_shapes=[pltpu.VMEM((terms, cells), jnp.float32)] * 2,
        compiler_params=BIG,
        name="finish",
    )(where, block_group, inverse, *pieces)
    return shares, sobol


def join_kernel(where_ref, *refs):
    out_ref = refs[-1]
    for step, ref in enumerate(refs[:-1]):
        wide = ref.shape[1]
        out_ref[:, pl.ds(pl.multiple_of((where_ref[0] ^ step) * wide, wide), wide)] = ref[...]


def join_columns(where, shares):
    rows, wide = shares[0].shape
    return pl.pallas_call(
        join_kernel,
        out_shape=jax.ShapeDtypeStruct((rows, wide * len(shares)), jnp.float32),
        in_specs=[SMEM] + [VMEM] * len(shares),
        out_specs=VMEM,
        name="join_columns",
    )(where, *shares)


def swap(values, axis, step):
    size = lax.axis_size(axis)
    return lax.ppermute(values, axis, [(at, at ^ step) for at in range(size)])


def exchange(pieces):
    return lax.all_to_all(pieces, "samp", split_axis=0, concat_axis=0)


def spread(piece):
    return jnp.broadcast_to(piece[None], (lax.axis_size("samp"),) + piece.shape)


def on_device(points, yields, term_index, block_group):
    n_samp = lax.axis_size("samp")
    n_cell = lax.axis_size("cell")
    cell = lax.axis_index("cell")
    psi, fold = design(points, term_index, cell, n_cell)
    pieces = fold.reshape((n_samp, 8, -1) if fold.shape[0] % (8 * n_samp) else (n_samp, -1, fold.shape[1]))
    came = exchange(pieces)
    cross = jnp.dot(psi, yields, preferred_element_type=jnp.float32)
    came, cross = lax.optimization_barrier((came, cross))
    copies, cross = lax.optimization_barrier((spread(jnp.sum(came, axis=0)), cross))
    fold = exchange(copies).reshape(fold.shape)
    parts = exchange(cross.reshape(n_samp, -1, cross.shape[1]))
    held, order = [fold], [0]
    step = n_cell // 2
    while step:
        held = held + [swap(value, "cell", step) for value in held]
        order = order + [value ^ step for value in order]
        step //= 2
    gram = first_block(cell.reshape(1), [held[order.index(at)] for at in range(n_cell)], term_index.shape[0])
    blocks = term_index.shape[0] // TILE
    for block in range(1, blocks):
        if block == 1:
            gram, parts = lax.optimization_barrier((gram, parts))
            summed = exchange(spread(jnp.sum(parts, axis=0)))
        gram = next_block(gram, block)
    gram, summed = lax.optimization_barrier((gram, summed))
    cross = summed.reshape(cross.shape)
    where = jnp.stack([jnp.zeros_like(cell), cell])
    shares, sobol = finish(where, gram, [cross], block_group, points.shape[1] * n_samp, n_cell)
    shares = [shares[0]] + [swap(shares[step], "cell", step) for step in range(1, n_cell)]
    return (join_columns(cell.reshape(1), shares), sobol)


def solution(mesh):
    placed = (P(None, "samp"), P("samp", "cell"), P(), P())
    return jax.shard_map(
        on_device,
        mesh=mesh,
        in_specs=placed,
        out_specs=(P("cell", None), P(None, "cell")),
        check_vma=False,
    )
```

```python
import functools

import jax
import jax.numpy as jnp
from jax import lax
from jax.experimental import pallas as pl
from jax.experimental.pallas import tpu as pltpu
from jax.sharding import PartitionSpec as P

BLOCK = 64
GROUPS = 8
TILE = 128
HIGH = lax.Precision.HIGHEST


def split3(values):
    top = values.astype(jnp.bfloat16).astype(jnp.float32)
    rest = values - top
    middle = rest.astype(jnp.bfloat16).astype(jnp.float32)
    return top, middle, rest - middle


def picks(column, params, width):
    span = 3 * params
    degree = column % 4
    place = (degree - 1) * params + column // 4
    lanes = lax.broadcasted_iota(jnp.int32, (column.shape[0], width), 1)
    hit = (lanes == place) | (lanes == place + span) | (lanes == place + 2 * span)
    hit = (hit & (degree > 0)) | ((lanes == 3 * span) & (degree == 0))
    return hit.astype(jnp.float32).astype(jnp.bfloat16)


def design_kernel(chunk, cell_ref, index_ref, points_ref, psi_ref, fold_ref, table_ref):
    params, samples = points_ref.shape
    terms = index_ref.shape[0]
    width = table_ref.shape[0]
    span = 3 * params
    xs = points_ref[...]
    first = 1.7320508075688772 * xs
    second = 2.23606797749979 * (1.5 * xs * xs - 0.5)
    third = 2.6457513110645907 * (2.5 * xs * xs * xs - 1.5 * xs)
    for at, rows in enumerate((first, second, third)):
        for part, values in enumerate(split3(rows)):
            table_ref[pl.ds(part * span + at * params, params), :] = values
    table_ref[pl.ds(3 * span, width - 3 * span), :] = jnp.ones((width - 3 * span, samples), jnp.float32)
    pick_a = picks(index_ref[:, 0:1], params, width)
    pick_b = picks(index_ref[:, 1:2], params, width)
    for start in range(0, samples, chunk):
        table = table_ref[:, start:start + chunk].astype(jnp.bfloat16)
        left = jnp.dot(pick_a, table, preferred_element_type=jnp.float32)
        right = jnp.dot(pick_b, table, preferred_element_type=jnp.float32)
        psi_ref[:, start:start + chunk] = (left * right).astype(jnp.bfloat16)
    blocks = terms // TILE
    part_rows = fold_ref.shape[0] // 2
    cell = cell_ref[0]
    for block in range(blocks):
        rows = psi_ref[pl.ds(pl.multiple_of(block * TILE + cell * part_rows, part_rows), part_rows), :]
        reach = (block + 1) * TILE
        value = lax.dot_general(
            rows, psi_ref[0:reach, :], (((1,), (1,)), ((), ())), preferred_element_type=jnp.float32
        )
        half, at = fold_place(block, blocks)
        fold_ref[half * part_rows:(half + 1) * part_rows, at:at + reach] = value


def fold_place(block, blocks):
    low = min(block, blocks - 1 - block)
    return low, 0 if block == low else (low + 1) * TILE


def design(points, term_index, cell, n_cell):
    params, samples = points.shape
    terms = term_index.shape[0]
    blocks = terms // TILE
    rows = 2 * TILE // n_cell
    return pl.pallas_call(
        functools.partial(design_kernel, 512),
        out_shape=(
            jax.ShapeDtypeStruct((terms, samples), jnp.bfloat16),
            jax.ShapeDtypeStruct((rows, (blocks + 1) * TILE), jnp.float32),
        ),
        in_specs=[
            pl.BlockSpec(memory_space=pltpu.SMEM),
            pl.BlockSpec(memory_space=pltpu.VMEM),
            pl.BlockSpec(memory_space=pltpu.VMEM),
        ],
        out_specs=(pl.BlockSpec(memory_space=pltpu.VMEM),) * 2,
        scratch_shapes=[pltpu.VMEM((256, samples), jnp.float32)],
        compiler_params=pltpu.CompilerParams(vmem_limit_bytes=32 * 2**20),
        name="design",
    )(cell.reshape(1), term_index, points)


def lane_of(values, at):
    return jnp.broadcast_to(values[:, at:at + 1], values.shape)


def row_of(values, at):
    return jnp.broadcast_to(values[at:at + 1, :], values.shape)


def sweep_tile(bands):
    bands = list(bands)
    shape = bands[0].shape
    subs = lax.broadcasted_iota(jnp.int32, shape, 0)
    lanes = lax.broadcasted_iota(jnp.int32, shape, 1)
    for at in range(len(bands)):
        base = 8 * at
        own = bands[at]
        inside = (lanes >= base) & (lanes < base + 8)
        columns = [lane_of(own, base + k) for k in range(8)]
        pivot = [[row_of(columns[k], i) if k <= i else None for k in range(8)] for i in range(8)]
        edged = jnp.where(inside, jnp.where(lanes == subs + base, -1.0, 0.0), own)
        rows = [row_of(edged, i) for i in range(8)]
        factor = [[None] * 8 for _ in range(8)]
        pairs = []
        for p in range(0, 8, 2):
            q = p + 1
            a, b, d = pivot[p][p], pivot[q][p], pivot[q][q]
            inverse = 1.0 / (a * d - b * b)
            pairs.append((a, b, d, inverse))
            mixed = [None] * 8
            for i in range(q + 1, 8):
                e, f = pivot[i][p], pivot[i][q]
                mixed[i] = (d * e - b * f, a * f - b * e)
                factor[i][p], factor[i][q] = mixed[i][0] * inverse, mixed[i][1] * inverse
            for i in range(q + 1, 8):
                for k in range(q + 1, i + 1):
                    less = mixed[i][0] * pivot[k][p] + mixed[i][1] * pivot[k][q]
                    pivot[i][k] = pivot[i][k] - less * inverse
                rows[i] = rows[i] - (factor[i][p] * rows[p] + factor[i][q] * rows[q])
        for p in range(0, 8, 2):
            a, b, d, inverse = pairs[p // 2]
            top, low = rows[p], rows[p + 1]
            rows[p], rows[p + 1] = (d * top - b * low) * inverse, (a * low - b * top) * inverse
        for p in range(6, 0, -2):
            for i in range(p):
                rows[i] = rows[i] - (factor[p][i] * rows[p] + factor[p + 1][i] * rows[p + 1])
        for step in range(1, len(bands)):
            other = (at + step) % len(bands)
            value = jnp.where(inside, 0.0, bands[other])
            for k in range(7, -1, -1):
                value = value - lane_of(bands[other], base + k) * rows[k]
            bands[other] = value
        fresh = rows[0]
        for i in range(1, 8):
            fresh = jnp.where(subs == i, rows[i], fresh)
        bands[at] = fresh
    return bands


def stacked_dot(left, right):
    a = [part.astype(jnp.bfloat16) for part in split3(left)]
    b = [part.astype(jnp.bfloat16) for part in split3(right)]
    left = jnp.concatenate([a[0], a[0], a[1], a[1], a[0], a[2]], axis=1)
    right = jnp.concatenate([b[0], b[1], b[0], b[1], b[2], b[0]], axis=0)
    return jnp.dot(left, right, preferred_element_type=jnp.float32)


def sweep_block(gram_ref, block):
    band = slice(block * TILE, (block + 1) * TILE)
    bands = sweep_tile(gram_ref[block * TILE + at:block * TILE + at + 8, band] for at in range(0, TILE, 8))
    minus = jnp.concatenate(bands, axis=0)
    old = gram_ref[band, :]
    columns = gram_ref[:, band]
    fresh = -stacked_dot(minus, old)
    gram_ref[...] -= stacked_dot(columns, fresh)
    gram_ref[band, :] = fresh
    gram_ref[:, band] = fresh.T
    gram_ref[band, band] = minus


def first_kernel(where_ref, *refs):
    out_ref, scale_ref = refs[-2:]
    terms = out_ref.shape[0]
    blocks = terms // TILE
    for step, ref in enumerate(refs[:-2]):
        piece = ref.shape[0] // 2
        start = pl.multiple_of((where_ref[0] ^ step) * piece, piece)
        for block in range(blocks):
            half, lane = fold_place(block, blocks)
            reach = (block + 1) * TILE
            out_ref[pl.ds(start + block * TILE, piece), 0:reach] = (
                ref[half * piece:(half + 1) * piece, lane:lane + reach]
            )
    for block in range(blocks):
        for other in range(block):
            tile = out_ref[block * TILE:(block + 1) * TILE, other * TILE:(other + 1) * TILE]
            out_ref[other * TILE:(other + 1) * TILE, block * TILE:(block + 1) * TILE] = tile.T
    diagonal = lax.broadcasted_iota(jnp.int32, (TILE, TILE), 0) == lax.broadcasted_iota(jnp.int32, (TILE, TILE), 1)
    across = []
    for block in range(blocks):
        band = slice(block * TILE, (block + 1) * TILE)
        only = jnp.where(diagonal, out_ref[band, band], 0.0)
        scale_ref[band, :] = lax.rsqrt(jnp.sum(only, axis=1, keepdims=True))
        across.append(lax.rsqrt(jnp.sum(only, axis=0, keepdims=True)))
    out_ref[...] = out_ref[...] * scale_ref[...] * jnp.concatenate(across, axis=1)
    sweep_block(out_ref, 0)


def next_kernel(block, in_ref, out_ref):
    out_ref[...] = in_ref[...]
    sweep_block(out_ref, block)


STEP_COST = pl.CostEstimate(flops=5 * 10**9, bytes_accessed=2 * 2**20, transcendentals=512)
VMEM = pl.BlockSpec(memory_space=pltpu.VMEM)
SMEM = pl.BlockSpec(memory_space=pltpu.SMEM)
BIG = pltpu.CompilerParams(vmem_limit_bytes=32 * 2**20)


def first_block(where, pieces, terms):
    return pl.pallas_call(
        first_kernel,
        out_shape=(
            jax.ShapeDtypeStruct((terms, terms), jnp.float32),
            jax.ShapeDtypeStruct((terms, 1), jnp.float32),
        ),
        in_specs=[SMEM] + [VMEM] * len(pieces),
        out_specs=(VMEM, VMEM),
        compiler_params=BIG,
        cost_estimate=STEP_COST,
        name="block_0",
    )(where, *pieces)


def next_block(gram, block):
    return pl.pallas_call(
        functools.partial(next_kernel, block),
        out_shape=jax.ShapeDtypeStruct(gram.shape, jnp.float32),
        in_specs=[VMEM],
        out_specs=VMEM,
        input_output_aliases={0: 0},
        compiler_params=BIG,
        cost_estimate=STEP_COST,
        name="block_%d" % block,
    )(gram)


def finish_kernel(samples, n_cell, rows, where_ref, group_ref, inverse_ref, scale_ref, *refs):
    pieces = refs[:-(n_cell + 3)]
    coef_refs = refs[-(n_cell + 3):-3]
    sobol_ref, cross_ref, hold_ref = refs[-3:]
    step = 0
    for ref in pieces:
        for at in range(0, ref.shape[0], rows):
            cross_ref[pl.ds(pl.multiple_of((where_ref[0] ^ step) * rows, rows), rows), :] = ref[at:at + rows, :]
            step += 1
    terms, cells = cross_ref.shape
    scaled = scale_ref[...] * cross_ref[...]
    scaled = jnp.dot(inverse_ref[...], scaled, precision=HIGH, preferred_element_type=jnp.float32)
    coef = -scale_ref[...] * scaled
    hold_ref[...] = coef * jnp.sqrt(jnp.float32(samples))
    share = terms // n_cell
    for step, ref in enumerate(coef_refs):
        ref[...] = hold_ref[pl.ds(pl.multiple_of((where_ref[1] ^ step) * share, share), share), :]
    squares = coef * coef
    keep = lax.broadcasted_iota(jnp.int32, squares.shape, 0) >= 1
    squares = jnp.where(keep, squares, 0.0)
    sums = [
        jnp.sum(squares[at:at + BLOCK], axis=0, keepdims=True) for at in range(0, terms, BLOCK)
    ]
    total = functools.reduce(jnp.add, sums)
    for group in range(GROUPS):
        part = jnp.zeros_like(total)
        for at, value in enumerate(sums):
            part = part + jnp.where(group_ref[at] == group, value, 0.0)
        sobol_ref[group:group + 1, :] = part / total


def finish(where, inverse, scale, pieces, rows, block_group, samples, n_cell):
    terms = inverse.shape[0]
    cells = pieces[0].shape[1]
    share = jax.ShapeDtypeStruct((terms // n_cell, cells), jnp.float32)
    *shares, sobol = pl.pallas_call(
        functools.partial(finish_kernel, samples, n_cell, rows),
        out_shape=(share,) * n_cell + (jax.ShapeDtypeStruct((GROUPS, cells), jnp.float32),),
        in_specs=[SMEM, SMEM] + [VMEM] * (2 + len(pieces)),
        out_specs=(VMEM,) * (n_cell + 1),
        scratch_shapes=[pltpu.VMEM((terms, cells), jnp.float32)] * 2,
        compiler_params=BIG,
        name="finish",
    )(where, block_group, inverse, scale, *pieces)
    return shares, sobol


def join_kernel(where_ref, *refs):
    out_ref = refs[-1]
    for step, ref in enumerate(refs[:-1]):
        wide = ref.shape[1]
        out_ref[:, pl.ds(pl.multiple_of((where_ref[0] ^ step) * wide, wide), wide)] = ref[...]


def join_columns(where, shares):
    rows, wide = shares[0].shape
    return pl.pallas_call(
        join_kernel,
        out_shape=jax.ShapeDtypeStruct((rows, wide * len(shares)), jnp.float32),
        in_specs=[SMEM] + [VMEM] * len(shares),
        out_specs=VMEM,
        name="join_columns",
    )(where, *shares)


def swap(values, axis, step):
    size = lax.axis_size(axis)
    return lax.ppermute(values, axis, [(at, at ^ step) for at in range(size)])


def exchange(pieces):
    return lax.all_to_all(pieces, "samp", split_axis=0, concat_axis=0)


def spread(piece):
    return jnp.broadcast_to(piece[None], (lax.axis_size("samp"),) + piece.shape)


def halve(values, me, bit):
    rows, lanes = values.shape
    halves = values.reshape(2, rows // 2, lanes)
    mine = (me >> bit) & 1
    kept = lax.dynamic_index_in_dim(halves, mine, axis=0, keepdims=False)
    sent = lax.dynamic_index_in_dim(halves, mine ^ 1, axis=0, keepdims=False)
    return kept + swap(sent, "samp", 1 << bit)


def on_device(points, yields, term_index, block_group):
    n_samp = lax.axis_size("samp")
    n_cell = lax.axis_size("cell")
    me, cell = lax.axis_index("samp"), lax.axis_index("cell")
    blocks = term_index.shape[0] // TILE
    psi, fold = design(points, term_index, cell, n_cell)
    pieces = fold.reshape((n_samp, 8, -1) if fold.shape[0] % (8 * n_samp) else (n_samp, -1, fold.shape[1]))
    came = exchange(pieces)
    cross = jnp.dot(psi, yields, preferred_element_type=jnp.float32)
    came, cross = lax.optimization_barrier((came, cross))
    part = halve(cross, me, 0)
    fold = exchange(spread(jnp.sum(came, axis=0))).reshape(fold.shape)
    part = halve(part, me, 1)
    fold, part = lax.optimization_barrier((fold, part))
    part = halve(part, me, 2)
    bit = 8
    while bit < n_samp:
        part = part + swap(part, "samp", bit)
        bit *= 2
    held, order = [fold], [0]
    step = n_cell // 2
    while step:
        held = held + [swap(value, "cell", step) for value in held]
        order = order + [value ^ step for value in order]
        step //= 2
    held, part = lax.optimization_barrier((held, part))
    gram, scale = first_block(cell.reshape(1), [held[order.index(at)] for at in range(n_cell)], term_index.shape[0])
    rows = part.shape[0]
    for block in range(1, blocks):
        if block <= 2:
            part = jnp.concatenate([part, swap(part, "samp", 8 >> block)], axis=0)
            gram, part = lax.optimization_barrier((gram, part))
        gram = next_block(gram, block)
    pieces = [part, swap(part, "samp", 1)]
    spot = ((me & 1) << 2) | (me & 2) | ((me >> 2) & 1)
    where = jnp.stack([spot, cell])
    shares, sobol = finish(where, gram, scale, pieces, rows, block_group, points.shape[1] * n_samp, n_cell)
    shares = [shares[0]] + [swap(shares[step], "cell", step) for step in range(1, n_cell)]
    return (join_columns(cell.reshape(1), shares), sobol)


def solution(mesh):
    placed = (P(None, "samp"), P("samp", "cell"), P(), P())
    return jax.shard_map(
        on_device,
        mesh=mesh,
        in_specs=placed,
        out_specs=(P("cell", None), P(None, "cell")),
        check_vma=False,
    )
```

```python
import functools

import jax
import jax.numpy as jnp
from jax import lax
from jax.experimental import pallas as pl
from jax.experimental.pallas import tpu as pltpu
from jax.sharding import PartitionSpec as P

BLOCK = 64
GROUPS = 8
TILE = 128
HIGH = lax.Precision.HIGHEST
VMEM = pl.BlockSpec(memory_space=pltpu.VMEM)
SMEM = pl.BlockSpec(memory_space=pltpu.SMEM)
BIG = pltpu.CompilerParams(vmem_limit_bytes=16 * 2**20)
SMALL = pltpu.CompilerParams(vmem_limit_bytes=8 * 2**20)


def split3(values):
    top = values.astype(jnp.bfloat16).astype(jnp.float32)
    rest = values - top
    middle = rest.astype(jnp.bfloat16).astype(jnp.float32)
    return top, middle, rest - middle


def picks(column, params, width):
    span = 3 * params
    degree = column % 4
    place = (degree - 1) * params + column // 4
    at = lax.broadcasted_iota(jnp.int32, (width, column.shape[1]), 0)
    hit = (at == place) | (at == place + span) | (at == place + 2 * span)
    hit = (hit & (degree > 0)) | ((at == 3 * span) & (degree == 0))
    return hit.astype(jnp.float32).T.astype(jnp.bfloat16)


def design_kernel(chunk, cell_ref, index_ref, points_ref, psi_ref, fold_ref, table_ref):
    params, samples = points_ref.shape
    terms = index_ref.shape[1]
    width = table_ref.shape[0]
    span = 3 * params
    xs = points_ref[...]
    first = 1.7320508075688772 * xs
    second = 2.23606797749979 * (1.5 * xs * xs - 0.5)
    third = 2.6457513110645907 * (2.5 * xs * xs * xs - 1.5 * xs)
    for at, rows in enumerate((first, second, third)):
        for part, values in enumerate(split3(rows)):
            table_ref[pl.ds(part * span + at * params, params), :] = values
    table_ref[pl.ds(3 * span, width - 3 * span), :] = jnp.ones((width - 3 * span, samples), jnp.float32)
    pick_a = picks(index_ref[0:1, :], params, width)
    pick_b = picks(index_ref[1:2, :], params, width)
    for start in range(0, samples, chunk):
        table = table_ref[:, start:start + chunk].astype(jnp.bfloat16)
        left = jnp.dot(pick_a, table, preferred_element_type=jnp.float32)
        right = jnp.dot(pick_b, table, preferred_element_type=jnp.float32)
        psi_ref[:, start:start + chunk] = (left * right).astype(jnp.bfloat16)
    blocks = terms // TILE
    part_rows = fold_ref.shape[0] // 2
    cell = cell_ref[0]
    for block in range(blocks):
        rows = psi_ref[pl.ds(pl.multiple_of(block * TILE + cell * part_rows, part_rows), part_rows), :]
        reach = (block + 1) * TILE
        value = lax.dot_general(
            rows, psi_ref[0:reach, :], (((1,), (1,)), ((), ())), preferred_element_type=jnp.float32
        )
        half, at = fold_place(block, blocks)
        fold_ref[half * part_rows:(half + 1) * part_rows, at:at + reach] = value


def fold_place(block, blocks):
    low = min(block, blocks - 1 - block)
    return low, 0 if block == low else (low + 1) * TILE


def design(points, term_index, cell, n_cell):
    params, samples = points.shape
    terms = term_index.shape[0]
    blocks = terms // TILE
    rows = 2 * TILE // n_cell
    return pl.pallas_call(
        functools.partial(design_kernel, 512),
        out_shape=(
            jax.ShapeDtypeStruct((terms, samples), jnp.bfloat16),
            jax.ShapeDtypeStruct((rows, (blocks + 1) * TILE), jnp.float32),
        ),
        in_specs=[SMEM, VMEM, VMEM],
        out_specs=(VMEM, VMEM),
        scratch_shapes=[
            pltpu.VMEM((256, samples), jnp.float32),
        ],
        compiler_params=BIG,
        name="design",
    )(cell.reshape(1), term_index.T, points)


def cross_kernel(low_ref, psi_ref, yields_ref, kept_ref, sent_ref):
    rows = kept_ref.shape[0]
    for ref, which in ((sent_ref, low_ref[0] ^ 1), (kept_ref, low_ref[0])):
        part = psi_ref[pl.ds(pl.multiple_of(which * rows, rows), rows), :]
        ref[...] = jnp.dot(part, yields_ref[...], preferred_element_type=jnp.float32)


def cross_halves(psi, yields, low):
    half = jax.ShapeDtypeStruct((psi.shape[0] // 2, yields.shape[1]), jnp.float32)
    return pl.pallas_call(
        cross_kernel,
        out_shape=(half, half),
        in_specs=[SMEM, VMEM, VMEM],
        out_specs=(VMEM, VMEM),
        compiler_params=SMALL,
        name="cross_halves",
    )(low.reshape(1), psi, yields)


def lane_of(values, at):
    lanes = jnp.full(values.shape, at, jnp.int32)
    return jnp.take_along_axis(values, lanes, axis=1, mode="promise_in_bounds")


def row_of(values, at):
    return jnp.broadcast_to(values[at:at + 1, :], values.shape)


def sweep_tile(bands):
    bands = list(bands)
    shape = bands[0].shape
    subs = lax.broadcasted_iota(jnp.int32, shape, 0)
    lanes = lax.broadcasted_iota(jnp.int32, shape, 1)
    for at in range(len(bands)):
        base = 8 * at
        own = bands[at]
        inside = (lanes >= base) & (lanes < base + 8)
        columns = [lane_of(own, base + k) for k in range(8)]
        pivot = [[row_of(columns[k], i) if k <= i else None for k in range(8)] for i in range(8)]
        edged = jnp.where(inside, jnp.where(lanes == subs + base, -1.0, 0.0), own)
        rows = [row_of(edged, i) for i in range(8)]
        factor = [[None] * 8 for _ in range(8)]
        pairs = []
        for p in range(0, 8, 2):
            q = p + 1
            a, b, d = pivot[p][p], pivot[q][p], pivot[q][q]
            inverse = 1.0 / (a * d - b * b)
            pairs.append((a, b, d, inverse))
            mixed = [None] * 8
            for i in range(q + 1, 8):
                e, f = pivot[i][p], pivot[i][q]
                mixed[i] = (d * e - b * f, a * f - b * e)
                factor[i][p], factor[i][q] = mixed[i][0] * inverse, mixed[i][1] * inverse
            for i in range(q + 1, 8):
                for k in range(q + 1, i + 1):
                    less = mixed[i][0] * pivot[k][p] + mixed[i][1] * pivot[k][q]
                    pivot[i][k] = pivot[i][k] - less * inverse
                rows[i] = rows[i] - (factor[i][p] * rows[p] + factor[i][q] * rows[q])
        for p in range(0, 8, 2):
            a, b, d, inverse = pairs[p // 2]
            top, low = rows[p], rows[p + 1]
            rows[p], rows[p + 1] = (d * top - b * low) * inverse, (a * low - b * top) * inverse
        for p in range(6, 0, -2):
            for i in range(p):
                rows[i] = rows[i] - (factor[p][i] * rows[p] + factor[p + 1][i] * rows[p + 1])
        for step in range(1, len(bands)):
            other = (at + step) % len(bands)
            value = jnp.where(inside, 0.0, bands[other])
            for k in range(7, -1, -1):
                value = value - lane_of(bands[other], base + k) * rows[k]
            bands[other] = value
        fresh = rows[0]
        for i in range(1, 8):
            fresh = jnp.where(subs == i, rows[i], fresh)
        bands[at] = fresh
    return bands


def stacked_dot(left, right):
    a = [part.astype(jnp.bfloat16) for part in split3(left)]
    b = [part.astype(jnp.bfloat16) for part in split3(right)]
    left = jnp.concatenate([a[0], a[0], a[1], a[1], a[0], a[2]], axis=1)
    right = jnp.concatenate([b[0], b[1], b[0], b[1], b[2], b[0]], axis=0)
    return jnp.dot(left, right, preferred_element_type=jnp.float32)


def sweep_block(gram_ref, block):
    band = slice(block * TILE, (block + 1) * TILE)
    bands = sweep_tile(gram_ref[block * TILE + at:block * TILE + at + 8, band] for at in range(0, TILE, 8))
    minus = jnp.concatenate(bands, axis=0)
    old = gram_ref[band, :]
    columns = gram_ref[:, band]
    fresh = -stacked_dot(minus, old)
    gram_ref[...] -= stacked_dot(columns, fresh)
    gram_ref[band, :] = fresh
    gram_ref[:, band] = fresh.T
    gram_ref[band, band] = minus


def first_kernel(where_ref, *refs):
    out_ref, scale_ref = refs[-2:]
    terms = out_ref.shape[0]
    blocks = terms // TILE
    for step, ref in enumerate(refs[:-2]):
        piece = ref.shape[0] // 2
        start = pl.multiple_of((where_ref[0] ^ step) * piece, piece)
        for block in range(blocks):
            half, lane = fold_place(block, blocks)
            reach = (block + 1) * TILE
            out_ref[pl.ds(start + block * TILE, piece), 0:reach] = (
                ref[half * piece:(half + 1) * piece, lane:lane + reach]
            )
    for block in range(blocks):
        for other in range(block):
            tile = out_ref[block * TILE:(block + 1) * TILE, other * TILE:(other + 1) * TILE]
            out_ref[other * TILE:(other + 1) * TILE, block * TILE:(block + 1) * TILE] = tile.T
    diagonal = lax.broadcasted_iota(jnp.int32, (TILE, TILE), 0) == lax.broadcasted_iota(jnp.int32, (TILE, TILE), 1)
    across = []
    for block in range(blocks):
        band = slice(block * TILE, (block + 1) * TILE)
        only = jnp.where(diagonal, out_ref[band, band], 0.0)
        scale_ref[band, :] = lax.rsqrt(jnp.sum(only, axis=1, keepdims=True))
        across.append(lax.rsqrt(jnp.sum(only, axis=0, keepdims=True)))
    out_ref[...] = out_ref[...] * scale_ref[...] * jnp.concatenate(across, axis=1)
    sweep_block(out_ref, 0)


def next_kernel(block, in_ref, out_ref):
    out_ref[...] = in_ref[...]
    sweep_block(out_ref, block)


STEP_COST = pl.CostEstimate(flops=5 * 10**9, bytes_accessed=2 * 2**20, transcendentals=512)


def first_block(where, pieces, terms):
    return pl.pallas_call(
        first_kernel,
        out_shape=(
            jax.ShapeDtypeStruct((terms, terms), jnp.float32),
            jax.ShapeDtypeStruct((terms, 1), jnp.float32),
        ),
        in_specs=[SMEM] + [VMEM] * len(pieces),
        out_specs=(VMEM, VMEM),
        compiler_params=BIG,
        cost_estimate=STEP_COST,
        name="block_0",
    )(where, *pieces)


def next_block(gram, block):
    return pl.pallas_call(
        functools.partial(next_kernel, block),
        out_shape=jax.ShapeDtypeStruct(gram.shape, jnp.float32),
        in_specs=[VMEM],
        out_specs=VMEM,
        input_output_aliases={0: 0},
        compiler_params=BIG,
        cost_estimate=STEP_COST,
        name="block_%d" % block,
    )(gram)


def solve_kernel(samples, steps, rows, finish, where_ref, group_ref, inverse_ref, scale_ref, *refs):
    count = len(steps)
    pieces = refs[:2]
    others = refs[2:-(count + finish + 1)]
    cross_ref = refs[-1]
    shares = refs[-(count + finish + 1):-(finish + 1)]
    step = 0
    for ref in pieces:
        for at in range(0, ref.shape[0], rows):
            cross_ref[pl.ds(pl.multiple_of((where_ref[0] ^ step) * rows, rows), rows), :] = ref[at:at + rows, :]
            step += 1
    terms, cells = cross_ref.shape
    scaled = scale_ref[...] * cross_ref[...]
    size = jnp.sqrt(jnp.float32(samples))
    share = shares[0].shape[0]
    for step, ref in zip(steps, shares):
        band = pl.ds(pl.multiple_of((where_ref[1] ^ step) * share, share), share)
        value = jnp.dot(inverse_ref[band, :], scaled, precision=HIGH, preferred_element_type=jnp.float32)
        ref[...] = -scale_ref[band, :] * value * size
    if not finish:
        return
    sobol_ref = refs[-2]
    totals, labels = [], []
    for step, ref in enumerate(shares + others):
        owner = where_ref[1] ^ step
        value = ref[...] / size
        squares = value * value
        row = lax.broadcasted_iota(jnp.int32, squares.shape, 0) + owner * share
        squares = jnp.where(row >= 1, squares, 0.0)
        for at in range(0, share, BLOCK):
            totals.append(jnp.sum(squares[at:at + BLOCK], axis=0, keepdims=True))
            labels.append(group_ref[owner * (share // BLOCK) + at // BLOCK])
    total = functools.reduce(jnp.add, totals)
    for group in range(GROUPS):
        part = jnp.zeros_like(total)
        for label, value in zip(labels, totals):
            part = part + jnp.where(label == group, value, 0.0)
        sobol_ref[group:group + 1, :] = part / total


def solve(where, inverse, scale, pieces, rows, block_group, samples, n_cell, steps, others=()):
    terms = inverse.shape[0]
    cells = pieces[0].shape[1]
    finish = len(others) > 0
    out = (jax.ShapeDtypeStruct((terms // n_cell, cells), jnp.float32),) * len(steps)
    if finish:
        out += (jax.ShapeDtypeStruct((GROUPS, cells), jnp.float32),)
    return pl.pallas_call(
        functools.partial(solve_kernel, samples, steps, rows, finish),
        out_shape=out,
        in_specs=[SMEM, SMEM] + [VMEM] * (2 + len(pieces) + len(others)),
        out_specs=(VMEM,) * len(out),
        scratch_shapes=[pltpu.VMEM((terms, cells), jnp.float32)],
        compiler_params=BIG,
        name="solve_near" if finish else "solve_far",
    )(where, block_group, inverse, scale, *pieces, *others)


def join_kernel(where_ref, *refs):
    out_ref = refs[-1]
    for step, ref in enumerate(refs[:-1]):
        wide = ref.shape[1]
        out_ref[:, pl.ds(pl.multiple_of((where_ref[0] ^ step) * wide, wide), wide)] = ref[...]


def join_columns(where, shares):
    rows, wide = shares[0].shape
    return pl.pallas_call(
        join_kernel,
        out_shape=jax.ShapeDtypeStruct((rows, wide * len(shares)), jnp.float32),
        in_specs=[SMEM] + [VMEM] * len(shares),
        out_specs=VMEM,
        compiler_params=SMALL,
        name="join_columns",
    )(where, *shares)


def swap(values, axis, step):
    size = lax.axis_size(axis)
    return lax.ppermute(values, axis, [(at, at ^ step) for at in range(size)])


def exchange(pieces):
    return lax.all_to_all(pieces, "samp", split_axis=0, concat_axis=0)


def spread(piece):
    return jnp.broadcast_to(piece[None], (lax.axis_size("samp"),) + piece.shape)


def halve(values, me, bit):
    rows, lanes = values.shape
    halves = values.reshape(2, rows // 2, lanes)
    mine = (me >> bit) & 1
    kept = lax.dynamic_index_in_dim(halves, mine, axis=0, keepdims=False)
    sent = lax.dynamic_index_in_dim(halves, mine ^ 1, axis=0, keepdims=False)
    return kept + swap(sent, "samp", 1 << bit)


def on_device(points, yields, term_index, block_group):
    n_samp = lax.axis_size("samp")
    n_cell = lax.axis_size("cell")
    me, cell = lax.axis_index("samp"), lax.axis_index("cell")
    blocks = term_index.shape[0] // TILE
    psi, fold = design(points, term_index, cell, n_cell)
    pieces = fold.reshape((n_samp, 8, -1) if fold.shape[0] % (8 * n_samp) else (n_samp, -1, fold.shape[1]))
    came = exchange(pieces)
    kept, sent = cross_halves(psi, yields, me & 1)
    part = kept + swap(sent, "samp", 1)
    came, part = lax.optimization_barrier((came, part))
    fold = exchange(spread(jnp.sum(came, axis=0))).reshape(fold.shape)
    part = halve(part, me, 1)
    fold, part = lax.optimization_barrier((fold, part))
    part = halve(part, me, 2)
    bit = 8
    while bit < n_samp:
        part = part + swap(part, "samp", bit)
        bit *= 2
    held, order = [fold], [0]
    step = n_cell // 2
    while step:
        held = held + [swap(value, "cell", step) for value in held]
        order = order + [value ^ step for value in order]
        step //= 2
    held, part = lax.optimization_barrier((held, part))
    gram, scale = first_block(cell.reshape(1), [held[order.index(at)] for at in range(n_cell)], term_index.shape[0])
    rows = part.shape[0]
    for block in range(1, blocks):
        if block <= 2:
            part = jnp.concatenate([part, swap(part, "samp", 8 >> block)], axis=0)
            gram, part = lax.optimization_barrier((gram, part))
        gram = next_block(gram, block)
    pieces = [part, swap(part, "samp", 1)]
    spot = ((me & 1) << 2) | (me & 2) | ((me >> 2) & 1)
    where = jnp.stack([spot, cell])
    given = (where, gram, scale, pieces, rows, block_group, points.shape[1] * n_samp, n_cell)
    far = list(solve(*given, tuple(range(n_cell // 2, n_cell))))
    came = [swap(value, "cell", n_cell // 2 + at) for at, value in enumerate(far)]
    *near, sobol = solve(*given, tuple(range(n_cell // 2)), far)
    shares = [near[0]] + [swap(near[step], "cell", step) for step in range(1, n_cell // 2)] + came
    return (join_columns(cell.reshape(1), shares), sobol)


def solution(mesh):
    placed = (P(None, "samp"), P("samp", "cell"), P(), P())
    return jax.shard_map(
        on_device,
        mesh=mesh,
        in_specs=placed,
        out_specs=(P("cell", None), P(None, "cell")),
        check_vma=False,
    )
```

```python
import functools

import jax
import jax.numpy as jnp
from jax import lax
from jax.experimental import pallas as pl
from jax.experimental.pallas import tpu as pltpu
from jax.sharding import PartitionSpec as P

BLOCK = 64
GROUPS = 8
TILE = 128
HIGH = lax.Precision.HIGHEST
VMEM = pl.BlockSpec(memory_space=pltpu.VMEM)
SMEM = pl.BlockSpec(memory_space=pltpu.SMEM)
BIG = pltpu.CompilerParams(vmem_limit_bytes=16 * 2**20)
SMALL = pltpu.CompilerParams(vmem_limit_bytes=8 * 2**20)


def split3(values):
    top = values.astype(jnp.bfloat16).astype(jnp.float32)
    rest = values - top
    middle = rest.astype(jnp.bfloat16).astype(jnp.float32)
    return top, middle, rest - middle


def picks(column, params, width):
    span = 3 * params
    degree = column % 4
    place = (degree - 1) * params + column // 4
    at = lax.broadcasted_iota(jnp.int32, (width, column.shape[1]), 0)
    hit = (at == place) | (at == place + span) | (at == place + 2 * span)
    hit = (hit & (degree > 0)) | ((at == 3 * span) & (degree == 0))
    return hit.astype(jnp.float32).T.astype(jnp.bfloat16)


def design_kernel(chunk, cell_ref, index_ref, points_ref, psi_ref, fold_ref, table_ref):
    params, samples = points_ref.shape
    terms = index_ref.shape[1]
    width = table_ref.shape[0]
    span = 3 * params
    xs = points_ref[...]
    first = 1.7320508075688772 * xs
    second = 2.23606797749979 * (1.5 * xs * xs - 0.5)
    third = 2.6457513110645907 * (2.5 * xs * xs * xs - 1.5 * xs)
    for at, rows in enumerate((first, second, third)):
        for part, values in enumerate(split3(rows)):
            table_ref[pl.ds(part * span + at * params, params), :] = values
    table_ref[pl.ds(3 * span, width - 3 * span), :] = jnp.ones((width - 3 * span, samples), jnp.float32)
    pick_a = picks(index_ref[0:1, :], params, width)
    pick_b = picks(index_ref[1:2, :], params, width)
    for start in range(0, samples, chunk):
        table = table_ref[:, start:start + chunk].astype(jnp.bfloat16)
        left = jnp.dot(pick_a, table, preferred_element_type=jnp.float32)
        right = jnp.dot(pick_b, table, preferred_element_type=jnp.float32)
        psi_ref[:, start:start + chunk] = (left * right).astype(jnp.bfloat16)
    blocks = terms // TILE
    part_rows = fold_ref.shape[0] // 2
    cell = cell_ref[0]
    for block in range(blocks):
        rows = psi_ref[pl.ds(pl.multiple_of(block * TILE + cell * part_rows, part_rows), part_rows), :]
        reach = (block + 1) * TILE
        value = lax.dot_general(
            rows, psi_ref[0:reach, :], (((1,), (1,)), ((), ())), preferred_element_type=jnp.float32
        )
        half, at = fold_place(block, blocks)
        fold_ref[half * part_rows:(half + 1) * part_rows, at:at + reach] = value


def fold_place(block, blocks):
    low = min(block, blocks - 1 - block)
    return low, 0 if block == low else (low + 1) * TILE


def design(points, term_index, cell, n_cell):
    params, samples = points.shape
    terms = term_index.shape[0]
    blocks = terms // TILE
    rows = 2 * TILE // n_cell
    return pl.pallas_call(
        functools.partial(design_kernel, 512),
        out_shape=(
            jax.ShapeDtypeStruct((terms, samples), jnp.bfloat16),
            jax.ShapeDtypeStruct((rows, (blocks + 1) * TILE), jnp.float32),
        ),
        in_specs=[SMEM, VMEM, VMEM],
        out_specs=(VMEM, VMEM),
        scratch_shapes=[
            pltpu.VMEM((256, samples), jnp.float32),
        ],
        compiler_params=BIG,
        name="design",
    )(cell.reshape(1), term_index.T, points)


def cross_kernel(low_ref, psi_ref, yields_ref, kept_ref, sent_ref):
    rows = kept_ref.shape[0]
    for ref, which in ((sent_ref, low_ref[0] ^ 1), (kept_ref, low_ref[0])):
        part = psi_ref[pl.ds(pl.multiple_of(which * rows, rows), rows), :]
        ref[...] = jnp.dot(part, yields_ref[...], preferred_element_type=jnp.float32)


def cross_halves(psi, yields, low):
    half = jax.ShapeDtypeStruct((psi.shape[0] // 2, yields.shape[1]), jnp.float32)
    return pl.pallas_call(
        cross_kernel,
        out_shape=(half, half),
        in_specs=[SMEM, VMEM, VMEM],
        out_specs=(VMEM, VMEM),
        compiler_params=SMALL,
        name="cross_halves",
    )(low.reshape(1), psi, yields)


def lane_of(values, at):
    lanes = jnp.full(values.shape, at, jnp.int32)
    return jnp.take_along_axis(values, lanes, axis=1, mode="promise_in_bounds")


def row_of(values, at):
    return jnp.broadcast_to(values[at:at + 1, :], values.shape)


def sweep_tile(bands):
    bands = list(bands)
    shape = bands[0].shape
    subs = lax.broadcasted_iota(jnp.int32, shape, 0)
    lanes = lax.broadcasted_iota(jnp.int32, shape, 1)
    for at in range(len(bands)):
        base = 8 * at
        own = bands[at]
        inside = (lanes >= base) & (lanes < base + 8)
        columns = [lane_of(own, base + k) for k in range(8)]
        pivot = [[row_of(columns[k], i) if k <= i else None for k in range(8)] for i in range(8)]
        edged = jnp.where(inside, jnp.where(lanes == subs + base, -1.0, 0.0), own)
        rows = [row_of(edged, i) for i in range(8)]
        factor = [[None] * 8 for _ in range(8)]
        pairs = []
        for p in range(0, 8, 2):
            q = p + 1
            a, b, d = pivot[p][p], pivot[q][p], pivot[q][q]
            inverse = 1.0 / (a * d - b * b)
            pairs.append((a, b, d, inverse))
            mixed = [None] * 8
            for i in range(q + 1, 8):
                e, f = pivot[i][p], pivot[i][q]
                mixed[i] = (d * e - b * f, a * f - b * e)
                factor[i][p], factor[i][q] = mixed[i][0] * inverse, mixed[i][1] * inverse
            for i in range(q + 1, 8):
                for k in range(q + 1, i + 1):
                    less = mixed[i][0] * pivot[k][p] + mixed[i][1] * pivot[k][q]
                    pivot[i][k] = pivot[i][k] - less * inverse
                rows[i] = rows[i] - (factor[i][p] * rows[p] + factor[i][q] * rows[q])
        for p in range(0, 8, 2):
            a, b, d, inverse = pairs[p // 2]
            top, low = rows[p], rows[p + 1]
            rows[p], rows[p + 1] = (d * top - b * low) * inverse, (a * low - b * top) * inverse
        for p in range(6, 0, -2):
            for i in range(p):
                rows[i] = rows[i] - (factor[p][i] * rows[p] + factor[p + 1][i] * rows[p + 1])
        for step in range(1, len(bands)):
            other = (at + step) % len(bands)
            value = jnp.where(inside, 0.0, bands[other])
            for k in range(7, -1, -1):
                value = value - lane_of(bands[other], base + k) * rows[k]
            bands[other] = value
        fresh = rows[0]
        for i in range(1, 8):
            fresh = jnp.where(subs == i, rows[i], fresh)
        bands[at] = fresh
    return bands


def stacked_dot(left, right):
    a = [part.astype(jnp.bfloat16) for part in split3(left)]
    b = [part.astype(jnp.bfloat16) for part in split3(right)]
    left = jnp.concatenate([a[0], a[0], a[1], a[1], a[0], a[2]], axis=1)
    right = jnp.concatenate([b[0], b[1], b[0], b[1], b[2], b[0]], axis=0)
    return jnp.dot(left, right, preferred_element_type=jnp.float32)


def sweep_block(gram_ref, block):
    band = slice(block * TILE, (block + 1) * TILE)
    bands = sweep_tile(gram_ref[block * TILE + at:block * TILE + at + 8, band] for at in range(0, TILE, 8))
    minus = jnp.concatenate(bands, axis=0)
    old = gram_ref[band, :]
    columns = gram_ref[:, band]
    fresh = -stacked_dot(minus, old)
    gram_ref[...] -= stacked_dot(columns, fresh)
    gram_ref[band, :] = fresh
    gram_ref[:, band] = fresh.T
    gram_ref[band, band] = minus


def first_kernel(where_ref, *refs):
    out_ref, scale_ref = refs[-2:]
    terms = out_ref.shape[0]
    blocks = terms // TILE
    for step, ref in enumerate(refs[:-2]):
        piece = ref.shape[0] // 2
        start = pl.multiple_of((where_ref[0] ^ step) * piece, piece)
        for block in range(blocks):
            half, lane = fold_place(block, blocks)
            reach = (block + 1) * TILE
            out_ref[pl.ds(start + block * TILE, piece), 0:reach] = (
                ref[half * piece:(half + 1) * piece, lane:lane + reach]
            )
    for block in range(blocks):
        for other in range(block):
            tile = out_ref[block * TILE:(block + 1) * TILE, other * TILE:(other + 1) * TILE]
            out_ref[other * TILE:(other + 1) * TILE, block * TILE:(block + 1) * TILE] = tile.T
    diagonal = lax.broadcasted_iota(jnp.int32, (TILE, TILE), 0) == lax.broadcasted_iota(jnp.int32, (TILE, TILE), 1)
    across = []
    for block in range(blocks):
        band = slice(block * TILE, (block + 1) * TILE)
        only = jnp.where(diagonal, out_ref[band, band], 0.0)
        scale_ref[band, :] = lax.rsqrt(jnp.sum(only, axis=1, keepdims=True))
        across.append(lax.rsqrt(jnp.sum(only, axis=0, keepdims=True)))
    out_ref[...] = out_ref[...] * scale_ref[...] * jnp.concatenate(across, axis=1)
    sweep_block(out_ref, 0)


def next_kernel(block, in_ref, out_ref):
    out_ref[...] = in_ref[...]
    sweep_block(out_ref, block)


STEP_COST = pl.CostEstimate(flops=10**9, bytes_accessed=2**20, transcendentals=512)


def first_block(where, pieces, terms):
    return pl.pallas_call(
        first_kernel,
        out_shape=(
            jax.ShapeDtypeStruct((terms, terms), jnp.float32),
            jax.ShapeDtypeStruct((terms, 1), jnp.float32),
        ),
        in_specs=[SMEM] + [VMEM] * len(pieces),
        out_specs=(VMEM, VMEM),
        compiler_params=BIG,
        cost_estimate=STEP_COST,
        name="block_0",
    )(where, *pieces)


def next_block(gram, block):
    return pl.pallas_call(
        functools.partial(next_kernel, block),
        out_shape=jax.ShapeDtypeStruct(gram.shape, jnp.float32),
        in_specs=[VMEM],
        out_specs=VMEM,
        input_output_aliases={0: 0},
        compiler_params=BIG,
        cost_estimate=STEP_COST,
        name="block_%d" % block,
    )(gram)


def solve_kernel(samples, steps, rows, finish, where_ref, group_ref, inverse_ref, scale_ref, *refs):
    count = len(steps)
    pieces = refs[:2]
    others = refs[2:-(count + finish + 1)]
    cross_ref = refs[-1]
    shares = refs[-(count + finish + 1):-(finish + 1)]
    step = 0
    for ref in pieces:
        for at in range(0, ref.shape[0], rows):
            cross_ref[pl.ds(pl.multiple_of((where_ref[0] ^ step) * rows, rows), rows), :] = ref[at:at + rows, :]
            step += 1
    terms, cells = cross_ref.shape
    scaled = scale_ref[...] * cross_ref[...]
    size = jnp.sqrt(jnp.float32(samples))
    share = shares[0].shape[0]
    for step, ref in zip(steps, shares):
        band = pl.ds(pl.multiple_of((where_ref[1] ^ step) * share, share), share)
        value = jnp.dot(inverse_ref[band, :], scaled, precision=HIGH, preferred_element_type=jnp.float32)
        ref[...] = -scale_ref[band, :] * value * size
    if not finish:
        return
    sobol_ref = refs[-2]
    totals, labels = [], []
    for step, ref in enumerate(shares + others):
        owner = where_ref[1] ^ step
        value = ref[...] / size
        squares = value * value
        row = lax.broadcasted_iota(jnp.int32, squares.shape, 0) + owner * share
        squares = jnp.where(row >= 1, squares, 0.0)
        for at in range(0, share, BLOCK):
            totals.append(jnp.sum(squares[at:at + BLOCK], axis=0, keepdims=True))
            labels.append(group_ref[owner * (share // BLOCK) + at // BLOCK])
    total = functools.reduce(jnp.add, totals)
    for group in range(GROUPS):
        part = jnp.zeros_like(total)
        for label, value in zip(labels, totals):
            part = part + jnp.where(label == group, value, 0.0)
        sobol_ref[group:group + 1, :] = part / total


def solve(where, inverse, scale, pieces, rows, block_group, samples, n_cell, steps, others=()):
    terms = inverse.shape[0]
    cells = pieces[0].shape[1]
    finish = len(others) > 0
    out = (jax.ShapeDtypeStruct((terms // n_cell, cells), jnp.float32),) * len(steps)
    if finish:
        out += (jax.ShapeDtypeStruct((GROUPS, cells), jnp.float32),)
    return pl.pallas_call(
        functools.partial(solve_kernel, samples, steps, rows, finish),
        out_shape=out,
        in_specs=[SMEM, SMEM] + [VMEM] * (2 + len(pieces) + len(others)),
        out_specs=(VMEM,) * len(out),
        scratch_shapes=[pltpu.VMEM((terms, cells), jnp.float32)],
        compiler_params=BIG,
        cost_estimate=pl.CostEstimate(flops=(5 if finish else 1) * 10**9, bytes_accessed=2**20, transcendentals=0),
        name="solve_near" if finish else "solve_far",
    )(where, block_group, inverse, scale, *pieces, *others)


def join_kernel(where_ref, *refs):
    out_ref = refs[-1]
    for step, ref in enumerate(refs[:-1]):
        wide = ref.shape[1]
        out_ref[:, pl.ds(pl.multiple_of((where_ref[0] ^ step) * wide, wide), wide)] = ref[...]


def join_columns(where, shares):
    rows, wide = shares[0].shape
    return pl.pallas_call(
        join_kernel,
        out_shape=jax.ShapeDtypeStruct((rows, wide * len(shares)), jnp.float32),
        in_specs=[SMEM] + [VMEM] * len(shares),
        out_specs=VMEM,
        compiler_params=SMALL,
        name="join_columns",
    )(where, *shares)


def swap(values, axis, step):
    size = lax.axis_size(axis)
    return lax.ppermute(values, axis, [(at, at ^ step) for at in range(size)])


def pick(values, at):
    return lax.dynamic_index_in_dim(values, at, axis=0, keepdims=False)


def exchange(pieces):
    return lax.all_to_all(pieces, "samp", split_axis=0, concat_axis=0)


def spread(piece):
    return jnp.broadcast_to(piece[None], (lax.axis_size("samp"),) + piece.shape)


def on_device(points, yields, term_index, block_group):
    n_samp = lax.axis_size("samp")
    n_cell = lax.axis_size("cell")
    me, cell = lax.axis_index("samp"), lax.axis_index("cell")
    blocks = term_index.shape[0] // TILE
    psi, fold = design(points, term_index, cell, n_cell)
    pieces = fold.reshape((n_samp, 8, -1) if fold.shape[0] % (8 * n_samp) else (n_samp, -1, fold.shape[1]))
    came = exchange(pieces)
    kept, sent = cross_halves(psi, yields, me & 1)
    came, kept, sent = lax.optimization_barrier((came, kept, sent))
    half = kept + swap(sent, "samp", 1)
    fold = exchange(spread(jnp.sum(came, axis=0))).reshape(fold.shape)
    fold, half = lax.optimization_barrier((fold, half))
    quarters = half.reshape(4, half.shape[0] // 4, half.shape[1])
    mine = (me & 2) | ((me >> 2) & 1)
    part = pick(quarters, mine)
    for flip, step in ((1, 4), (2, 2), (3, 6)):
        part = part + swap(pick(quarters, mine ^ flip), "samp", step)
    bit = 8
    while bit < n_samp:
        part = part + swap(part, "samp", bit)
        bit *= 2
    held, order = [fold], [0]
    step = n_cell // 2
    while step:
        held = held + [swap(value, "cell", step) for value in held]
        order = order + [value ^ step for value in order]
        step //= 2
    held, part = lax.optimization_barrier((held, part))
    gram, scale = first_block(cell.reshape(1), [held[order.index(at)] for at in range(n_cell)], term_index.shape[0])
    rows = part.shape[0]
    for block in range(1, blocks):
        if block <= 2:
            part = jnp.concatenate([part, swap(part, "samp", 8 >> block)], axis=0)
            gram, part = lax.optimization_barrier((gram, part))
        gram = next_block(gram, block)
    pieces = [part, swap(part, "samp", 1)]
    spot = ((me & 1) << 2) | mine
    where = jnp.stack([spot, cell])
    given = (where, gram, scale, pieces, rows, block_group, points.shape[1] * n_samp, n_cell)
    far = list(solve(*given, tuple(range(n_cell // 2, n_cell))))
    came = [swap(value, "cell", n_cell // 2 + at) for at, value in enumerate(far)]
    *near, sobol = solve(*given, tuple(range(n_cell // 2)), far)
    shares = [near[0]] + [swap(near[step], "cell", step) for step in range(1, n_cell // 2)] + came
    return (join_columns(cell.reshape(1), shares), sobol)


def solution(mesh):
    placed = (P(None, "samp"), P("samp", "cell"), P(), P())
    return jax.shard_map(
        on_device,
        mesh=mesh,
        in_specs=placed,
        out_specs=(P("cell", None), P(None, "cell")),
        check_vma=False,
    )
```

```python
import functools

import jax
import jax.numpy as jnp
from jax import lax
from jax.experimental import pallas as pl
from jax.experimental.pallas import tpu as pltpu
from jax.sharding import PartitionSpec as P

BLOCK = 64
GROUPS = 8
TILE = 128
HIGH = lax.Precision.HIGHEST
VMEM = pl.BlockSpec(memory_space=pltpu.VMEM)
SMEM = pl.BlockSpec(memory_space=pltpu.SMEM)
BIG = pltpu.CompilerParams(vmem_limit_bytes=16 * 2**20)
SMALL = pltpu.CompilerParams(vmem_limit_bytes=8 * 2**20)


def split3(values):
    top = values.astype(jnp.bfloat16).astype(jnp.float32)
    rest = values - top
    middle = rest.astype(jnp.bfloat16).astype(jnp.float32)
    return top, middle, rest - middle


def picks(column, params, width):
    span = 3 * params
    degree = column % 4
    place = (degree - 1) * params + column // 4
    at = lax.broadcasted_iota(jnp.int32, (width, column.shape[1]), 0)
    hit = (at == place) | (at == place + span) | (at == place + 2 * span)
    hit = (hit & (degree > 0)) | ((at == 3 * span) & (degree == 0))
    return hit.astype(jnp.float32).T.astype(jnp.bfloat16)


def design_kernel(chunk, cell_ref, index_ref, points_ref, psi_ref, fold_ref, table_ref):
    params, samples = points_ref.shape
    terms = index_ref.shape[1]
    width = table_ref.shape[0]
    span = 3 * params
    xs = points_ref[...]
    first = 1.7320508075688772 * xs
    second = 2.23606797749979 * (1.5 * xs * xs - 0.5)
    third = 2.6457513110645907 * (2.5 * xs * xs * xs - 1.5 * xs)
    for at, rows in enumerate((first, second, third)):
        for part, values in enumerate(split3(rows)):
            table_ref[pl.ds(part * span + at * params, params), :] = values
    table_ref[pl.ds(3 * span, width - 3 * span), :] = jnp.ones((width - 3 * span, samples), jnp.float32)
    pick_a = picks(index_ref[0:1, :], params, width)
    pick_b = picks(index_ref[1:2, :], params, width)
    for start in range(0, samples, chunk):
        table = table_ref[:, start:start + chunk].astype(jnp.bfloat16)
        left = jnp.dot(pick_a, table, preferred_element_type=jnp.float32)
        right = jnp.dot(pick_b, table, preferred_element_type=jnp.float32)
        psi_ref[:, start:start + chunk] = (left * right).astype(jnp.bfloat16)
    blocks = terms // TILE
    part_rows = fold_ref.shape[0] // 2
    cell = cell_ref[0]
    for block in range(blocks):
        rows = psi_ref[pl.ds(pl.multiple_of(block * TILE + cell * part_rows, part_rows), part_rows), :]
        reach = (block + 1) * TILE
        value = lax.dot_general(
            rows, psi_ref[0:reach, :], (((1,), (1,)), ((), ())), preferred_element_type=jnp.float32
        )
        half, at = fold_place(block, blocks)
        fold_ref[half * part_rows:(half + 1) * part_rows, at:at + reach] = value


def fold_place(block, blocks):
    low = min(block, blocks - 1 - block)
    return low, 0 if block == low else (low + 1) * TILE


def design(points, term_index, cell, n_cell):
    params, samples = points.shape
    terms = term_index.shape[0]
    blocks = terms // TILE
    rows = 2 * TILE // n_cell
    return pl.pallas_call(
        functools.partial(design_kernel, 512),
        out_shape=(
            jax.ShapeDtypeStruct((terms, samples), jnp.bfloat16),
            jax.ShapeDtypeStruct((rows, (blocks + 1) * TILE), jnp.float32),
        ),
        in_specs=[SMEM, VMEM, VMEM],
        out_specs=(VMEM, VMEM),
        scratch_shapes=[
            pltpu.VMEM((256, samples), jnp.float32),
        ],
        compiler_params=BIG,
        name="design",
    )(cell.reshape(1), term_index.T, points)


def cross_kernel(low_ref, psi_ref, yields_ref, kept_ref, sent_ref):
    rows = kept_ref.shape[0]
    for ref, which in ((sent_ref, low_ref[0] ^ 1), (kept_ref, low_ref[0])):
        part = psi_ref[pl.ds(pl.multiple_of(which * rows, rows), rows), :]
        ref[...] = jnp.dot(part, yields_ref[...], preferred_element_type=jnp.float32)


def cross_halves(psi, yields, low):
    half = jax.ShapeDtypeStruct((psi.shape[0] // 2, yields.shape[1]), jnp.float32)
    return pl.pallas_call(
        cross_kernel,
        out_shape=(half, half),
        in_specs=[SMEM, VMEM, VMEM],
        out_specs=(VMEM, VMEM),
        compiler_params=SMALL,
        name="cross_halves",
    )(low.reshape(1), psi, yields)


def lane_of(values, at):
    lanes = jnp.full(values.shape, at, jnp.int32)
    return jnp.take_along_axis(values, lanes, axis=1, mode="promise_in_bounds")


def row_of(values, at):
    return jnp.broadcast_to(values[at:at + 1, :], values.shape)


def sweep_tile(bands):
    bands = list(bands)
    shape = bands[0].shape
    subs = lax.broadcasted_iota(jnp.int32, shape, 0)
    lanes = lax.broadcasted_iota(jnp.int32, shape, 1)
    for at in range(len(bands)):
        base = 8 * at
        own = bands[at]
        inside = (lanes >= base) & (lanes < base + 8)
        columns = [lane_of(own, base + k) for k in range(8)]
        fresh = jnp.where(inside, jnp.where(lanes == subs + base, -1.0, 0.0), own)
        for p in range(8):
            inverse = 1.0 / row_of(columns[p], p)
            factor = jnp.where(subs == p, 1.0 - inverse, columns[p] * inverse)
            for k in range(p + 1, 8):
                columns[k] = columns[k] - factor * row_of(columns[k], p)
            fresh = fresh - factor * row_of(fresh, p)
        rows = [row_of(fresh, k) for k in range(8)]
        for step in range(1, len(bands)):
            other = (at + step) % len(bands)
            value = jnp.where(inside, 0.0, bands[other])
            for k in range(8):
                value = value - lane_of(bands[other], base + k) * rows[k]
            bands[other] = value
        bands[at] = fresh
    return bands


def stacked_dot(left, right):
    a = [part.astype(jnp.bfloat16) for part in split3(left)]
    b = [part.astype(jnp.bfloat16) for part in split3(right)]
    left = jnp.concatenate([a[0], a[0], a[1], a[1], a[0], a[2]], axis=1)
    right = jnp.concatenate([b[0], b[1], b[0], b[1], b[2], b[0]], axis=0)
    return jnp.dot(left, right, preferred_element_type=jnp.float32)


def sweep_block(gram_ref, block):
    band = slice(block * TILE, (block + 1) * TILE)
    bands = sweep_tile(gram_ref[block * TILE + at:block * TILE + at + 8, band] for at in range(0, TILE, 8))
    minus = jnp.concatenate(bands, axis=0)
    old = gram_ref[band, :]
    columns = gram_ref[:, band]
    fresh = -stacked_dot(minus, old)
    gram_ref[...] -= stacked_dot(columns, fresh)
    gram_ref[band, :] = fresh
    gram_ref[:, band] = fresh.T
    gram_ref[band, band] = minus


def first_kernel(where_ref, *refs):
    out_ref, scale_ref = refs[-2:]
    terms = out_ref.shape[0]
    blocks = terms // TILE
    for step, ref in enumerate(refs[:-2]):
        piece = ref.shape[0] // 2
        start = pl.multiple_of((where_ref[0] ^ step) * piece, piece)
        for block in range(blocks):
            half, lane = fold_place(block, blocks)
            reach = (block + 1) * TILE
            out_ref[pl.ds(start + block * TILE, piece), 0:reach] = (
                ref[half * piece:(half + 1) * piece, lane:lane + reach]
            )
    for block in range(blocks):
        for other in range(block):
            tile = out_ref[block * TILE:(block + 1) * TILE, other * TILE:(other + 1) * TILE]
            out_ref[other * TILE:(other + 1) * TILE, block * TILE:(block + 1) * TILE] = tile.T
    diagonal = lax.broadcasted_iota(jnp.int32, (TILE, TILE), 0) == lax.broadcasted_iota(jnp.int32, (TILE, TILE), 1)
    across = []
    for block in range(blocks):
        band = slice(block * TILE, (block + 1) * TILE)
        only = jnp.where(diagonal, out_ref[band, band], 0.0)
        scale_ref[band, :] = lax.rsqrt(jnp.sum(only, axis=1, keepdims=True))
        across.append(lax.rsqrt(jnp.sum(only, axis=0, keepdims=True)))
    out_ref[...] = out_ref[...] * scale_ref[...] * jnp.concatenate(across, axis=1)
    sweep_block(out_ref, 0)


def next_kernel(block, in_ref, out_ref):
    out_ref[...] = in_ref[...]
    sweep_block(out_ref, block)


STEP_COST = pl.CostEstimate(flops=10**9, bytes_accessed=2**20, transcendentals=512)


def first_block(where, pieces, terms):
    return pl.pallas_call(
        first_kernel,
        out_shape=(
            jax.ShapeDtypeStruct((terms, terms), jnp.float32),
            jax.ShapeDtypeStruct((terms, 1), jnp.float32),
        ),
        in_specs=[SMEM] + [VMEM] * len(pieces),
        out_specs=(VMEM, VMEM),
        compiler_params=BIG,
        cost_estimate=STEP_COST,
        name="block_0",
    )(where, *pieces)


def next_block(gram, block):
    return pl.pallas_call(
        functools.partial(next_kernel, block),
        out_shape=jax.ShapeDtypeStruct(gram.shape, jnp.float32),
        in_specs=[VMEM],
        out_specs=VMEM,
        input_output_aliases={0: 0},
        compiler_params=BIG,
        cost_estimate=STEP_COST,
        name="block_%d" % block,
    )(gram)


def solve_kernel(samples, steps, rows, finish, where_ref, group_ref, inverse_ref, scale_ref, *refs):
    count = len(steps)
    pieces = refs[:4]
    others = refs[4:-(count + finish + 1)]
    cross_ref = refs[-1]
    shares = refs[-(count + finish + 1):-(finish + 1)]
    step = 0
    for ref in pieces:
        for at in range(0, ref.shape[0], rows):
            cross_ref[pl.ds(pl.multiple_of((where_ref[0] ^ step) * rows, rows), rows), :] = ref[at:at + rows, :]
            step += 1
    terms, cells = cross_ref.shape
    scaled = scale_ref[...] * cross_ref[...]
    size = jnp.sqrt(jnp.float32(samples))
    share = shares[0].shape[0]
    for step, ref in zip(steps, shares):
        band = pl.ds(pl.multiple_of((where_ref[1] ^ step) * share, share), share)
        value = jnp.dot(inverse_ref[band, :], scaled, precision=HIGH, preferred_element_type=jnp.float32)
        ref[...] = -scale_ref[band, :] * value * size
    if not finish:
        return
    sobol_ref = refs[-2]
    totals, labels = [], []
    for step, ref in enumerate(shares + others):
        owner = where_ref[1] ^ step
        value = ref[...] / size
        squares = value * value
        row = lax.broadcasted_iota(jnp.int32, squares.shape, 0) + owner * share
        squares = jnp.where(row >= 1, squares, 0.0)
        for at in range(0, share, BLOCK):
            totals.append(jnp.sum(squares[at:at + BLOCK], axis=0, keepdims=True))
            labels.append(group_ref[owner * (share // BLOCK) + at // BLOCK])
    total = functools.reduce(jnp.add, totals)
    for group in range(GROUPS):
        part = jnp.zeros_like(total)
        for label, value in zip(labels, totals):
            part = part + jnp.where(label == group, value, 0.0)
        sobol_ref[group:group + 1, :] = part / total


def solve(where, inverse, scale, pieces, rows, block_group, samples, n_cell, steps, others=()):
    terms = inverse.shape[0]
    cells = pieces[0].shape[1]
    finish = len(others) > 0
    out = (jax.ShapeDtypeStruct((terms // n_cell, cells), jnp.float32),) * len(steps)
    if finish:
        out += (jax.ShapeDtypeStruct((GROUPS, cells), jnp.float32),)
    return pl.pallas_call(
        functools.partial(solve_kernel, samples, steps, rows, finish),
        out_shape=out,
        in_specs=[SMEM, SMEM] + [VMEM] * (2 + len(pieces) + len(others)),
        out_specs=(VMEM,) * len(out),
        scratch_shapes=[pltpu.VMEM((terms, cells), jnp.float32)],
        compiler_params=BIG,
        cost_estimate=pl.CostEstimate(flops=(5 if finish else 1) * 10**9, bytes_accessed=2**20, transcendentals=0),
        name="solve_near" if finish else "solve_far",
    )(where, block_group, inverse, scale, *pieces, *others)


def join_kernel(where_ref, *refs):
    out_ref = refs[-1]
    for step, ref in enumerate(refs[:-1]):
        wide = ref.shape[1]
        out_ref[:, pl.ds(pl.multiple_of((where_ref[0] ^ step) * wide, wide), wide)] = ref[...]


def join_columns(where, shares):
    rows, wide = shares[0].shape
    return pl.pallas_call(
        join_kernel,
        out_shape=jax.ShapeDtypeStruct((rows, wide * len(shares)), jnp.float32),
        in_specs=[SMEM] + [VMEM] * len(shares),
        out_specs=VMEM,
        compiler_params=SMALL,
        name="join_columns",
    )(where, *shares)


def swap(values, axis, step):
    size = lax.axis_size(axis)
    return lax.ppermute(values, axis, [(at, at ^ step) for at in range(size)])


def pick(values, at):
    return lax.dynamic_index_in_dim(values, at, axis=0, keepdims=False)


def halve(values, me, bit):
    halves = values.reshape(2, values.shape[0] // 2, values.shape[1])
    mine = (me >> bit) & 1
    return pick(halves, mine) + swap(pick(halves, mine ^ 1), "samp", 1 << bit)


def exchange(pieces):
    return lax.all_to_all(pieces, "samp", split_axis=0, concat_axis=0)


def spread(piece):
    return jnp.broadcast_to(piece[None], (lax.axis_size("samp"),) + piece.shape)


def on_device(points, yields, term_index, block_group):
    n_samp = lax.axis_size("samp")
    n_cell = lax.axis_size("cell")
    me, cell = lax.axis_index("samp"), lax.axis_index("cell")
    blocks = term_index.shape[0] // TILE
    psi, fold = design(points, term_index, cell, n_cell)
    pieces = fold.reshape((n_samp, 8, -1) if fold.shape[0] % (8 * n_samp) else (n_samp, -1, fold.shape[1]))
    came = exchange(pieces)
    kept, sent = cross_halves(psi, yields, me & 1)
    came, kept, sent = lax.optimization_barrier((came, kept, sent))
    half = kept + swap(sent, "samp", 1)
    fold = exchange(spread(jnp.sum(came, axis=0))).reshape(fold.shape)
    fold, half = lax.optimization_barrier((fold, half))
    part = halve(half, me, 1)
    held, order = [fold], [0]
    step = n_cell // 2
    while step:
        held = held + [swap(value, "cell", step) for value in held]
        order = order + [value ^ step for value in order]
        step //= 2
    held, part = lax.optimization_barrier((held, part))
    gram, scale = first_block(cell.reshape(1), [held[order.index(at)] for at in range(n_cell)], term_index.shape[0])
    part = halve(part, me, 2)
    bit = 8
    while bit < n_samp:
        part = part + swap(part, "samp", bit)
        bit *= 2
    rows = part.shape[0]
    for block in range(1, blocks):
        if block == 1:
            gram, part = lax.optimization_barrier((gram, part))
            pair = jnp.concatenate([part, swap(part, "samp", 4)], axis=0)
        elif block == 2:
            gram, pair = lax.optimization_barrier((gram, pair))
            pieces = [pair, swap(pair, "samp", 2), swap(pair, "samp", 1)]
        elif block == 3:
            gram, pieces = lax.optimization_barrier((gram, pieces))
            pieces = pieces + [swap(pieces[1], "samp", 1)]
        gram = next_block(gram, block)
    spot = ((me & 1) << 2) | (me & 2) | ((me >> 2) & 1)
    where = jnp.stack([spot, cell])
    given = (where, gram, scale, pieces, rows, block_group, points.shape[1] * n_samp, n_cell)
    far = list(solve(*given, tuple(range(1, n_cell))))
    came = [swap(value, "cell", 1 + at) for at, value in enumerate(far)]
    near, sobol = solve(*given, (0,), far)
    shares = [near] + came
    return (join_columns(cell.reshape(1), shares), sobol)


def solution(mesh):
    placed = (P(None, "samp"), P("samp", "cell"), P(), P())
    return jax.shard_map(
        on_device,
        mesh=mesh,
        in_specs=placed,
        out_specs=(P("cell", None), P(None, "cell")),
        check_vma=False,
    )
```

```python
import functools

import jax
import jax.numpy as jnp
from jax import lax
from jax.experimental import pallas as pl
from jax.experimental.pallas import tpu as pltpu
from jax.sharding import PartitionSpec as P

BLOCK = 64
GROUPS = 8
TILE = 128
HIGH = lax.Precision.HIGHEST
VMEM = pl.BlockSpec(memory_space=pltpu.VMEM)
SMEM = pl.BlockSpec(memory_space=pltpu.SMEM)
BIG = pltpu.CompilerParams(vmem_limit_bytes=16 * 2**20)
SMALL = pltpu.CompilerParams(vmem_limit_bytes=8 * 2**20)


def split3(values):
    top = values.astype(jnp.bfloat16).astype(jnp.float32)
    rest = values - top
    middle = rest.astype(jnp.bfloat16).astype(jnp.float32)
    return top, middle, rest - middle


def picks(column, params, width):
    span = 3 * params
    degree = column % 4
    place = (degree - 1) * params + column // 4
    at = lax.broadcasted_iota(jnp.int32, (width, column.shape[1]), 0)
    hit = (at == place) | (at == place + span) | (at == place + 2 * span)
    hit = (hit & (degree > 0)) | ((at == 3 * span) & (degree == 0))
    return hit.astype(jnp.float32).T.astype(jnp.bfloat16)


def design_kernel(chunk, cell_ref, index_ref, points_ref, psi_ref, fold_ref, table_ref):
    params, samples = points_ref.shape
    terms = index_ref.shape[1]
    width = table_ref.shape[0]
    span = 3 * params
    xs = points_ref[...]
    first = 1.7320508075688772 * xs
    second = 2.23606797749979 * (1.5 * xs * xs - 0.5)
    third = 2.6457513110645907 * (2.5 * xs * xs * xs - 1.5 * xs)
    for at, rows in enumerate((first, second, third)):
        for part, values in enumerate(split3(rows)):
            table_ref[pl.ds(part * span + at * params, params), :] = values
    table_ref[pl.ds(3 * span, width - 3 * span), :] = jnp.ones((width - 3 * span, samples), jnp.float32)
    pick_a = picks(index_ref[0:1, :], params, width)
    pick_b = picks(index_ref[1:2, :], params, width)
    for start in range(0, samples, chunk):
        table = table_ref[:, start:start + chunk].astype(jnp.bfloat16)
        left = jnp.dot(pick_a, table, preferred_element_type=jnp.float32)
        right = jnp.dot(pick_b, table, preferred_element_type=jnp.float32)
        psi_ref[:, start:start + chunk] = (left * right).astype(jnp.bfloat16)
    blocks = terms // TILE
    part_rows = fold_ref.shape[0] // 2
    cell = cell_ref[0]
    for block in range(blocks):
        rows = psi_ref[pl.ds(pl.multiple_of(block * TILE + cell * part_rows, part_rows), part_rows), :]
        reach = (block + 1) * TILE
        value = lax.dot_general(
            rows, psi_ref[0:reach, :], (((1,), (1,)), ((), ())), preferred_element_type=jnp.float32
        )
        half, at = fold_place(block, blocks)
        fold_ref[half * part_rows:(half + 1) * part_rows, at:at + reach] = value


def fold_place(block, blocks):
    low = min(block, blocks - 1 - block)
    return low, 0 if block == low else (low + 1) * TILE


def design(points, term_index, cell, n_cell):
    params, samples = points.shape
    terms = term_index.shape[0]
    blocks = terms // TILE
    rows = 2 * TILE // n_cell
    return pl.pallas_call(
        functools.partial(design_kernel, 512),
        out_shape=(
            jax.ShapeDtypeStruct((terms, samples), jnp.bfloat16),
            jax.ShapeDtypeStruct((rows, (blocks + 1) * TILE), jnp.float32),
        ),
        in_specs=[SMEM, VMEM, VMEM],
        out_specs=(VMEM, VMEM),
        scratch_shapes=[
            pltpu.VMEM((256, samples), jnp.float32),
        ],
        compiler_params=BIG,
        name="design",
    )(cell.reshape(1), term_index.T, points)


def cross_kernel(low_ref, psi_ref, yields_ref, kept_ref, sent_ref):
    rows = kept_ref.shape[0]
    for ref, which in ((sent_ref, low_ref[0] ^ 1), (kept_ref, low_ref[0])):
        part = psi_ref[pl.ds(pl.multiple_of(which * rows, rows), rows), :]
        ref[...] = jnp.dot(part, yields_ref[...], preferred_element_type=jnp.float32)


def cross_halves(psi, yields, low):
    half = jax.ShapeDtypeStruct((psi.shape[0] // 2, yields.shape[1]), jnp.float32)
    return pl.pallas_call(
        cross_kernel,
        out_shape=(half, half),
        in_specs=[SMEM, VMEM, VMEM],
        out_specs=(VMEM, VMEM),
        compiler_params=SMALL,
        name="cross_halves",
    )(low.reshape(1), psi, yields)


def lane_of(values, at):
    lanes = jnp.full(values.shape, at, jnp.int32)
    return jnp.take_along_axis(values, lanes, axis=1, mode="promise_in_bounds")


def row_of(values, at):
    return jnp.broadcast_to(values[at:at + 1, :], values.shape)


def stacked_outer(left, right):
    a, b = split3(left), split3(right)
    left = jnp.concatenate([a[0], a[0], a[1], a[1], a[0], a[2]], axis=0).astype(jnp.bfloat16)
    right = jnp.concatenate([b[0], b[1], b[0], b[1], b[2], b[0]], axis=0).astype(jnp.bfloat16)
    return lax.dot_general(left, right, (((0,), (0,)), ((), ())), preferred_element_type=jnp.float32)


def sweep_tile(bands):
    bands = list(bands)
    shape = bands[0].shape
    subs = lax.broadcasted_iota(jnp.int32, shape, 0)
    lanes = lax.broadcasted_iota(jnp.int32, shape, 1)
    for at in range(len(bands)):
        base = 8 * at
        own = bands[at]
        inside = (lanes >= base) & (lanes < base + 8)
        columns = [lane_of(own, base + k) for k in range(8)]
        fresh = jnp.where(inside, jnp.where(lanes == subs + base, -1.0, 0.0), own)
        for p in range(8):
            inverse = 1.0 / row_of(columns[p], p)
            factor = jnp.where(subs == p, 1.0 - inverse, columns[p] * inverse)
            for k in range(p + 1, 8):
                columns[k] = columns[k] - factor * row_of(columns[k], p)
            fresh = fresh - factor * row_of(fresh, p)
        delta = stacked_outer(own, fresh)
        following = (at + 1) % len(bands)
        for other in range(len(bands)):
            value = jnp.where(inside, 0.0, bands[other])
            if other == following:
                for k in range(8):
                    value = value - lane_of(bands[other], base + k) * row_of(fresh, k)
            else:
                value = value - delta[8 * other:8 * other + 8]
            bands[other] = value
        bands[at] = fresh
    return bands


def stacked_dot(left, right):
    a = [part.astype(jnp.bfloat16) for part in split3(left)]
    b = [part.astype(jnp.bfloat16) for part in split3(right)]
    left = jnp.concatenate([a[0], a[0], a[1], a[1], a[0], a[2]], axis=1)
    right = jnp.concatenate([b[0], b[1], b[0], b[1], b[2], b[0]], axis=0)
    return jnp.dot(left, right, preferred_element_type=jnp.float32)


def sweep_block(gram_ref, block):
    band = slice(block * TILE, (block + 1) * TILE)
    bands = sweep_tile(gram_ref[block * TILE + at:block * TILE + at + 8, band] for at in range(0, TILE, 8))
    minus = jnp.concatenate(bands, axis=0)
    old = gram_ref[band, :]
    columns = gram_ref[:, band]
    fresh = -stacked_dot(minus, old)
    gram_ref[...] -= stacked_dot(columns, fresh)
    gram_ref[band, :] = fresh
    gram_ref[:, band] = fresh.T
    gram_ref[band, band] = minus


def first_kernel(where_ref, *refs):
    out_ref, scale_ref = refs[-2:]
    terms = out_ref.shape[0]
    blocks = terms // TILE
    for step, ref in enumerate(refs[:-2]):
        piece = ref.shape[0] // 2
        start = pl.multiple_of((where_ref[0] ^ step) * piece, piece)
        for block in range(blocks):
            half, lane = fold_place(block, blocks)
            reach = (block + 1) * TILE
            out_ref[pl.ds(start + block * TILE, piece), 0:reach] = (
                ref[half * piece:(half + 1) * piece, lane:lane + reach]
            )
    for block in range(blocks):
        for other in range(block):
            tile = out_ref[block * TILE:(block + 1) * TILE, other * TILE:(other + 1) * TILE]
            out_ref[other * TILE:(other + 1) * TILE, block * TILE:(block + 1) * TILE] = tile.T
    diagonal = lax.broadcasted_iota(jnp.int32, (TILE, TILE), 0) == lax.broadcasted_iota(jnp.int32, (TILE, TILE), 1)
    across = []
    for block in range(blocks):
        band = slice(block * TILE, (block + 1) * TILE)
        only = jnp.where(diagonal, out_ref[band, band], 0.0)
        scale_ref[band, :] = lax.rsqrt(jnp.sum(only, axis=1, keepdims=True))
        across.append(lax.rsqrt(jnp.sum(only, axis=0, keepdims=True)))
    out_ref[...] = out_ref[...] * scale_ref[...] * jnp.concatenate(across, axis=1)
    sweep_block(out_ref, 0)


def next_kernel(block, in_ref, out_ref):
    out_ref[...] = in_ref[...]
    sweep_block(out_ref, block)


STEP_COST = pl.CostEstimate(flops=10**9, bytes_accessed=2**20, transcendentals=512)


def first_block(where, pieces, terms):
    return pl.pallas_call(
        first_kernel,
        out_shape=(
            jax.ShapeDtypeStruct((terms, terms), jnp.float32),
            jax.ShapeDtypeStruct((terms, 1), jnp.float32),
        ),
        in_specs=[SMEM] + [VMEM] * len(pieces),
        out_specs=(VMEM, VMEM),
        compiler_params=BIG,
        cost_estimate=STEP_COST,
        name="block_0",
    )(where, *pieces)


def next_block(gram, block):
    return pl.pallas_call(
        functools.partial(next_kernel, block),
        out_shape=jax.ShapeDtypeStruct(gram.shape, jnp.float32),
        in_specs=[VMEM],
        out_specs=VMEM,
        input_output_aliases={0: 0},
        compiler_params=BIG,
        cost_estimate=STEP_COST,
        name="block_%d" % block,
    )(gram)


def solve_kernel(samples, steps, rows, finish, where_ref, group_ref, inverse_ref, scale_ref, *refs):
    count = len(steps)
    pieces = refs[:4]
    others = refs[4:-(count + finish + 1)]
    cross_ref = refs[-1]
    shares = refs[-(count + finish + 1):-(finish + 1)]
    step = 0
    for ref in pieces:
        for at in range(0, ref.shape[0], rows):
            cross_ref[pl.ds(pl.multiple_of((where_ref[0] ^ step) * rows, rows), rows), :] = ref[at:at + rows, :]
            step += 1
    terms, cells = cross_ref.shape
    scaled = scale_ref[...] * cross_ref[...]
    size = jnp.sqrt(jnp.float32(samples))
    share = shares[0].shape[0]
    for step, ref in zip(steps, shares):
        band = pl.ds(pl.multiple_of((where_ref[1] ^ step) * share, share), share)
        value = jnp.dot(inverse_ref[band, :], scaled, precision=HIGH, preferred_element_type=jnp.float32)
        ref[...] = -scale_ref[band, :] * value * size
    if not finish:
        return
    sobol_ref = refs[-2]
    totals, labels = [], []
    for step, ref in enumerate(shares + others):
        owner = where_ref[1] ^ step
        value = ref[...] / size
        squares = value * value
        row = lax.broadcasted_iota(jnp.int32, squares.shape, 0) + owner * share
        squares = jnp.where(row >= 1, squares, 0.0)
        for at in range(0, share, BLOCK):
            totals.append(jnp.sum(squares[at:at + BLOCK], axis=0, keepdims=True))
            labels.append(group_ref[owner * (share // BLOCK) + at // BLOCK])
    total = functools.reduce(jnp.add, totals)
    for group in range(GROUPS):
        part = jnp.zeros_like(total)
        for label, value in zip(labels, totals):
            part = part + jnp.where(label == group, value, 0.0)
        sobol_ref[group:group + 1, :] = part / total


def solve(where, inverse, scale, pieces, rows, block_group, samples, n_cell, steps, others=()):
    terms = inverse.shape[0]
    cells = pieces[0].shape[1]
    finish = len(others) > 0
    out = (jax.ShapeDtypeStruct((terms // n_cell, cells), jnp.float32),) * len(steps)
    if finish:
        out += (jax.ShapeDtypeStruct((GROUPS, cells), jnp.float32),)
    return pl.pallas_call(
        functools.partial(solve_kernel, samples, steps, rows, finish),
        out_shape=out,
        in_specs=[SMEM, SMEM] + [VMEM] * (2 + len(pieces) + len(others)),
        out_specs=(VMEM,) * len(out),
        scratch_shapes=[pltpu.VMEM((terms, cells), jnp.float32)],
        compiler_params=BIG,
        cost_estimate=pl.CostEstimate(flops=(5 if finish else 1) * 10**9, bytes_accessed=2**20, transcendentals=0),
        name="solve_near" if finish else "solve_far",
    )(where, block_group, inverse, scale, *pieces, *others)


def join_kernel(where_ref, *refs):
    out_ref = refs[-1]
    for step, ref in enumerate(refs[:-1]):
        wide = ref.shape[1]
        out_ref[:, pl.ds(pl.multiple_of((where_ref[0] ^ step) * wide, wide), wide)] = ref[...]


def join_columns(where, shares):
    rows, wide = shares[0].shape
    return pl.pallas_call(
        join_kernel,
        out_shape=jax.ShapeDtypeStruct((rows, wide * len(shares)), jnp.float32),
        in_specs=[SMEM] + [VMEM] * len(shares),
        out_specs=VMEM,
        compiler_params=SMALL,
        name="join_columns",
    )(where, *shares)


def swap(values, axis, step):
    size = lax.axis_size(axis)
    return lax.ppermute(values, axis, [(at, at ^ step) for at in range(size)])


def pick(values, at):
    return lax.dynamic_index_in_dim(values, at, axis=0, keepdims=False)


def halve(values, me, bit):
    halves = values.reshape(2, values.shape[0] // 2, values.shape[1])
    mine = (me >> bit) & 1
    return pick(halves, mine) + swap(pick(halves, mine ^ 1), "samp", 1 << bit)


def exchange(pieces):
    return lax.all_to_all(pieces, "samp", split_axis=0, concat_axis=0)


def spread(piece):
    return jnp.broadcast_to(piece[None], (lax.axis_size("samp"),) + piece.shape)


def on_device(points, yields, term_index, block_group):
    n_samp = lax.axis_size("samp")
    n_cell = lax.axis_size("cell")
    me, cell = lax.axis_index("samp"), lax.axis_index("cell")
    blocks = term_index.shape[0] // TILE
    psi, fold = design(points, term_index, cell, n_cell)
    pieces = fold.reshape((n_samp, 8, -1) if fold.shape[0] % (8 * n_samp) else (n_samp, -1, fold.shape[1]))
    came = exchange(pieces)
    kept, sent = cross_halves(psi, yields, me & 1)
    came, kept, sent = lax.optimization_barrier((came, kept, sent))
    half = kept + swap(sent, "samp", 1)
    fold = exchange(spread(jnp.sum(came, axis=0))).reshape(fold.shape)
    fold, half = lax.optimization_barrier((fold, half))
    part = halve(half, me, 1)
    held, order = [fold], [0]
    step = n_cell // 2
    while step:
        held = held + [swap(value, "cell", step) for value in held]
        order = order + [value ^ step for value in order]
        step //= 2
    held, part = lax.optimization_barrier((held, part))
    gram, scale = first_block(cell.reshape(1), [held[order.index(at)] for at in range(n_cell)], term_index.shape[0])
    part = halve(part, me, 2)
    bit = 8
    while bit < n_samp:
        part = part + swap(part, "samp", bit)
        bit *= 2
    rows = part.shape[0]
    for block in range(1, blocks):
        if block == 1:
            gram, part = lax.optimization_barrier((gram, part))
            pair = jnp.concatenate([part, swap(part, "samp", 4)], axis=0)
        elif block == 2:
            gram, pair = lax.optimization_barrier((gram, pair))
            pieces = [pair, swap(pair, "samp", 2), swap(pair, "samp", 1)]
        elif block == 3:
            gram, pieces = lax.optimization_barrier((gram, pieces))
            pieces = pieces + [swap(pieces[1], "samp", 1)]
        gram = next_block(gram, block)
    spot = ((me & 1) << 2) | (me & 2) | ((me >> 2) & 1)
    where = jnp.stack([spot, cell])
    given = (where, gram, scale, pieces, rows, block_group, points.shape[1] * n_samp, n_cell)
    far = list(solve(*given, tuple(range(1, n_cell))))
    came = [swap(value, "cell", 1 + at) for at, value in enumerate(far)]
    near, sobol = solve(*given, (0,), far)
    shares = [near] + came
    return (join_columns(cell.reshape(1), shares), sobol)


def solution(mesh):
    placed = (P(None, "samp"), P("samp", "cell"), P(), P())
    return jax.shard_map(
        on_device,
        mesh=mesh,
        in_specs=placed,
        out_specs=(P("cell", None), P(None, "cell")),
        check_vma=False,
    )
```

```python
import functools

import jax
import jax.numpy as jnp
from jax import lax
from jax.experimental import pallas as pl
from jax.experimental.pallas import tpu as pltpu
from jax.sharding import PartitionSpec as P

BLOCK = 64
GROUPS = 8
TILE = 128
HIGH = lax.Precision.HIGHEST
VMEM = pl.BlockSpec(memory_space=pltpu.VMEM)
SMEM = pl.BlockSpec(memory_space=pltpu.SMEM)
BIG = pltpu.CompilerParams(vmem_limit_bytes=16 * 2**20)
SMALL = pltpu.CompilerParams(vmem_limit_bytes=8 * 2**20)


def split3(values):
    top = values.astype(jnp.bfloat16).astype(jnp.float32)
    rest = values - top
    middle = rest.astype(jnp.bfloat16).astype(jnp.float32)
    return top, middle, rest - middle


def picks(column, params, width):
    span = 3 * params
    degree = column % 4
    place = (degree - 1) * params + column // 4
    at = lax.broadcasted_iota(jnp.int32, (width, column.shape[1]), 0)
    hit = (at == place) | (at == place + span) | (at == place + 2 * span)
    hit = (hit & (degree > 0)) | ((at == 3 * span) & (degree == 0))
    return hit.astype(jnp.float32).T.astype(jnp.bfloat16)


def design_kernel(chunk, cell_ref, index_ref, points_ref, psi_ref, fold_ref, table_ref):
    params, samples = points_ref.shape
    terms = index_ref.shape[1]
    width = table_ref.shape[0]
    span = 3 * params
    xs = points_ref[...]
    first = 1.7320508075688772 * xs
    second = 2.23606797749979 * (1.5 * xs * xs - 0.5)
    third = 2.6457513110645907 * (2.5 * xs * xs * xs - 1.5 * xs)
    for at, rows in enumerate((first, second, third)):
        for part, values in enumerate(split3(rows)):
            table_ref[pl.ds(part * span + at * params, params), :] = values
    table_ref[pl.ds(3 * span, width - 3 * span), :] = jnp.ones((width - 3 * span, samples), jnp.float32)
    pick_a = picks(index_ref[0:1, :], params, width)
    pick_b = picks(index_ref[1:2, :], params, width)
    for start in range(0, samples, chunk):
        table = table_ref[:, start:start + chunk].astype(jnp.bfloat16)
        left = jnp.dot(pick_a, table, preferred_element_type=jnp.float32)
        right = jnp.dot(pick_b, table, preferred_element_type=jnp.float32)
        psi_ref[:, start:start + chunk] = (left * right).astype(jnp.bfloat16)
    blocks = terms // TILE
    part_rows = fold_ref.shape[0] // 2
    cell = cell_ref[0]
    for block in range(blocks):
        rows = psi_ref[pl.ds(pl.multiple_of(block * TILE + cell * part_rows, part_rows), part_rows), :]
        reach = (block + 1) * TILE
        value = lax.dot_general(
            rows, psi_ref[0:reach, :], (((1,), (1,)), ((), ())), preferred_element_type=jnp.float32
        )
        half, at = fold_place(block, blocks)
        fold_ref[half * part_rows:(half + 1) * part_rows, at:at + reach] = value


def fold_place(block, blocks):
    low = min(block, blocks - 1 - block)
    return low, 0 if block == low else (low + 1) * TILE


def design(points, term_index, cell, n_cell):
    params, samples = points.shape
    terms = term_index.shape[0]
    blocks = terms // TILE
    rows = 2 * TILE // n_cell
    return pl.pallas_call(
        functools.partial(design_kernel, 512),
        out_shape=(
            jax.ShapeDtypeStruct((terms, samples), jnp.bfloat16),
            jax.ShapeDtypeStruct((rows, (blocks + 1) * TILE), jnp.float32),
        ),
        in_specs=[SMEM, VMEM, VMEM],
        out_specs=(VMEM, VMEM),
        scratch_shapes=[
            pltpu.VMEM((256, samples), jnp.float32),
        ],
        compiler_params=BIG,
        name="design",
    )(cell.reshape(1), term_index.T, points)


def cross_kernel(low_ref, psi_ref, yields_ref, kept_ref, sent_ref):
    rows = kept_ref.shape[0]
    for ref, which in ((sent_ref, low_ref[0] ^ 1), (kept_ref, low_ref[0])):
        part = psi_ref[pl.ds(pl.multiple_of(which * rows, rows), rows), :]
        ref[...] = jnp.dot(part, yields_ref[...], preferred_element_type=jnp.float32)


def cross_halves(psi, yields, low):
    half = jax.ShapeDtypeStruct((psi.shape[0] // 2, yields.shape[1]), jnp.float32)
    return pl.pallas_call(
        cross_kernel,
        out_shape=(half, half),
        in_specs=[SMEM, VMEM, VMEM],
        out_specs=(VMEM, VMEM),
        compiler_params=SMALL,
        name="cross_halves",
    )(low.reshape(1), psi, yields)


def lane_of(values, at):
    lanes = jnp.full(values.shape, at, jnp.int32)
    return jnp.take_along_axis(values, lanes, axis=1, mode="promise_in_bounds")


def row_of(values, at):
    return jnp.broadcast_to(values[at:at + 1, :], values.shape)


def stacked_outer(left, right):
    a, b = split3(left), split3(right)
    left = jnp.concatenate([a[0], a[0], a[1], a[1], a[0], a[2]], axis=0).astype(jnp.bfloat16)
    right = jnp.concatenate([b[0], b[1], b[0], b[1], b[2], b[0]], axis=0).astype(jnp.bfloat16)
    return lax.dot_general(left, right, (((0,), (0,)), ((), ())), preferred_element_type=jnp.float32)


def sweep_tile(bands):
    bands = list(bands)
    shape = bands[0].shape
    subs = lax.broadcasted_iota(jnp.int32, shape, 0)
    lanes = lax.broadcasted_iota(jnp.int32, shape, 1)
    for at in range(len(bands)):
        base = 8 * at
        own = bands[at]
        inside = (lanes >= base) & (lanes < base + 8)
        columns = [lane_of(own, base + k) for k in range(8)]
        fresh = jnp.where(inside, jnp.where(lanes == subs + base, -1.0, 0.0), own)
        for p in range(8):
            inverse = 1.0 / row_of(columns[p], p)
            factor = jnp.where(subs == p, 1.0 - inverse, columns[p] * inverse)
            for k in range(p + 1, 8):
                columns[k] = columns[k] - factor * row_of(columns[k], p)
            fresh = fresh - factor * row_of(fresh, p)
        delta = stacked_outer(own, fresh)
        following = (at + 1) % len(bands)
        for other in range(len(bands)):
            value = jnp.where(inside, 0.0, bands[other])
            if other == following:
                for k in range(8):
                    value = value - lane_of(bands[other], base + k) * row_of(fresh, k)
            else:
                value = value - delta[8 * other:8 * other + 8]
            bands[other] = value
        bands[at] = fresh
    return bands


def stacked_dot(left, right):
    a = [part.astype(jnp.bfloat16) for part in split3(left)]
    b = [part.astype(jnp.bfloat16) for part in split3(right)]
    left = jnp.concatenate([a[0], a[0], a[1], a[1], a[0], a[2]], axis=1)
    right = jnp.concatenate([b[0], b[1], b[0], b[1], b[2], b[0]], axis=0)
    return jnp.dot(left, right, preferred_element_type=jnp.float32)


def sweep_block(gram, out_ref, minus, block):
    terms = out_ref.shape[0]
    band = slice(block * TILE, (block + 1) * TILE)
    whole = slice(0, terms)
    fresh = -stacked_dot(minus, gram(band, whole))
    parts = [minus if at == block * TILE else fresh[:, at:at + TILE] for at in range(0, terms, TILE)]
    fresh = jnp.concatenate(parts, axis=1)
    change = stacked_dot(gram(whole, band), fresh)
    inside = (lax.broadcasted_iota(jnp.int32, (TILE, terms), 1) // TILE) == block
    for at in range(0, terms, TILE):
        rows = slice(at, at + TILE)
        if at == block * TILE:
            out_ref[rows, :] = fresh
        else:
            out_ref[rows, :] = jnp.where(inside, 0.0, gram(rows, whole)) - change[rows, :]


def sweep(tile):
    return jnp.concatenate(sweep_tile([tile[at:at + 8, :] for at in range(0, TILE, 8)]), axis=0)


def first_kernel(where_ref, *refs):
    out_ref, scale_ref, gram_ref = refs[-3:]
    terms = out_ref.shape[0]
    blocks = terms // TILE
    for step, ref in enumerate(refs[:-3]):
        piece = ref.shape[0] // 2
        start = pl.multiple_of((where_ref[0] ^ step) * piece, piece)
        for block in range(blocks):
            half, lane = fold_place(block, blocks)
            reach = (block + 1) * TILE
            gram_ref[pl.ds(start + block * TILE, piece), 0:reach] = (
                ref[half * piece:(half + 1) * piece, lane:lane + reach]
            )
    diagonal = lax.broadcasted_iota(jnp.int32, (TILE, TILE), 0) == lax.broadcasted_iota(jnp.int32, (TILE, TILE), 1)
    bands = [slice(block * TILE, (block + 1) * TILE) for block in range(blocks)]
    across, down = [], []
    for band in bands:
        only = jnp.where(diagonal, gram_ref[band, band], 0.0)
        down.append(lax.rsqrt(jnp.sum(only, axis=1, keepdims=True)))
        across.append(lax.rsqrt(jnp.sum(only, axis=0, keepdims=True)))
    tiles = {}
    for i, band in enumerate(bands):
        scale_ref[band, :] = down[i]
        for j in range(i + 1):
            tiles[i, j] = gram_ref[band, bands[j]] * down[i] * across[j]
    minus = sweep(tiles[0, 0])
    for i, band in enumerate(bands):
        for j in range(i + 1):
            gram_ref[band, bands[j]] = tiles[i, j]
            if j < i:
                gram_ref[bands[j], band] = tiles[i, j].T
    sweep_block(lambda rows, lanes: gram_ref[rows, lanes], out_ref, minus, 0)


def next_kernel(block, in_ref, out_ref):
    band = slice(block * TILE, (block + 1) * TILE)
    sweep_block(lambda rows, lanes: in_ref[rows, lanes], out_ref, sweep(in_ref[band, band]), block)


STEP_COST = pl.CostEstimate(flops=10**9, bytes_accessed=2**20, transcendentals=512)


def first_block(where, pieces, terms):
    return pl.pallas_call(
        first_kernel,
        out_shape=(
            jax.ShapeDtypeStruct((terms, terms), jnp.float32),
            jax.ShapeDtypeStruct((terms, 1), jnp.float32),
        ),
        in_specs=[SMEM] + [VMEM] * len(pieces),
        out_specs=(VMEM, VMEM),
        scratch_shapes=[pltpu.VMEM((terms, terms), jnp.float32)],
        compiler_params=BIG,
        cost_estimate=STEP_COST,
        name="block_0",
    )(where, *pieces)


def next_block(gram, block):
    return pl.pallas_call(
        functools.partial(next_kernel, block),
        out_shape=jax.ShapeDtypeStruct(gram.shape, jnp.float32),
        in_specs=[VMEM],
        out_specs=VMEM,
        compiler_params=BIG,
        cost_estimate=STEP_COST,
        name="block_%d" % block,
    )(gram)


def solve_kernel(samples, steps, rows, finish, where_ref, group_ref, inverse_ref, scale_ref, *refs):
    count = len(steps)
    pieces = refs[:4]
    others = refs[4:-(count + finish + 1)]
    cross_ref = refs[-1]
    shares = refs[-(count + finish + 1):-(finish + 1)]
    step = 0
    for ref in pieces:
        for at in range(0, ref.shape[0], rows):
            cross_ref[pl.ds(pl.multiple_of((where_ref[0] ^ step) * rows, rows), rows), :] = ref[at:at + rows, :]
            step += 1
    terms, cells = cross_ref.shape
    scaled = scale_ref[...] * cross_ref[...]
    size = jnp.sqrt(jnp.float32(samples))
    share = shares[0].shape[0]
    for step, ref in zip(steps, shares):
        band = pl.ds(pl.multiple_of((where_ref[1] ^ step) * share, share), share)
        value = jnp.dot(inverse_ref[band, :], scaled, precision=HIGH, preferred_element_type=jnp.float32)
        ref[...] = -scale_ref[band, :] * value * size
    if not finish:
        return
    sobol_ref = refs[-2]
    totals, labels = [], []
    for step, ref in enumerate(shares + others):
        owner = where_ref[1] ^ step
        value = ref[...] / size
        squares = value * value
        row = lax.broadcasted_iota(jnp.int32, squares.shape, 0) + owner * share
        squares = jnp.where(row >= 1, squares, 0.0)
        for at in range(0, share, BLOCK):
            totals.append(jnp.sum(squares[at:at + BLOCK], axis=0, keepdims=True))
            labels.append(group_ref[owner * (share // BLOCK) + at // BLOCK])
    total = functools.reduce(jnp.add, totals)
    for group in range(GROUPS):
        part = jnp.zeros_like(total)
        for label, value in zip(labels, totals):
            part = part + jnp.where(label == group, value, 0.0)
        sobol_ref[group:group + 1, :] = part / total


def solve(where, inverse, scale, pieces, rows, block_group, samples, n_cell, steps, others=()):
    terms = inverse.shape[0]
    cells = pieces[0].shape[1]
    finish = len(others) > 0
    out = (jax.ShapeDtypeStruct((terms // n_cell, cells), jnp.float32),) * len(steps)
    if finish:
        out += (jax.ShapeDtypeStruct((GROUPS, cells), jnp.float32),)
    return pl.pallas_call(
        functools.partial(solve_kernel, samples, steps, rows, finish),
        out_shape=out,
        in_specs=[SMEM, SMEM] + [VMEM] * (2 + len(pieces) + len(others)),
        out_specs=(VMEM,) * len(out),
        scratch_shapes=[pltpu.VMEM((terms, cells), jnp.float32)],
        compiler_params=BIG,
        cost_estimate=pl.CostEstimate(flops=(5 if finish else 1) * 10**9, bytes_accessed=2**20, transcendentals=0),
        name="solve_near" if finish else "solve_far",
    )(where, block_group, inverse, scale, *pieces, *others)


def join_kernel(where_ref, *refs):
    out_ref = refs[-1]
    for step, ref in enumerate(refs[:-1]):
        wide = ref.shape[1]
        out_ref[:, pl.ds(pl.multiple_of((where_ref[0] ^ step) * wide, wide), wide)] = ref[...]


def join_columns(where, shares):
    rows, wide = shares[0].shape
    return pl.pallas_call(
        join_kernel,
        out_shape=jax.ShapeDtypeStruct((rows, wide * len(shares)), jnp.float32),
        in_specs=[SMEM] + [VMEM] * len(shares),
        out_specs=VMEM,
        compiler_params=SMALL,
        name="join_columns",
    )(where, *shares)


def swap(values, axis, step):
    size = lax.axis_size(axis)
    return lax.ppermute(values, axis, [(at, at ^ step) for at in range(size)])


def pick(values, at):
    return lax.dynamic_index_in_dim(values, at, axis=0, keepdims=False)


def halve(values, me, bit):
    halves = values.reshape(2, values.shape[0] // 2, values.shape[1])
    mine = (me >> bit) & 1
    return pick(halves, mine) + swap(pick(halves, mine ^ 1), "samp", 1 << bit)


def exchange(pieces):
    return lax.all_to_all(pieces, "samp", split_axis=0, concat_axis=0)


def spread(piece):
    return jnp.broadcast_to(piece[None], (lax.axis_size("samp"),) + piece.shape)


def on_device(points, yields, term_index, block_group):
    n_samp = lax.axis_size("samp")
    n_cell = lax.axis_size("cell")
    me, cell = lax.axis_index("samp"), lax.axis_index("cell")
    blocks = term_index.shape[0] // TILE
    psi, fold = design(points, term_index, cell, n_cell)
    pieces = fold.reshape((n_samp, 8, -1) if fold.shape[0] % (8 * n_samp) else (n_samp, -1, fold.shape[1]))
    came = exchange(pieces)
    kept, sent = cross_halves(psi, yields, me & 1)
    came, kept, sent = lax.optimization_barrier((came, kept, sent))
    half = kept + swap(sent, "samp", 1)
    fold = exchange(spread(jnp.sum(came, axis=0))).reshape(fold.shape)
    fold, half = lax.optimization_barrier((fold, half))
    part = halve(half, me, 1)
    held, order = [fold], [0]
    step = n_cell // 2
    while step:
        held = held + [swap(value, "cell", step) for value in held]
        order = order + [value ^ step for value in order]
        step //= 2
    held, part = lax.optimization_barrier((held, part))
    gram, scale = first_block(cell.reshape(1), [held[order.index(at)] for at in range(n_cell)], term_index.shape[0])
    part = halve(part, me, 2)
    bit = 8
    while bit < n_samp:
        part = part + swap(part, "samp", bit)
        bit *= 2
    rows = part.shape[0]
    for block in range(1, blocks):
        if block == 1:
            gram, part = lax.optimization_barrier((gram, part))
            pair = jnp.concatenate([part, swap(part, "samp", 4)], axis=0)
        elif block == 2:
            gram, pair = lax.optimization_barrier((gram, pair))
            pieces = [pair, swap(pair, "samp", 2), swap(pair, "samp", 1)]
        elif block == 3:
            gram, pieces = lax.optimization_barrier((gram, pieces))
            pieces = pieces + [swap(pieces[1], "samp", 1)]
        gram = next_block(gram, block)
    spot = ((me & 1) << 2) | (me & 2) | ((me >> 2) & 1)
    where = jnp.stack([spot, cell])
    given = (where, gram, scale, pieces, rows, block_group, points.shape[1] * n_samp, n_cell)
    far = list(solve(*given, tuple(range(1, n_cell))))
    came = [swap(value, "cell", 1 + at) for at, value in enumerate(far)]
    near, sobol = solve(*given, (0,), far)
    shares = [near] + came
    return (join_columns(cell.reshape(1), shares), sobol)


def solution(mesh):
    placed = (P(None, "samp"), P("samp", "cell"), P(), P())
    return jax.shard_map(
        on_device,
        mesh=mesh,
        in_specs=placed,
        out_specs=(P("cell", None), P(None, "cell")),
        check_vma=False,
    )
```

```python
import functools

import jax
import jax.numpy as jnp
from jax import lax
from jax.experimental import pallas as pl
from jax.experimental.pallas import tpu as pltpu
from jax.sharding import PartitionSpec as P

BLOCK = 64
GROUPS = 8
TILE = 128
HIGH = lax.Precision.HIGHEST
VMEM = pl.BlockSpec(memory_space=pltpu.VMEM)
SMEM = pl.BlockSpec(memory_space=pltpu.SMEM)
BIG = pltpu.CompilerParams(vmem_limit_bytes=16 * 2**20)
SMALL = pltpu.CompilerParams(vmem_limit_bytes=8 * 2**20)


def split3(values):
    top = values.astype(jnp.bfloat16).astype(jnp.float32)
    rest = values - top
    middle = rest.astype(jnp.bfloat16).astype(jnp.float32)
    return top, middle, rest - middle


def picks(column, params, width):
    span = 3 * params
    degree = column % 4
    place = (degree - 1) * params + column // 4
    at = lax.broadcasted_iota(jnp.int32, (width, column.shape[1]), 0)
    hit = (at == place) | (at == place + span) | (at == place + 2 * span)
    hit = (hit & (degree > 0)) | ((at == 3 * span) & (degree == 0))
    return hit.astype(jnp.float32).T.astype(jnp.bfloat16)


def design_kernel(chunk, cell_ref, index_ref, points_ref, psi_ref, fold_ref, table_ref):
    params, samples = points_ref.shape
    terms = index_ref.shape[1]
    width = table_ref.shape[0]
    span = 3 * params
    xs = points_ref[...]
    first = 1.7320508075688772 * xs
    second = 2.23606797749979 * (1.5 * xs * xs - 0.5)
    third = 2.6457513110645907 * (2.5 * xs * xs * xs - 1.5 * xs)
    for at, rows in enumerate((first, second, third)):
        for part, values in enumerate(split3(rows)):
            table_ref[pl.ds(part * span + at * params, params), :] = values
    table_ref[pl.ds(3 * span, width - 3 * span), :] = jnp.ones((width - 3 * span, samples), jnp.float32)
    pick_a = picks(index_ref[0:1, :], params, width)
    pick_b = picks(index_ref[1:2, :], params, width)
    for start in range(0, samples, chunk):
        table = table_ref[:, start:start + chunk].astype(jnp.bfloat16)
        left = jnp.dot(pick_a, table, preferred_element_type=jnp.float32)
        right = jnp.dot(pick_b, table, preferred_element_type=jnp.float32)
        psi_ref[:, start:start + chunk] = (left * right).astype(jnp.bfloat16)
    blocks = terms // TILE
    part_rows = fold_ref.shape[0] // 2
    cell = cell_ref[0]
    for block in range(blocks):
        rows = psi_ref[pl.ds(pl.multiple_of(block * TILE + cell * part_rows, part_rows), part_rows), :]
        reach = (block + 1) * TILE
        value = lax.dot_general(
            rows, psi_ref[0:reach, :], (((1,), (1,)), ((), ())), preferred_element_type=jnp.float32
        )
        half, at = fold_place(block, blocks)
        fold_ref[half * part_rows:(half + 1) * part_rows, at:at + reach] = value


def fold_place(block, blocks):
    low = min(block, blocks - 1 - block)
    return low, 0 if block == low else (low + 1) * TILE


def design(points, term_index, cell, n_cell):
    params, samples = points.shape
    terms = term_index.shape[0]
    blocks = terms // TILE
    rows = 2 * TILE // n_cell
    return pl.pallas_call(
        functools.partial(design_kernel, 512),
        out_shape=(
            jax.ShapeDtypeStruct((terms, samples), jnp.bfloat16),
            jax.ShapeDtypeStruct((rows, (blocks + 1) * TILE), jnp.float32),
        ),
        in_specs=[SMEM, VMEM, VMEM],
        out_specs=(VMEM, VMEM),
        scratch_shapes=[
            pltpu.VMEM((256, samples), jnp.float32),
        ],
        compiler_params=BIG,
        name="design",
    )(cell.reshape(1), term_index.T, points)


def cross_kernel(low_ref, psi_ref, yields_ref, kept_ref, sent_ref):
    rows = kept_ref.shape[0]
    for ref, which in ((sent_ref, low_ref[0] ^ 1), (kept_ref, low_ref[0])):
        part = psi_ref[pl.ds(pl.multiple_of(which * rows, rows), rows), :]
        ref[...] = jnp.dot(part, yields_ref[...], preferred_element_type=jnp.float32)


def cross_halves(psi, yields, low):
    half = jax.ShapeDtypeStruct((psi.shape[0] // 2, yields.shape[1]), jnp.float32)
    return pl.pallas_call(
        cross_kernel,
        out_shape=(half, half),
        in_specs=[SMEM, VMEM, VMEM],
        out_specs=(VMEM, VMEM),
        compiler_params=SMALL,
        name="cross_halves",
    )(low.reshape(1), psi, yields)


def lane_of(values, at):
    lanes = jnp.full(values.shape, at, jnp.int32)
    return jnp.take_along_axis(values, lanes, axis=1, mode="promise_in_bounds")


def row_of(values, at):
    return jnp.broadcast_to(values[at:at + 1, :], values.shape)


def stacked_outer(left, right):
    a, b = split3(left), split3(right)
    left = jnp.concatenate([a[0], a[0], a[1], a[1], a[0], a[2]], axis=0).astype(jnp.bfloat16)
    right = jnp.concatenate([b[0], b[1], b[0], b[1], b[2], b[0]], axis=0).astype(jnp.bfloat16)
    return lax.dot_general(left, right, (((0,), (0,)), ((), ())), preferred_element_type=jnp.float32)


def sweep_tile(bands):
    bands = list(bands)
    shape = bands[0].shape
    subs = lax.broadcasted_iota(jnp.int32, shape, 0)
    lanes = lax.broadcasted_iota(jnp.int32, shape, 1)
    for at in range(len(bands)):
        base = 8 * at
        own = bands[at]
        inside = (lanes >= base) & (lanes < base + 8)
        columns = [lane_of(own, base + k) for k in range(8)]
        fresh = jnp.where(inside, jnp.where(lanes == subs + base, -1.0, 0.0), own)
        for p in range(8):
            inverse = 1.0 / row_of(columns[p], p)
            factor = jnp.where(subs == p, 1.0 - inverse, columns[p] * inverse)
            for k in range(p + 1, 8):
                columns[k] = columns[k] - factor * row_of(columns[k], p)
            fresh = fresh - factor * row_of(fresh, p)
        delta = stacked_outer(own, fresh)
        following = (at + 1) % len(bands)
        for other in range(len(bands)):
            value = jnp.where(inside, 0.0, bands[other])
            if other == following:
                for k in range(8):
                    value = value - lane_of(bands[other], base + k) * row_of(fresh, k)
            else:
                value = value - delta[8 * other:8 * other + 8]
            bands[other] = value
        bands[at] = fresh
    return bands


def stacked_dot(left, right):
    a = [part.astype(jnp.bfloat16) for part in split3(left)]
    b = [part.astype(jnp.bfloat16) for part in split3(right)]
    left = jnp.concatenate([a[0], a[0], a[1], a[1], a[0], a[2]], axis=1)
    right = jnp.concatenate([b[0], b[1], b[0], b[1], b[2], b[0]], axis=0)
    return jnp.dot(left, right, preferred_element_type=jnp.float32)


def sweep_block(gram, out_ref, minus, block):
    terms = out_ref.shape[0]
    band = slice(block * TILE, (block + 1) * TILE)
    whole = slice(0, terms)
    fresh = -stacked_dot(minus, gram(band, whole))
    parts = [minus if at == block * TILE else fresh[:, at:at + TILE] for at in range(0, terms, TILE)]
    fresh = jnp.concatenate(parts, axis=1)
    change = stacked_dot(gram(whole, band), fresh)
    inside = (lax.broadcasted_iota(jnp.int32, (TILE, terms), 1) // TILE) == block
    for at in range(0, terms, TILE):
        rows = slice(at, at + TILE)
        if at == block * TILE:
            out_ref[rows, :] = fresh
        else:
            out_ref[rows, :] = jnp.where(inside, 0.0, gram(rows, whole)) - change[rows, :]


def sweep(tile):
    return jnp.concatenate(sweep_tile([tile[at:at + 8, :] for at in range(0, TILE, 8)]), axis=0)


def first_kernel(where_ref, *refs):
    out_ref, scale_ref, gram_ref, fold_ref = refs[-4:]
    terms = out_ref.shape[0]
    blocks = terms // TILE
    for step, ref in enumerate(refs[:-4]):
        piece = ref.shape[0] // 2
        eighth = ref.shape[0] // 8
        for at in range(8):
            row = pl.multiple_of((where_ref[0] ^ at) * eighth, eighth)
            fold_ref[pl.ds(row, eighth), :] = ref[at * eighth:(at + 1) * eighth, :]
        start = pl.multiple_of((where_ref[1] ^ step) * piece, piece)
        for block in range(blocks):
            half, lane = fold_place(block, blocks)
            reach = (block + 1) * TILE
            gram_ref[pl.ds(start + block * TILE, piece), 0:reach] = (
                fold_ref[half * piece:(half + 1) * piece, lane:lane + reach]
            )
    diagonal = lax.broadcasted_iota(jnp.int32, (TILE, TILE), 0) == lax.broadcasted_iota(jnp.int32, (TILE, TILE), 1)
    bands = [slice(block * TILE, (block + 1) * TILE) for block in range(blocks)]
    across, down = [], []
    for band in bands:
        only = jnp.where(diagonal, gram_ref[band, band], 0.0)
        down.append(lax.rsqrt(jnp.sum(only, axis=1, keepdims=True)))
        across.append(lax.rsqrt(jnp.sum(only, axis=0, keepdims=True)))
    tiles = {}
    for i, band in enumerate(bands):
        scale_ref[band, :] = down[i]
        for j in range(i + 1):
            tiles[i, j] = gram_ref[band, bands[j]] * down[i] * across[j]
    minus = sweep(tiles[0, 0])
    for i, band in enumerate(bands):
        for j in range(i + 1):
            gram_ref[band, bands[j]] = tiles[i, j]
            if j < i:
                gram_ref[bands[j], band] = tiles[i, j].T
    sweep_block(lambda rows, lanes: gram_ref[rows, lanes], out_ref, minus, 0)


def next_kernel(block, in_ref, out_ref):
    band = slice(block * TILE, (block + 1) * TILE)
    sweep_block(lambda rows, lanes: in_ref[rows, lanes], out_ref, sweep(in_ref[band, band]), block)


STEP_COST = pl.CostEstimate(flops=10**9, bytes_accessed=2**20, transcendentals=512)


def first_block(where, pieces, terms):
    return pl.pallas_call(
        first_kernel,
        out_shape=(
            jax.ShapeDtypeStruct((terms, terms), jnp.float32),
            jax.ShapeDtypeStruct((terms, 1), jnp.float32),
        ),
        in_specs=[SMEM] + [VMEM] * len(pieces),
        out_specs=(VMEM, VMEM),
        scratch_shapes=[pltpu.VMEM((terms, terms), jnp.float32), pltpu.VMEM(pieces[0].shape, jnp.float32)],
        compiler_params=BIG,
        cost_estimate=STEP_COST,
        name="block_0",
    )(where, *pieces)


def next_block(gram, block):
    return pl.pallas_call(
        functools.partial(next_kernel, block),
        out_shape=jax.ShapeDtypeStruct(gram.shape, jnp.float32),
        in_specs=[VMEM],
        out_specs=VMEM,
        compiler_params=BIG,
        cost_estimate=STEP_COST,
        name="block_%d" % block,
    )(gram)


def solve_kernel(samples, steps, rows, finish, where_ref, group_ref, inverse_ref, scale_ref, *refs):
    count = len(steps)
    pieces = refs[:4]
    others = refs[4:-(count + finish + 1)]
    cross_ref = refs[-1]
    shares = refs[-(count + finish + 1):-(finish + 1)]
    step = 0
    for ref in pieces:
        for at in range(0, ref.shape[0], rows):
            cross_ref[pl.ds(pl.multiple_of((where_ref[0] ^ step) * rows, rows), rows), :] = ref[at:at + rows, :]
            step += 1
    terms, cells = cross_ref.shape
    scaled = scale_ref[...] * cross_ref[...]
    size = jnp.sqrt(jnp.float32(samples))
    share = shares[0].shape[0]
    for step, ref in zip(steps, shares):
        band = pl.ds(pl.multiple_of((where_ref[1] ^ step) * share, share), share)
        value = jnp.dot(inverse_ref[band, :], scaled, precision=HIGH, preferred_element_type=jnp.float32)
        ref[...] = -scale_ref[band, :] * value * size
    if not finish:
        return
    sobol_ref = refs[-2]
    totals, labels = [], []
    for step, ref in enumerate(shares + others):
        owner = where_ref[1] ^ step
        value = ref[...] / size
        squares = value * value
        row = lax.broadcasted_iota(jnp.int32, squares.shape, 0) + owner * share
        squares = jnp.where(row >= 1, squares, 0.0)
        for at in range(0, share, BLOCK):
            totals.append(jnp.sum(squares[at:at + BLOCK], axis=0, keepdims=True))
            labels.append(group_ref[owner * (share // BLOCK) + at // BLOCK])
    total = functools.reduce(jnp.add, totals)
    for group in range(GROUPS):
        part = jnp.zeros_like(total)
        for label, value in zip(labels, totals):
            part = part + jnp.where(label == group, value, 0.0)
        sobol_ref[group:group + 1, :] = part / total


def solve(where, inverse, scale, pieces, rows, block_group, samples, n_cell, steps, others=()):
    terms = inverse.shape[0]
    cells = pieces[0].shape[1]
    finish = len(others) > 0
    out = (jax.ShapeDtypeStruct((terms // n_cell, cells), jnp.float32),) * len(steps)
    if finish:
        out += (jax.ShapeDtypeStruct((GROUPS, cells), jnp.float32),)
    return pl.pallas_call(
        functools.partial(solve_kernel, samples, steps, rows, finish),
        out_shape=out,
        in_specs=[SMEM, SMEM] + [VMEM] * (2 + len(pieces) + len(others)),
        out_specs=(VMEM,) * len(out),
        scratch_shapes=[pltpu.VMEM((terms, cells), jnp.float32)],
        compiler_params=BIG,
        cost_estimate=pl.CostEstimate(flops=(5 if finish else 1) * 10**9, bytes_accessed=2**20, transcendentals=0),
        name="solve_near" if finish else "solve_far",
    )(where, block_group, inverse, scale, *pieces, *others)


def join_kernel(where_ref, *refs):
    out_ref = refs[-1]
    for step, ref in enumerate(refs[:-1]):
        wide = ref.shape[1]
        out_ref[:, pl.ds(pl.multiple_of((where_ref[0] ^ step) * wide, wide), wide)] = ref[...]


def join_columns(where, shares):
    rows, wide = shares[0].shape
    return pl.pallas_call(
        join_kernel,
        out_shape=jax.ShapeDtypeStruct((rows, wide * len(shares)), jnp.float32),
        in_specs=[SMEM] + [VMEM] * len(shares),
        out_specs=VMEM,
        compiler_params=SMALL,
        name="join_columns",
    )(where, *shares)


def swap(values, axis, step):
    size = lax.axis_size(axis)
    return lax.ppermute(values, axis, [(at, at ^ step) for at in range(size)])


def pick(values, at):
    return lax.dynamic_index_in_dim(values, at, axis=0, keepdims=False)


def halve(values, me, bit):
    halves = values.reshape(2, values.shape[0] // 2, values.shape[1])
    mine = (me >> bit) & 1
    return pick(halves, mine) + swap(pick(halves, mine ^ 1), "samp", 1 << bit)


def join(values, step):
    return jnp.concatenate([values, swap(values, "samp", step)], axis=0)


def add_rest(values):
    step = 8
    while step < lax.axis_size("samp"):
        values = values + swap(values, "samp", step)
        step *= 2
    return values


def on_device(points, yields, term_index, block_group):
    n_samp = lax.axis_size("samp")
    n_cell = lax.axis_size("cell")
    me, cell = lax.axis_index("samp"), lax.axis_index("cell")
    blocks = term_index.shape[0] // TILE
    psi, fold = design(points, term_index, cell, n_cell)
    spot = ((me & 1) << 2) | (me & 2) | ((me >> 2) & 1)
    fold = halve(fold, me, 0)
    kept, sent = cross_halves(psi, yields, me & 1)
    fold, kept, sent = lax.optimization_barrier((fold, kept, sent))
    part = kept + swap(sent, "samp", 1)
    fold = add_rest(halve(halve(fold, me, 1), me, 2))
    fold, part = lax.optimization_barrier((fold, part))
    part = halve(part, me, 1)
    fold = join(join(fold, 4), 2)
    fold, part = lax.optimization_barrier((fold, part))
    part = add_rest(halve(part, me, 2))
    rows = part.shape[0]
    fold = join(fold, 1)
    fold, part = lax.optimization_barrier((fold, part))
    pair = join(part, 4)
    held, order = [fold], [0]
    step = n_cell // 2
    while step:
        held = held + [swap(value, "cell", step) for value in held]
        order = order + [value ^ step for value in order]
        step //= 2
    held, pair = lax.optimization_barrier((held, pair))
    where = jnp.stack([spot, cell])
    gram, scale = first_block(where, [held[order.index(at)] for at in range(n_cell)], term_index.shape[0])
    pieces = [pair, swap(pair, "samp", 2), swap(pair, "samp", 1)]
    for block in range(1, blocks):
        if block == 1:
            gram, pieces = lax.optimization_barrier((gram, pieces))
            pieces = pieces + [swap(pieces[1], "samp", 1)]
        gram = next_block(gram, block)
    given = (where, gram, scale, pieces, rows, block_group, points.shape[1] * n_samp, n_cell)
    far = list(solve(*given, tuple(range(1, n_cell))))
    came = [swap(value, "cell", 1 + at) for at, value in enumerate(far)]
    near, sobol = solve(*given, (0,), far)
    shares = [near] + came
    return (join_columns(cell.reshape(1), shares), sobol)


def solution(mesh):
    placed = (P(None, "samp"), P("samp", "cell"), P(), P())
    return jax.shard_map(
        on_device,
        mesh=mesh,
        in_specs=placed,
        out_specs=(P("cell", None), P(None, "cell")),
        check_vma=False,
    )
```

```python
import functools

import jax
import jax.numpy as jnp
from jax import lax
from jax.experimental import pallas as pl
from jax.experimental.pallas import tpu as pltpu
from jax.sharding import PartitionSpec as P

BLOCK = 64
GROUPS = 8
TILE = 128
HIGH = lax.Precision.HIGHEST
VMEM = pl.BlockSpec(memory_space=pltpu.VMEM)
SMEM = pl.BlockSpec(memory_space=pltpu.SMEM)
BIG = pltpu.CompilerParams(vmem_limit_bytes=16 * 2**20)
SMALL = pltpu.CompilerParams(vmem_limit_bytes=8 * 2**20)


def split3(values):
    top = values.astype(jnp.bfloat16).astype(jnp.float32)
    rest = values - top
    middle = rest.astype(jnp.bfloat16).astype(jnp.float32)
    return top, middle, rest - middle


def picks(column, params, width):
    span = 3 * params
    degree = column % 4
    place = (degree - 1) * params + column // 4
    at = lax.broadcasted_iota(jnp.int32, (width, column.shape[1]), 0)
    hit = (at == place) | (at == place + span) | (at == place + 2 * span)
    hit = (hit & (degree > 0)) | ((at == 3 * span) & (degree == 0))
    return hit.astype(jnp.float32).T.astype(jnp.bfloat16)


def design_kernel(chunk, cell_ref, index_ref, points_ref, psi_ref, fold_ref, table_ref):
    params, samples = points_ref.shape
    terms = index_ref.shape[1]
    width = table_ref.shape[0]
    span = 3 * params
    xs = points_ref[...]
    first = 1.7320508075688772 * xs
    second = 2.23606797749979 * (1.5 * xs * xs - 0.5)
    third = 2.6457513110645907 * (2.5 * xs * xs * xs - 1.5 * xs)
    for at, rows in enumerate((first, second, third)):
        for part, values in enumerate(split3(rows)):
            table_ref[pl.ds(part * span + at * params, params), :] = values
    table_ref[pl.ds(3 * span, width - 3 * span), :] = jnp.ones((width - 3 * span, samples), jnp.float32)
    pick_a = picks(index_ref[0:1, :], params, width)
    pick_b = picks(index_ref[1:2, :], params, width)
    for start in range(0, samples, chunk):
        table = table_ref[:, start:start + chunk].astype(jnp.bfloat16)
        left = jnp.dot(pick_a, table, preferred_element_type=jnp.float32)
        right = jnp.dot(pick_b, table, preferred_element_type=jnp.float32)
        psi_ref[:, start:start + chunk] = (left * right).astype(jnp.bfloat16)
    blocks = terms // TILE
    part_rows = fold_ref.shape[0] // 2
    cell = cell_ref[0]
    for block in range(blocks):
        rows = psi_ref[pl.ds(pl.multiple_of(block * TILE + cell * part_rows, part_rows), part_rows), :]
        reach = (block + 1) * TILE
        value = lax.dot_general(
            rows, psi_ref[0:reach, :], (((1,), (1,)), ((), ())), preferred_element_type=jnp.float32
        )
        half, at = fold_place(block, blocks)
        fold_ref[half * part_rows:(half + 1) * part_rows, at:at + reach] = value


def fold_place(block, blocks):
    low = min(block, blocks - 1 - block)
    return low, 0 if block == low else (low + 1) * TILE


def design(points, term_index, cell, n_cell):
    params, samples = points.shape
    terms = term_index.shape[0]
    blocks = terms // TILE
    rows = 2 * TILE // n_cell
    return pl.pallas_call(
        functools.partial(design_kernel, 512),
        out_shape=(
            jax.ShapeDtypeStruct((terms, samples), jnp.bfloat16),
            jax.ShapeDtypeStruct((rows, (blocks + 1) * TILE), jnp.float32),
        ),
        in_specs=[SMEM, VMEM, VMEM],
        out_specs=(VMEM, VMEM),
        scratch_shapes=[
            pltpu.VMEM((256, samples), jnp.float32),
        ],
        compiler_params=BIG,
        name="design",
    )(cell.reshape(1), term_index.T, points)


def cross_kernel(low_ref, psi_ref, yields_ref, kept_ref, sent_ref):
    rows = kept_ref.shape[0]
    for ref, which in ((sent_ref, low_ref[0] ^ 1), (kept_ref, low_ref[0])):
        part = psi_ref[pl.ds(pl.multiple_of(which * rows, rows), rows), :]
        ref[...] = jnp.dot(part, yields_ref[...], preferred_element_type=jnp.float32)


def cross_halves(psi, yields, low):
    half = jax.ShapeDtypeStruct((psi.shape[0] // 2, yields.shape[1]), jnp.float32)
    return pl.pallas_call(
        cross_kernel,
        out_shape=(half, half),
        in_specs=[SMEM, VMEM, VMEM],
        out_specs=(VMEM, VMEM),
        compiler_params=SMALL,
        name="cross_halves",
    )(low.reshape(1), psi, yields)


def lane_of(values, at):
    lanes = jnp.full(values.shape, at, jnp.int32)
    return jnp.take_along_axis(values, lanes, axis=1, mode="promise_in_bounds")


def row_of(values, at):
    return jnp.broadcast_to(values[at:at + 1, :], values.shape)


def stacked_outer(left, right):
    a, b = split3(left), split3(right)
    left = jnp.concatenate([a[0], a[0], a[1], a[1], a[0], a[2]], axis=0).astype(jnp.bfloat16)
    right = jnp.concatenate([b[0], b[1], b[0], b[1], b[2], b[0]], axis=0).astype(jnp.bfloat16)
    return lax.dot_general(left, right, (((0,), (0,)), ((), ())), preferred_element_type=jnp.float32)


def sweep_tile(bands):
    bands = list(bands)
    shape = bands[0].shape
    subs = lax.broadcasted_iota(jnp.int32, shape, 0)
    lanes = lax.broadcasted_iota(jnp.int32, shape, 1)
    for at in range(len(bands)):
        base = 8 * at
        own = bands[at]
        inside = (lanes >= base) & (lanes < base + 8)
        columns = [lane_of(own, base + k) for k in range(8)]
        fresh = jnp.where(inside, jnp.where(lanes == subs + base, -1.0, 0.0), own)
        for p in range(0, 8, 2):
            q = p + 1
            a, b, d = row_of(columns[p], p), row_of(columns[p], q), row_of(columns[q], q)
            det = a * d - b * b
            first = d * columns[p] - b * columns[q]
            second = a * columns[q] - b * columns[p]
            first = jnp.where(subs == p, det - d, jnp.where(subs == q, b, first))
            second = jnp.where(subs == p, b, jnp.where(subs == q, det - a, second))
            inverse = 1.0 / det
            for k in range(q + 1, 8):
                less = first * row_of(columns[k], p) + second * row_of(columns[k], q)
                columns[k] = columns[k] - less * inverse
            less = first * row_of(fresh, p) + second * row_of(fresh, q)
            fresh = fresh - less * inverse
        delta = stacked_outer(own, fresh)
        following = (at + 1) % len(bands)
        for other in range(len(bands)):
            value = jnp.where(inside, 0.0, bands[other])
            if other == following:
                for k in range(8):
                    value = value - lane_of(bands[other], base + k) * row_of(fresh, k)
            else:
                value = value - delta[8 * other:8 * other + 8]
            bands[other] = value
        bands[at] = fresh
    return bands


def stacked_dot(left, right):
    a = [part.astype(jnp.bfloat16) for part in split3(left)]
    b = [part.astype(jnp.bfloat16) for part in split3(right)]
    left = jnp.concatenate([a[0], a[0], a[1], a[1], a[0], a[2]], axis=1)
    right = jnp.concatenate([b[0], b[1], b[0], b[1], b[2], b[0]], axis=0)
    return jnp.dot(left, right, preferred_element_type=jnp.float32)


def sweep_block(gram, out_ref, minus, block):
    terms = out_ref.shape[0]
    band = slice(block * TILE, (block + 1) * TILE)
    whole = slice(0, terms)
    fresh = -stacked_dot(minus, gram(band, whole))
    parts = [minus if at == block * TILE else fresh[:, at:at + TILE] for at in range(0, terms, TILE)]
    fresh = jnp.concatenate(parts, axis=1)
    change = stacked_dot(gram(whole, band), fresh)
    inside = (lax.broadcasted_iota(jnp.int32, (TILE, terms), 1) // TILE) == block
    for at in range(0, terms, TILE):
        rows = slice(at, at + TILE)
        if at == block * TILE:
            out_ref[rows, :] = fresh
        else:
            out_ref[rows, :] = jnp.where(inside, 0.0, gram(rows, whole)) - change[rows, :]


def sweep(tile):
    return jnp.concatenate(sweep_tile([tile[at:at + 8, :] for at in range(0, TILE, 8)]), axis=0)


def first_kernel(where_ref, *refs):
    out_ref, scale_ref, gram_ref, fold_ref = refs[-4:]
    terms = out_ref.shape[0]
    blocks = terms // TILE
    for step, ref in enumerate(refs[:-4]):
        piece = ref.shape[0] // 2
        eighth = ref.shape[0] // 8
        for at in range(8):
            row = pl.multiple_of((where_ref[0] ^ at) * eighth, eighth)
            fold_ref[pl.ds(row, eighth), :] = ref[at * eighth:(at + 1) * eighth, :]
        start = pl.multiple_of((where_ref[1] ^ step) * piece, piece)
        for block in range(blocks):
            half, lane = fold_place(block, blocks)
            reach = (block + 1) * TILE
            gram_ref[pl.ds(start + block * TILE, piece), 0:reach] = (
                fold_ref[half * piece:(half + 1) * piece, lane:lane + reach]
            )
    diagonal = lax.broadcasted_iota(jnp.int32, (TILE, TILE), 0) == lax.broadcasted_iota(jnp.int32, (TILE, TILE), 1)
    bands = [slice(block * TILE, (block + 1) * TILE) for block in range(blocks)]
    across, down = [], []
    for band in bands:
        only = jnp.where(diagonal, gram_ref[band, band], 0.0)
        down.append(lax.rsqrt(jnp.sum(only, axis=1, keepdims=True)))
        across.append(lax.rsqrt(jnp.sum(only, axis=0, keepdims=True)))
    tiles = {}
    for i, band in enumerate(bands):
        scale_ref[band, :] = down[i]
        for j in range(i + 1):
            tiles[i, j] = gram_ref[band, bands[j]] * down[i] * across[j]
    minus = sweep(tiles[0, 0])
    for i, band in enumerate(bands):
        for j in range(i + 1):
            gram_ref[band, bands[j]] = tiles[i, j]
            if j < i:
                gram_ref[bands[j], band] = tiles[i, j].T
    sweep_block(lambda rows, lanes: gram_ref[rows, lanes], out_ref, minus, 0)


def next_kernel(block, in_ref, out_ref):
    band = slice(block * TILE, (block + 1) * TILE)
    sweep_block(lambda rows, lanes: in_ref[rows, lanes], out_ref, sweep(in_ref[band, band]), block)


STEP_COST = pl.CostEstimate(flops=10**9, bytes_accessed=2**20, transcendentals=512)


def first_block(where, pieces, terms):
    return pl.pallas_call(
        first_kernel,
        out_shape=(
            jax.ShapeDtypeStruct((terms, terms), jnp.float32),
            jax.ShapeDtypeStruct((terms, 1), jnp.float32),
        ),
        in_specs=[SMEM] + [VMEM] * len(pieces),
        out_specs=(VMEM, VMEM),
        scratch_shapes=[pltpu.VMEM((terms, terms), jnp.float32), pltpu.VMEM(pieces[0].shape, jnp.float32)],
        compiler_params=BIG,
        cost_estimate=STEP_COST,
        name="block_0",
    )(where, *pieces)


def next_block(gram, block):
    return pl.pallas_call(
        functools.partial(next_kernel, block),
        out_shape=jax.ShapeDtypeStruct(gram.shape, jnp.float32),
        in_specs=[VMEM],
        out_specs=VMEM,
        compiler_params=BIG,
        cost_estimate=STEP_COST,
        name="block_%d" % block,
    )(gram)


def solve_kernel(samples, steps, rows, finish, where_ref, group_ref, inverse_ref, scale_ref, *refs):
    count = len(steps)
    pieces = refs[:4]
    others = refs[4:-(count + finish + 1)]
    cross_ref = refs[-1]
    shares = refs[-(count + finish + 1):-(finish + 1)]
    step = 0
    for ref in pieces:
        for at in range(0, ref.shape[0], rows):
            cross_ref[pl.ds(pl.multiple_of((where_ref[0] ^ step) * rows, rows), rows), :] = ref[at:at + rows, :]
            step += 1
    terms, cells = cross_ref.shape
    scaled = scale_ref[...] * cross_ref[...]
    size = jnp.sqrt(jnp.float32(samples))
    share = shares[0].shape[0]
    for step, ref in zip(steps, shares):
        band = pl.ds(pl.multiple_of((where_ref[1] ^ step) * share, share), share)
        value = jnp.dot(inverse_ref[band, :], scaled, precision=HIGH, preferred_element_type=jnp.float32)
        ref[...] = -scale_ref[band, :] * value * size
    if not finish:
        return
    sobol_ref = refs[-2]
    totals, labels = [], []
    for step, ref in enumerate(shares + others):
        owner = where_ref[1] ^ step
        value = ref[...] / size
        squares = value * value
        row = lax.broadcasted_iota(jnp.int32, squares.shape, 0) + owner * share
        squares = jnp.where(row >= 1, squares, 0.0)
        for at in range(0, share, BLOCK):
            totals.append(jnp.sum(squares[at:at + BLOCK], axis=0, keepdims=True))
            labels.append(group_ref[owner * (share // BLOCK) + at // BLOCK])
    total = functools.reduce(jnp.add, totals)
    for group in range(GROUPS):
        part = jnp.zeros_like(total)
        for label, value in zip(labels, totals):
            part = part + jnp.where(label == group, value, 0.0)
        sobol_ref[group:group + 1, :] = part / total


def solve(where, inverse, scale, pieces, rows, block_group, samples, n_cell, steps, others=()):
    terms = inverse.shape[0]
    cells = pieces[0].shape[1]
    finish = len(others) > 0
    out = (jax.ShapeDtypeStruct((terms // n_cell, cells), jnp.float32),) * len(steps)
    if finish:
        out += (jax.ShapeDtypeStruct((GROUPS, cells), jnp.float32),)
    return pl.pallas_call(
        functools.partial(solve_kernel, samples, steps, rows, finish),
        out_shape=out,
        in_specs=[SMEM, SMEM] + [VMEM] * (2 + len(pieces) + len(others)),
        out_specs=(VMEM,) * len(out),
        scratch_shapes=[pltpu.VMEM((terms, cells), jnp.float32)],
        compiler_params=BIG,
        cost_estimate=pl.CostEstimate(flops=(5 if finish else 1) * 10**9, bytes_accessed=2**20, transcendentals=0),
        name="solve_near" if finish else "solve_far_%d" % steps[0],
    )(where, block_group, inverse, scale, *pieces, *others)


def join_kernel(where_ref, *refs):
    out_ref = refs[-1]
    for step, ref in enumerate(refs[:-1]):
        wide = ref.shape[1]
        out_ref[:, pl.ds(pl.multiple_of((where_ref[0] ^ step) * wide, wide), wide)] = ref[...]


def join_columns(where, shares):
    rows, wide = shares[0].shape
    return pl.pallas_call(
        join_kernel,
        out_shape=jax.ShapeDtypeStruct((rows, wide * len(shares)), jnp.float32),
        in_specs=[SMEM] + [VMEM] * len(shares),
        out_specs=VMEM,
        compiler_params=SMALL,
        name="join_columns",
    )(where, *shares)


def swap(values, axis, step):
    size = lax.axis_size(axis)
    return lax.ppermute(values, axis, [(at, at ^ step) for at in range(size)])


def pick(values, at):
    return lax.dynamic_index_in_dim(values, at, axis=0, keepdims=False)


def halve(values, me, bit):
    halves = values.reshape(2, values.shape[0] // 2, values.shape[1])
    mine = (me >> bit) & 1
    return pick(halves, mine) + swap(pick(halves, mine ^ 1), "samp", 1 << bit)


def join(values, step):
    return jnp.concatenate([values, swap(values, "samp", step)], axis=0)


def add_rest(values):
    step = 8
    while step < lax.axis_size("samp"):
        values = values + swap(values, "samp", step)
        step *= 2
    return values


def on_device(points, yields, term_index, block_group):
    n_samp = lax.axis_size("samp")
    n_cell = lax.axis_size("cell")
    me, cell = lax.axis_index("samp"), lax.axis_index("cell")
    blocks = term_index.shape[0] // TILE
    psi, fold = design(points, term_index, cell, n_cell)
    spot = ((me & 1) << 2) | (me & 2) | ((me >> 2) & 1)
    fold = halve(fold, me, 0)
    kept, sent = cross_halves(psi, yields, me & 1)
    fold, kept, sent = lax.optimization_barrier((fold, kept, sent))
    part = kept + swap(sent, "samp", 1)
    fold = add_rest(halve(halve(fold, me, 1), me, 2))
    fold, part = lax.optimization_barrier((fold, part))
    part = halve(part, me, 1)
    fold = join(fold, 4)
    fold, part = lax.optimization_barrier((fold, part))
    part = add_rest(halve(part, me, 2))
    rows = part.shape[0]
    fold = join(join(fold, 2), 1)
    fold, part = lax.optimization_barrier((fold, part))
    pair = join(part, 4)
    held, order = [fold], [0]
    step = n_cell // 2
    while step:
        held = held + [swap(value, "cell", step) for value in held]
        order = order + [value ^ step for value in order]
        step //= 2
    held, pair = lax.optimization_barrier((held, pair))
    where = jnp.stack([spot, cell])
    gram, scale = first_block(where, [held[order.index(at)] for at in range(n_cell)], term_index.shape[0])
    pieces = [pair, swap(pair, "samp", 2), swap(pair, "samp", 1)]
    for block in range(1, blocks):
        if block == 1:
            gram, pieces = lax.optimization_barrier((gram, pieces))
            pieces = pieces + [swap(pieces[1], "samp", 1)]
        gram = next_block(gram, block)
    given = (where, gram, scale, pieces, rows, block_group, points.shape[1] * n_samp, n_cell)
    far = [None] * n_cell
    for step in range(n_cell - 1, 0, -1):
        far[step], = solve(*given, (step,))
    came = [swap(far[step], "cell", step) for step in range(1, n_cell)]
    near, sobol = solve(*given, (0,), far[1:])
    shares = [near] + came
    return (join_columns(cell.reshape(1), shares), sobol)


def solution(mesh):
    placed = (P(None, "samp"), P("samp", "cell"), P(), P())
    return jax.shard_map(
        on_device,
        mesh=mesh,
        in_specs=placed,
        out_specs=(P("cell", None), P(None, "cell")),
        check_vma=False,
    )
```

```python
import functools

import jax
import jax.numpy as jnp
from jax import lax
from jax.experimental import pallas as pl
from jax.experimental.pallas import tpu as pltpu
from jax.sharding import PartitionSpec as P

BLOCK = 64
GROUPS = 8
TILE = 128
HIGH = lax.Precision.HIGHEST
VMEM = pl.BlockSpec(memory_space=pltpu.VMEM)
SMEM = pl.BlockSpec(memory_space=pltpu.SMEM)
BIG = pltpu.CompilerParams(vmem_limit_bytes=16 * 2**20)
SMALL = pltpu.CompilerParams(vmem_limit_bytes=8 * 2**20)


def split3(values):
    top = values.astype(jnp.bfloat16).astype(jnp.float32)
    rest = values - top
    middle = rest.astype(jnp.bfloat16).astype(jnp.float32)
    return top, middle, rest - middle


def picks(column, params, width):
    span = 3 * params
    degree = column % 4
    place = (degree - 1) * params + column // 4
    at = lax.broadcasted_iota(jnp.int32, (width, column.shape[1]), 0)
    hit = (at == place) | (at == place + span) | (at == place + 2 * span)
    hit = (hit & (degree > 0)) | ((at == 3 * span) & (degree == 0))
    return hit.astype(jnp.float32).T.astype(jnp.bfloat16)


def design_kernel(chunk, cell_ref, index_ref, points_ref, psi_ref, fold_ref, table_ref):
    params, samples = points_ref.shape
    terms = index_ref.shape[1]
    width = table_ref.shape[0]
    span = 3 * params
    xs = points_ref[...]
    first = 1.7320508075688772 * xs
    second = 2.23606797749979 * (1.5 * xs * xs - 0.5)
    third = 2.6457513110645907 * (2.5 * xs * xs * xs - 1.5 * xs)
    for at, rows in enumerate((first, second, third)):
        for part, values in enumerate(split3(rows)):
            table_ref[pl.ds(part * span + at * params, params), :] = values
    table_ref[pl.ds(3 * span, width - 3 * span), :] = jnp.ones((width - 3 * span, samples), jnp.float32)
    pick_a = picks(index_ref[0:1, :], params, width)
    pick_b = picks(index_ref[1:2, :], params, width)
    for start in range(0, samples, chunk):
        table = table_ref[:, start:start + chunk].astype(jnp.bfloat16)
        left = jnp.dot(pick_a, table, preferred_element_type=jnp.float32)
        right = jnp.dot(pick_b, table, preferred_element_type=jnp.float32)
        psi_ref[:, start:start + chunk] = (left * right).astype(jnp.bfloat16)
    blocks = terms // TILE
    part_rows = fold_ref.shape[0] // 2
    cell = cell_ref[0]
    for block in range(blocks):
        rows = psi_ref[pl.ds(pl.multiple_of(block * TILE + cell * part_rows, part_rows), part_rows), :]
        reach = (block + 1) * TILE
        value = lax.dot_general(
            rows, psi_ref[0:reach, :], (((1,), (1,)), ((), ())), preferred_element_type=jnp.float32
        )
        half, at = fold_place(block, blocks)
        fold_ref[half * part_rows:(half + 1) * part_rows, at:at + reach] = value


def fold_place(block, blocks):
    low = min(block, blocks - 1 - block)
    return low, 0 if block == low else (low + 1) * TILE


def design(points, term_index, cell, n_cell):
    params, samples = points.shape
    terms = term_index.shape[0]
    blocks = terms // TILE
    rows = 2 * TILE // n_cell
    return pl.pallas_call(
        functools.partial(design_kernel, 512),
        out_shape=(
            jax.ShapeDtypeStruct((terms, samples), jnp.bfloat16),
            jax.ShapeDtypeStruct((rows, (blocks + 1) * TILE), jnp.float32),
        ),
        in_specs=[SMEM, VMEM, VMEM],
        out_specs=(VMEM, VMEM),
        scratch_shapes=[
            pltpu.VMEM((256, samples), jnp.float32),
        ],
        compiler_params=BIG,
        name="design",
    )(cell.reshape(1), term_index.T, points)


def cross_kernel(low_ref, psi_ref, yields_ref, kept_ref, sent_ref):
    rows = kept_ref.shape[0]
    for ref, which in ((sent_ref, low_ref[0] ^ 1), (kept_ref, low_ref[0])):
        part = psi_ref[pl.ds(pl.multiple_of(which * rows, rows), rows), :]
        ref[...] = jnp.dot(part, yields_ref[...], preferred_element_type=jnp.float32)


def cross_halves(psi, yields, low):
    half = jax.ShapeDtypeStruct((psi.shape[0] // 2, yields.shape[1]), jnp.float32)
    return pl.pallas_call(
        cross_kernel,
        out_shape=(half, half),
        in_specs=[SMEM, VMEM, VMEM],
        out_specs=(VMEM, VMEM),
        compiler_params=SMALL,
        name="cross_halves",
    )(low.reshape(1), psi, yields)


def lane_of(values, at):
    lanes = jnp.full(values.shape, at, jnp.int32)
    return jnp.take_along_axis(values, lanes, axis=1, mode="promise_in_bounds")


def row_of(values, at):
    return jnp.broadcast_to(values[at:at + 1, :], values.shape)


def stacked_outer(left, right):
    a, b = split3(left), split3(right)
    left = jnp.concatenate([a[0], a[0], a[1], a[1], a[0], a[2]], axis=0).astype(jnp.bfloat16)
    right = jnp.concatenate([b[0], b[1], b[0], b[1], b[2], b[0]], axis=0).astype(jnp.bfloat16)
    return lax.dot_general(left, right, (((0,), (0,)), ((), ())), preferred_element_type=jnp.float32)


def sweep_tile(bands):
    bands = list(bands)
    shape = bands[0].shape
    subs = lax.broadcasted_iota(jnp.int32, shape, 0)
    lanes = lax.broadcasted_iota(jnp.int32, shape, 1)
    for at in range(len(bands)):
        base = 8 * at
        own = bands[at]
        inside = (lanes >= base) & (lanes < base + 8)
        columns = [lane_of(own, base + k) for k in range(8)]
        fresh = jnp.where(inside, jnp.where(lanes == subs + base, -1.0, 0.0), own)
        for p in range(0, 8, 2):
            q = p + 1
            a, b, d = row_of(columns[p], p), row_of(columns[p], q), row_of(columns[q], q)
            det = a * d - b * b
            first = d * columns[p] - b * columns[q]
            second = a * columns[q] - b * columns[p]
            first = jnp.where(subs == p, det - d, jnp.where(subs == q, b, first))
            second = jnp.where(subs == p, b, jnp.where(subs == q, det - a, second))
            inverse = 1.0 / det
            for k in range(q + 1, 8):
                less = first * row_of(columns[k], p) + second * row_of(columns[k], q)
                columns[k] = columns[k] - less * inverse
            less = first * row_of(fresh, p) + second * row_of(fresh, q)
            fresh = fresh - less * inverse
        delta = stacked_outer(own, fresh)
        following = (at + 1) % len(bands)
        for other in range(len(bands)):
            value = jnp.where(inside, 0.0, bands[other])
            if other == following:
                for k in range(8):
                    value = value - lane_of(bands[other], base + k) * row_of(fresh, k)
            else:
                value = value - delta[8 * other:8 * other + 8]
            bands[other] = value
        bands[at] = fresh
    return bands


def stacked_dot(left, right):
    a = [part.astype(jnp.bfloat16) for part in split3(left)]
    b = [part.astype(jnp.bfloat16) for part in split3(right)]
    left = jnp.concatenate([a[0], a[0], a[1], a[1], a[0], a[2]], axis=1)
    right = jnp.concatenate([b[0], b[1], b[0], b[1], b[2], b[0]], axis=0)
    return jnp.dot(left, right, preferred_element_type=jnp.float32)


def sweep_block(gram, out_ref, minus, block):
    terms = out_ref.shape[0]
    band = slice(block * TILE, (block + 1) * TILE)
    whole = slice(0, terms)
    fresh = -stacked_dot(minus, gram(band, whole))
    parts = [minus if at == block * TILE else fresh[:, at:at + TILE] for at in range(0, terms, TILE)]
    fresh = jnp.concatenate(parts, axis=1)
    change = stacked_dot(gram(whole, band), fresh)
    inside = (lax.broadcasted_iota(jnp.int32, (TILE, terms), 1) // TILE) == block
    for at in range(0, terms, TILE):
        rows = slice(at, at + TILE)
        if at == block * TILE:
            out_ref[rows, :] = fresh
        else:
            out_ref[rows, :] = jnp.where(inside, 0.0, gram(rows, whole)) - change[rows, :]


def sweep(tile):
    return jnp.concatenate(sweep_tile([tile[at:at + 8, :] for at in range(0, TILE, 8)]), axis=0)


def first_kernel(where_ref, *refs):
    out_ref, scale_ref, gram_ref, fold_ref = refs[-4:]
    terms = out_ref.shape[0]
    blocks = terms // TILE
    for step, ref in enumerate(refs[:-4]):
        piece = ref.shape[0] // 2
        eighth = ref.shape[0] // 8
        for at in range(8):
            row = ((at & 1) * 4 + (at & 2) + (at >> 2)) * eighth
            fold_ref[row:row + eighth, :] = ref[at * eighth:(at + 1) * eighth, :]
        start = pl.multiple_of((where_ref[0] ^ step) * piece, piece)
        for block in range(blocks):
            half, lane = fold_place(block, blocks)
            reach = (block + 1) * TILE
            gram_ref[pl.ds(start + block * TILE, piece), 0:reach] = (
                fold_ref[half * piece:(half + 1) * piece, lane:lane + reach]
            )
    diagonal = lax.broadcasted_iota(jnp.int32, (TILE, TILE), 0) == lax.broadcasted_iota(jnp.int32, (TILE, TILE), 1)
    bands = [slice(block * TILE, (block + 1) * TILE) for block in range(blocks)]
    across, down = [], []
    for band in bands:
        only = jnp.where(diagonal, gram_ref[band, band], 0.0)
        down.append(lax.rsqrt(jnp.sum(only, axis=1, keepdims=True)))
        across.append(lax.rsqrt(jnp.sum(only, axis=0, keepdims=True)))
    tiles = {}
    for i, band in enumerate(bands):
        scale_ref[band, :] = down[i]
        for j in range(i + 1):
            tiles[i, j] = gram_ref[band, bands[j]] * down[i] * across[j]
    minus = sweep(tiles[0, 0])
    for i, band in enumerate(bands):
        for j in range(i + 1):
            gram_ref[band, bands[j]] = tiles[i, j]
            if j < i:
                gram_ref[bands[j], band] = tiles[i, j].T
    sweep_block(lambda rows, lanes: gram_ref[rows, lanes], out_ref, minus, 0)


def next_kernel(block, in_ref, out_ref):
    band = slice(block * TILE, (block + 1) * TILE)
    sweep_block(lambda rows, lanes: in_ref[rows, lanes], out_ref, sweep(in_ref[band, band]), block)


STEP_COST = pl.CostEstimate(flops=10**9, bytes_accessed=2**20, transcendentals=512)


def first_block(where, pieces, terms):
    return pl.pallas_call(
        first_kernel,
        out_shape=(
            jax.ShapeDtypeStruct((terms, terms), jnp.float32),
            jax.ShapeDtypeStruct((terms, 1), jnp.float32),
        ),
        in_specs=[SMEM] + [VMEM] * len(pieces),
        out_specs=(VMEM, VMEM),
        scratch_shapes=[pltpu.VMEM((terms, terms), jnp.float32), pltpu.VMEM(pieces[0].shape, jnp.float32)],
        compiler_params=BIG,
        cost_estimate=STEP_COST,
        name="block_0",
    )(where, *pieces)


def next_block(gram, block):
    return pl.pallas_call(
        functools.partial(next_kernel, block),
        out_shape=jax.ShapeDtypeStruct(gram.shape, jnp.float32),
        in_specs=[VMEM],
        out_specs=VMEM,
        compiler_params=BIG,
        cost_estimate=STEP_COST,
        name="block_%d" % block,
    )(gram)


def solve_kernel(samples, steps, rows, finish, where_ref, group_ref, inverse_ref, scale_ref, *refs):
    count = len(steps)
    pieces = refs[:2]
    others = refs[2:-(count + finish + 1)]
    cross_ref = refs[-1]
    shares = refs[-(count + finish + 1):-(finish + 1)]
    step = 0
    for ref in pieces:
        for at in range(0, ref.shape[0], rows):
            cross_ref[pl.ds(pl.multiple_of((where_ref[0] ^ step) * rows, rows), rows), :] = ref[at:at + rows, :]
            step += 1
    terms, cells = cross_ref.shape
    scaled = scale_ref[...] * cross_ref[...]
    size = jnp.sqrt(jnp.float32(samples))
    share = shares[0].shape[0]
    for step, ref in zip(steps, shares):
        band = pl.ds(pl.multiple_of((where_ref[1] ^ step) * share, share), share)
        value = jnp.dot(inverse_ref[band, :], scaled, precision=HIGH, preferred_element_type=jnp.float32)
        ref[...] = -scale_ref[band, :] * value * size
    if not finish:
        return
    sobol_ref = refs[-2]
    totals, labels = [], []
    for step, ref in enumerate(shares + others):
        owner = where_ref[1] ^ step
        value = ref[...] / size
        squares = value * value
        row = lax.broadcasted_iota(jnp.int32, squares.shape, 0) + owner * share
        squares = jnp.where(row >= 1, squares, 0.0)
        for at in range(0, share, BLOCK):
            totals.append(jnp.sum(squares[at:at + BLOCK], axis=0, keepdims=True))
            labels.append(group_ref[owner * (share // BLOCK) + at // BLOCK])
    total = functools.reduce(jnp.add, totals)
    for group in range(GROUPS):
        part = jnp.zeros_like(total)
        for label, value in zip(labels, totals):
            part = part + jnp.where(label == group, value, 0.0)
        sobol_ref[group:group + 1, :] = part / total


def solve(where, inverse, scale, pieces, rows, block_group, samples, n_cell, steps, others=()):
    terms = inverse.shape[0]
    cells = pieces[0].shape[1]
    finish = len(others) > 0
    out = (jax.ShapeDtypeStruct((terms // n_cell, cells), jnp.float32),) * len(steps)
    if finish:
        out += (jax.ShapeDtypeStruct((GROUPS, cells), jnp.float32),)
    return pl.pallas_call(
        functools.partial(solve_kernel, samples, steps, rows, finish),
        out_shape=out,
        in_specs=[SMEM, SMEM] + [VMEM] * (2 + len(pieces) + len(others)),
        out_specs=(VMEM,) * len(out),
        scratch_shapes=[pltpu.VMEM((terms, cells), jnp.float32)],
        compiler_params=BIG,
        cost_estimate=pl.CostEstimate(flops=(5 if finish else 1) * 10**9, bytes_accessed=2**20, transcendentals=0),
        name="solve_near" if finish else "solve_far",
    )(where, block_group, inverse, scale, *pieces, *others)


def join_kernel(where_ref, *refs):
    out_ref = refs[-1]
    for step, ref in enumerate(refs[:-1]):
        wide = ref.shape[1]
        out_ref[:, pl.ds(pl.multiple_of((where_ref[0] ^ step) * wide, wide), wide)] = ref[...]


def join_columns(where, shares):
    rows, wide = shares[0].shape
    return pl.pallas_call(
        join_kernel,
        out_shape=jax.ShapeDtypeStruct((rows, wide * len(shares)), jnp.float32),
        in_specs=[SMEM] + [VMEM] * len(shares),
        out_specs=VMEM,
        compiler_params=SMALL,
        name="join_columns",
    )(where, *shares)


def swap(values, axis, step):
    size = lax.axis_size(axis)
    return lax.ppermute(values, axis, [(at, at ^ step) for at in range(size)])


def pick(values, at):
    return lax.dynamic_index_in_dim(values, at, axis=0, keepdims=False)


def halve(values, me, bit):
    halves = values.reshape(2, values.shape[0] // 2, values.shape[1])
    mine = (me >> bit) & 1
    return pick(halves, mine) + swap(pick(halves, mine ^ 1), "samp", 1 << bit)


def join(values, step):
    return jnp.concatenate([values, swap(values, "samp", step)], axis=0)


def add_rest(values):
    step = 8
    while step < lax.axis_size("samp"):
        values = values + swap(values, "samp", step)
        step *= 2
    return values


def on_device(points, yields, term_index, block_group):
    n_samp = lax.axis_size("samp")
    n_cell = lax.axis_size("cell")
    me, cell = lax.axis_index("samp"), lax.axis_index("cell")
    blocks = term_index.shape[0] // TILE
    psi, fold = design(points, term_index, cell, n_cell)
    spot = ((me & 1) << 2) | (me & 2) | ((me >> 2) & 1)
    fold = halve(fold, me, 0)
    kept, sent = cross_halves(psi, yields, me & 1)
    fold, kept, sent = lax.optimization_barrier((fold, kept, sent))
    part = kept + swap(sent, "samp", 1)
    fold = add_rest(halve(halve(fold, me, 1), me, 2))
    fold, part = lax.optimization_barrier((fold, part))
    part = halve(part, me, 1)
    copies = jnp.broadcast_to(fold[None], (n_samp,) + fold.shape)
    fold = lax.all_to_all(copies, "samp", split_axis=0, concat_axis=0)[:8].reshape(-1, fold.shape[1])
    fold, part = lax.optimization_barrier((fold, part))
    part = add_rest(halve(part, me, 2))
    rows = part.shape[0]
    held, order = [fold], [0]
    step = n_cell // 2
    while step:
        held = held + [swap(value, "cell", step) for value in held]
        order = order + [value ^ step for value in order]
        step //= 2
    held, part = lax.optimization_barrier((held, part))
    gram, scale = first_block(cell.reshape(1), [held[order.index(at)] for at in range(n_cell)], term_index.shape[0])
    for block in range(1, blocks):
        if block <= 2:
            part = join(part, 8 >> block)
            gram, part = lax.optimization_barrier((gram, part))
        gram = next_block(gram, block)
    pieces = [part, swap(part, "samp", 1)]
    where = jnp.stack([spot, cell])
    given = (where, gram, scale, pieces, rows, block_group, points.shape[1] * n_samp, n_cell)
    far = solve(*given, tuple(range(1, n_cell)))
    came = [swap(value, "cell", 1 + at) for at, value in enumerate(far)]
    near, sobol = solve(*given, (0,), far)
    shares = [near] + came
    return (join_columns(cell.reshape(1), shares), sobol)


def solution(mesh):
    placed = (P(None, "samp"), P("samp", "cell"), P(), P())
    return jax.shard_map(
        on_device,
        mesh=mesh,
        in_specs=placed,
        out_specs=(P("cell", None), P(None, "cell")),
        check_vma=False,
    )
```

```python
import functools

import jax
import jax.numpy as jnp
from jax import lax
from jax.experimental import pallas as pl
from jax.experimental.pallas import tpu as pltpu
from jax.sharding import PartitionSpec as P

BLOCK = 64
GROUPS = 8
TILE = 128
HIGH = lax.Precision.HIGHEST
VMEM = pl.BlockSpec(memory_space=pltpu.VMEM)
SMEM = pl.BlockSpec(memory_space=pltpu.SMEM)
BIG = pltpu.CompilerParams(vmem_limit_bytes=16 * 2**20)
SMALL = pltpu.CompilerParams(vmem_limit_bytes=8 * 2**20)


def split3(values):
    top = values.astype(jnp.bfloat16).astype(jnp.float32)
    rest = values - top
    middle = rest.astype(jnp.bfloat16).astype(jnp.float32)
    return top, middle, rest - middle


def picks(column, params, width):
    span = 3 * params
    degree = column % 4
    place = (degree - 1) * params + column // 4
    at = lax.broadcasted_iota(jnp.int32, (width, column.shape[1]), 0)
    hit = (at == place) | (at == place + span) | (at == place + 2 * span)
    hit = (hit & (degree > 0)) | ((at == 3 * span) & (degree == 0))
    return hit.astype(jnp.float32).T.astype(jnp.bfloat16)


def design_kernel(chunk, cell_ref, index_ref, points_ref, psi_ref, fold_ref, table_ref):
    params, samples = points_ref.shape
    terms = index_ref.shape[1]
    width = table_ref.shape[0]
    span = 3 * params
    xs = points_ref[...]
    first = 1.7320508075688772 * xs
    second = 2.23606797749979 * (1.5 * xs * xs - 0.5)
    third = 2.6457513110645907 * (2.5 * xs * xs * xs - 1.5 * xs)
    for at, rows in enumerate((first, second, third)):
        for part, values in enumerate(split3(rows)):
            table_ref[pl.ds(part * span + at * params, params), :] = values
    table_ref[pl.ds(3 * span, width - 3 * span), :] = jnp.ones((width - 3 * span, samples), jnp.float32)
    pick_a = picks(index_ref[0:1, :], params, width)
    pick_b = picks(index_ref[1:2, :], params, width)
    for start in range(0, samples, chunk):
        table = table_ref[:, start:start + chunk].astype(jnp.bfloat16)
        left = jnp.dot(pick_a, table, preferred_element_type=jnp.float32)
        right = jnp.dot(pick_b, table, preferred_element_type=jnp.float32)
        psi_ref[:, start:start + chunk] = (left * right).astype(jnp.bfloat16)
    blocks = terms // TILE
    part_rows = fold_ref.shape[0] // 2
    cell = cell_ref[0]
    for block in range(blocks):
        rows = psi_ref[pl.ds(pl.multiple_of(block * TILE + cell * part_rows, part_rows), part_rows), :]
        reach = (block + 1) * TILE
        value = lax.dot_general(
            rows, psi_ref[0:reach, :], (((1,), (1,)), ((), ())), preferred_element_type=jnp.float32
        )
        half, at = fold_place(block, blocks)
        fold_ref[half * part_rows:(half + 1) * part_rows, at:at + reach] = value


def fold_place(block, blocks):
    low = min(block, blocks - 1 - block)
    return low, 0 if block == low else (low + 1) * TILE


def design(points, term_index, cell, n_cell):
    params, samples = points.shape
    terms = term_index.shape[0]
    blocks = terms // TILE
    rows = 2 * TILE // n_cell
    return pl.pallas_call(
        functools.partial(design_kernel, 512),
        out_shape=(
            jax.ShapeDtypeStruct((terms, samples), jnp.bfloat16),
            jax.ShapeDtypeStruct((rows, (blocks + 1) * TILE), jnp.float32),
        ),
        in_specs=[SMEM, VMEM, VMEM],
        out_specs=(VMEM, VMEM),
        scratch_shapes=[
            pltpu.VMEM((256, samples), jnp.float32),
        ],
        compiler_params=BIG,
        name="design",
    )(cell.reshape(1), term_index.T, points)


def cross_kernel(low_ref, psi_ref, yields_ref, kept_ref, sent_ref):
    rows = kept_ref.shape[0]
    for ref, which in ((sent_ref, low_ref[0] ^ 1), (kept_ref, low_ref[0])):
        part = psi_ref[pl.ds(pl.multiple_of(which * rows, rows), rows), :]
        ref[...] = jnp.dot(part, yields_ref[...], preferred_element_type=jnp.float32)


def cross_halves(psi, yields, low):
    half = jax.ShapeDtypeStruct((psi.shape[0] // 2, yields.shape[1]), jnp.float32)
    return pl.pallas_call(
        cross_kernel,
        out_shape=(half, half),
        in_specs=[SMEM, VMEM, VMEM],
        out_specs=(VMEM, VMEM),
        compiler_params=SMALL,
        name="cross_halves",
    )(low.reshape(1), psi, yields)


def lane_of(values, at):
    lanes = jnp.full(values.shape, at, jnp.int32)
    return jnp.take_along_axis(values, lanes, axis=1, mode="promise_in_bounds")


def row_of(values, at):
    return jnp.broadcast_to(values[at:at + 1, :], values.shape)


def stacked_outer(left, right):
    a, b = split3(left), split3(right)
    left = jnp.concatenate([a[0], a[0], a[1], a[1], a[0], a[2]], axis=0).astype(jnp.bfloat16)
    right = jnp.concatenate([b[0], b[1], b[0], b[1], b[2], b[0]], axis=0).astype(jnp.bfloat16)
    return lax.dot_general(left, right, (((0,), (0,)), ((), ())), preferred_element_type=jnp.float32)


def sweep_tile(bands):
    bands = list(bands)
    shape = bands[0].shape
    subs = lax.broadcasted_iota(jnp.int32, shape, 0)
    lanes = lax.broadcasted_iota(jnp.int32, shape, 1)
    for at in range(len(bands)):
        base = 8 * at
        own = bands[at]
        inside = (lanes >= base) & (lanes < base + 8)
        columns = [lane_of(own, base + k) for k in range(8)]
        fresh = jnp.where(inside, jnp.where(lanes == subs + base, -1.0, 0.0), own)
        for p in range(0, 8, 2):
            q = p + 1
            a, b, d = row_of(columns[p], p), row_of(columns[p], q), row_of(columns[q], q)
            det = a * d - b * b
            first = d * columns[p] - b * columns[q]
            second = a * columns[q] - b * columns[p]
            first = jnp.where(subs == p, det - d, jnp.where(subs == q, b, first))
            second = jnp.where(subs == p, b, jnp.where(subs == q, det - a, second))
            inverse = pltpu.reciprocal(det, approx=True)
            for k in range(q + 1, 8):
                less = first * row_of(columns[k], p) + second * row_of(columns[k], q)
                columns[k] = columns[k] - less * inverse
            less = first * row_of(fresh, p) + second * row_of(fresh, q)
            fresh = fresh - less * inverse
        delta = stacked_outer(own, fresh)
        following = (at + 1) % len(bands)
        for other in range(len(bands)):
            value = jnp.where(inside, 0.0, bands[other])
            if other == following:
                terms = [lane_of(bands[other], base + k) * row_of(fresh, k) for k in range(8)]
                while len(terms) > 1:
                    terms = [terms[k] + terms[k + 1] for k in range(0, len(terms), 2)]
                value = value - terms[0]
            else:
                value = value - delta[8 * other:8 * other + 8]
            bands[other] = value
        bands[at] = fresh
    return bands


def stacked_dot(left, right):
    a = [part.astype(jnp.bfloat16) for part in split3(left)]
    b = [part.astype(jnp.bfloat16) for part in split3(right)]
    left = jnp.concatenate([a[0], a[0], a[1], a[1], a[0], a[2]], axis=1)
    right = jnp.concatenate([b[0], b[1], b[0], b[1], b[2], b[0]], axis=0)
    return jnp.dot(left, right, preferred_element_type=jnp.float32)


def sweep_block(gram, out_ref, minus, block):
    terms = out_ref.shape[0]
    band = slice(block * TILE, (block + 1) * TILE)
    whole = slice(0, terms)
    fresh = -stacked_dot(minus, gram(band, whole))
    parts = [minus if at == block * TILE else fresh[:, at:at + TILE] for at in range(0, terms, TILE)]
    fresh = jnp.concatenate(parts, axis=1)
    change = stacked_dot(gram(whole, band), fresh)
    inside = (lax.broadcasted_iota(jnp.int32, (TILE, terms), 1) // TILE) == block
    for at in range(0, terms, TILE):
        rows = slice(at, at + TILE)
        if at == block * TILE:
            out_ref[rows, :] = fresh
        else:
            out_ref[rows, :] = jnp.where(inside, 0.0, gram(rows, whole)) - change[rows, :]


def sweep(tile):
    return jnp.concatenate(sweep_tile([tile[at:at + 8, :] for at in range(0, TILE, 8)]), axis=0)


def first_kernel(where_ref, *refs):
    out_ref, scale_ref, gram_ref, fold_ref = refs[-4:]
    terms = out_ref.shape[0]
    blocks = terms // TILE
    for step, ref in enumerate(refs[:-4]):
        piece = ref.shape[0] // 2
        eighth = ref.shape[0] // 8
        for at in range(8):
            row = ((at & 1) * 4 + (at & 2) + (at >> 2)) * eighth
            fold_ref[row:row + eighth, :] = ref[at * eighth:(at + 1) * eighth, :]
        start = pl.multiple_of((where_ref[0] ^ step) * piece, piece)
        for block in range(blocks):
            half, lane = fold_place(block, blocks)
            reach = (block + 1) * TILE
            gram_ref[pl.ds(start + block * TILE, piece), 0:reach] = (
                fold_ref[half * piece:(half + 1) * piece, lane:lane + reach]
            )
    diagonal = lax.broadcasted_iota(jnp.int32, (TILE, TILE), 0) == lax.broadcasted_iota(jnp.int32, (TILE, TILE), 1)
    bands = [slice(block * TILE, (block + 1) * TILE) for block in range(blocks)]
    across, down = [], []
    for band in bands:
        only = jnp.where(diagonal, gram_ref[band, band], 0.0)
        down.append(lax.rsqrt(jnp.sum(only, axis=1, keepdims=True)))
        across.append(lax.rsqrt(jnp.sum(only, axis=0, keepdims=True)))
    tiles = {}
    for i, band in enumerate(bands):
        scale_ref[band, :] = down[i]
        for j in range(i + 1):
            tiles[i, j] = gram_ref[band, bands[j]] * down[i] * across[j]
    minus = sweep(tiles[0, 0])
    for i, band in enumerate(bands):
        for j in range(i + 1):
            gram_ref[band, bands[j]] = tiles[i, j]
            if j < i:
                gram_ref[bands[j], band] = tiles[i, j].T
    sweep_block(lambda rows, lanes: gram_ref[rows, lanes], out_ref, minus, 0)


def next_kernel(block, in_ref, out_ref):
    band = slice(block * TILE, (block + 1) * TILE)
    sweep_block(lambda rows, lanes: in_ref[rows, lanes], out_ref, sweep(in_ref[band, band]), block)


STEP_COST = pl.CostEstimate(flops=10**9, bytes_accessed=2**20, transcendentals=512)


def first_block(where, pieces, terms):
    return pl.pallas_call(
        first_kernel,
        out_shape=(
            jax.ShapeDtypeStruct((terms, terms), jnp.float32),
            jax.ShapeDtypeStruct((terms, 1), jnp.float32),
        ),
        in_specs=[SMEM] + [VMEM] * len(pieces),
        out_specs=(VMEM, VMEM),
        scratch_shapes=[pltpu.VMEM((terms, terms), jnp.float32), pltpu.VMEM(pieces[0].shape, jnp.float32)],
        compiler_params=BIG,
        cost_estimate=STEP_COST,
        name="block_0",
    )(where, *pieces)


def next_block(gram, block):
    return pl.pallas_call(
        functools.partial(next_kernel, block),
        out_shape=jax.ShapeDtypeStruct(gram.shape, jnp.float32),
        in_specs=[VMEM],
        out_specs=VMEM,
        compiler_params=BIG,
        cost_estimate=STEP_COST,
        name="block_%d" % block,
    )(gram)


def solve_kernel(samples, steps, rows, finish, where_ref, group_ref, inverse_ref, scale_ref, *refs):
    count = len(steps)
    pieces = refs[:2]
    others = refs[2:-(count + finish + 1)]
    cross_ref = refs[-1]
    shares = refs[-(count + finish + 1):-(finish + 1)]
    steps_back = [0, 1, 4, 5, 2, 3, 6, 7]
    for ref in pieces:
        for at in range(0, ref.shape[0], rows):
            place = (where_ref[0] ^ steps_back.pop(0)) * rows
            cross_ref[pl.ds(pl.multiple_of(place, rows), rows), :] = ref[at:at + rows, :]
    terms, cells = cross_ref.shape
    scaled = scale_ref[...] * cross_ref[...]
    size = jnp.sqrt(jnp.float32(samples))
    share = shares[0].shape[0]
    for step, ref in zip(steps, shares):
        band = pl.ds(pl.multiple_of((where_ref[1] ^ step) * share, share), share)
        value = jnp.dot(inverse_ref[band, :], scaled, precision=HIGH, preferred_element_type=jnp.float32)
        ref[...] = -scale_ref[band, :] * value * size
    if not finish:
        return
    sobol_ref = refs[-2]
    totals, labels = [], []
    for step, ref in enumerate(shares + others):
        owner = where_ref[1] ^ step
        value = ref[...] / size
        squares = value * value
        row = lax.broadcasted_iota(jnp.int32, squares.shape, 0) + owner * share
        squares = jnp.where(row >= 1, squares, 0.0)
        for at in range(0, share, BLOCK):
            totals.append(jnp.sum(squares[at:at + BLOCK], axis=0, keepdims=True))
            labels.append(group_ref[owner * (share // BLOCK) + at // BLOCK])
    total = functools.reduce(jnp.add, totals)
    for group in range(GROUPS):
        part = jnp.zeros_like(total)
        for label, value in zip(labels, totals):
            part = part + jnp.where(label == group, value, 0.0)
        sobol_ref[group:group + 1, :] = part / total


def solve(where, inverse, scale, pieces, rows, block_group, samples, n_cell, steps, others=()):
    terms = inverse.shape[0]
    cells = pieces[0].shape[1]
    finish = len(others) > 0
    out = (jax.ShapeDtypeStruct((terms // n_cell, cells), jnp.float32),) * len(steps)
    if finish:
        out += (jax.ShapeDtypeStruct((GROUPS, cells), jnp.float32),)
    return pl.pallas_call(
        functools.partial(solve_kernel, samples, steps, rows, finish),
        out_shape=out,
        in_specs=[SMEM, SMEM] + [VMEM] * (2 + len(pieces) + len(others)),
        out_specs=(VMEM,) * len(out),
        scratch_shapes=[pltpu.VMEM((terms, cells), jnp.float32)],
        compiler_params=BIG,
        cost_estimate=pl.CostEstimate(flops=(5 if finish else 1) * 10**9, bytes_accessed=2**20, transcendentals=0),
        name="solve_near" if finish else "solve_far",
    )(where, block_group, inverse, scale, *pieces, *others)


def join_kernel(where_ref, *refs):
    out_ref = refs[-1]
    for step, ref in enumerate(refs[:-1]):
        wide = ref.shape[1]
        out_ref[:, pl.ds(pl.multiple_of((where_ref[0] ^ step) * wide, wide), wide)] = ref[...]


def join_columns(where, shares):
    rows, wide = shares[0].shape
    return pl.pallas_call(
        join_kernel,
        out_shape=jax.ShapeDtypeStruct((rows, wide * len(shares)), jnp.float32),
        in_specs=[SMEM] + [VMEM] * len(shares),
        out_specs=VMEM,
        compiler_params=SMALL,
        name="join_columns",
    )(where, *shares)


def swap(values, axis, step):
    size = lax.axis_size(axis)
    return lax.ppermute(values, axis, [(at, at ^ step) for at in range(size)])


def pick(values, at):
    return lax.dynamic_index_in_dim(values, at, axis=0, keepdims=False)


def halve(values, me, bit):
    halves = values.reshape(2, values.shape[0] // 2, values.shape[1])
    mine = (me >> bit) & 1
    return pick(halves, mine) + swap(pick(halves, mine ^ 1), "samp", 1 << bit)


def join(values, step):
    return jnp.concatenate([values, swap(values, "samp", step)], axis=0)


def add_rest(values):
    step = 8
    while step < lax.axis_size("samp"):
        values = values + swap(values, "samp", step)
        step *= 2
    return values


def on_device(points, yields, term_index, block_group):
    n_samp = lax.axis_size("samp")
    n_cell = lax.axis_size("cell")
    me, cell = lax.axis_index("samp"), lax.axis_index("cell")
    blocks = term_index.shape[0] // TILE
    psi, fold = design(points, term_index, cell, n_cell)
    spot = ((me & 1) << 2) | (me & 2) | ((me >> 2) & 1)
    fold = halve(fold, me, 0)
    kept, sent = cross_halves(psi, yields, me & 1)
    fold, kept, sent = lax.optimization_barrier((fold, kept, sent))
    part = kept + swap(sent, "samp", 1)
    fold = add_rest(halve(halve(fold, me, 1), me, 2))
    fold, part = lax.optimization_barrier((fold, part))
    part = halve(part, me, 1)
    copies = jnp.broadcast_to(fold[None], (n_samp,) + fold.shape)
    fold = lax.all_to_all(copies, "samp", split_axis=0, concat_axis=0)[:8].reshape(-1, fold.shape[1])
    fold, part = lax.optimization_barrier((fold, part))
    part = add_rest(halve(part, me, 2))
    rows = part.shape[0]
    held, order = [fold], [0]
    step = n_cell // 2
    while step:
        held = held + [swap(value, "cell", step) for value in held]
        order = order + [value ^ step for value in order]
        step //= 2
    held, part = lax.optimization_barrier((held, part))
    gram, scale = first_block(cell.reshape(1), [held[order.index(at)] for at in range(n_cell)], term_index.shape[0])
    for block in range(1, blocks):
        if block <= 2:
            part = join(part, (4, 1)[block - 1])
            gram, part = lax.optimization_barrier((gram, part))
        gram = next_block(gram, block)
    pieces = [part, swap(part, "samp", 2)]
    where = jnp.stack([spot, cell])
    given = (where, gram, scale, pieces, rows, block_group, points.shape[1] * n_samp, n_cell)
    far = solve(*given, tuple(range(1, n_cell)))
    came = [swap(value, "cell", 1 + at) for at, value in enumerate(far)]
    near, sobol = solve(*given, (0,), far)
    shares = [near] + came
    return (join_columns(cell.reshape(1), shares), sobol)


def solution(mesh):
    placed = (P(None, "samp"), P("samp", "cell"), P(), P())
    return jax.shard_map(
        on_device,
        mesh=mesh,
        in_specs=placed,
        out_specs=(P("cell", None), P(None, "cell")),
        check_vma=False,
    )
```

```python
import functools

import jax
import jax.numpy as jnp
from jax import lax
from jax.experimental import pallas as pl
from jax.experimental.pallas import tpu as pltpu
from jax.sharding import PartitionSpec as P

BLOCK = 64
GROUPS = 8
TILE = 128
HIGH = lax.Precision.HIGHEST
VMEM = pl.BlockSpec(memory_space=pltpu.VMEM)
SMEM = pl.BlockSpec(memory_space=pltpu.SMEM)
BIG = pltpu.CompilerParams(vmem_limit_bytes=16 * 2**20)
SMALL = pltpu.CompilerParams(vmem_limit_bytes=8 * 2**20)


def split3(values):
    top = values.astype(jnp.bfloat16).astype(jnp.float32)
    rest = values - top
    middle = rest.astype(jnp.bfloat16).astype(jnp.float32)
    return top, middle, rest - middle


def picks(column, params, width):
    span = 3 * params
    degree = column % 4
    place = (degree - 1) * params + column // 4
    at = lax.broadcasted_iota(jnp.int32, (width, column.shape[1]), 0)
    hit = (at == place) | (at == place + span) | (at == place + 2 * span)
    hit = (hit & (degree > 0)) | ((at == 3 * span) & (degree == 0))
    return hit.astype(jnp.float32).T.astype(jnp.bfloat16)


def design_kernel(chunk, cell_ref, index_ref, points_ref, psi_ref, fold_ref, table_ref):
    params, samples = points_ref.shape
    terms = index_ref.shape[1]
    width = table_ref.shape[0]
    span = 3 * params
    xs = points_ref[...]
    first = 1.7320508075688772 * xs
    second = 2.23606797749979 * (1.5 * xs * xs - 0.5)
    third = 2.6457513110645907 * (2.5 * xs * xs * xs - 1.5 * xs)
    for at, rows in enumerate((first, second, third)):
        for part, values in enumerate(split3(rows)):
            table_ref[pl.ds(part * span + at * params, params), :] = values
    table_ref[pl.ds(3 * span, width - 3 * span), :] = jnp.ones((width - 3 * span, samples), jnp.float32)
    pick_a = picks(index_ref[0:1, :], params, width)
    pick_b = picks(index_ref[1:2, :], params, width)
    for start in range(0, samples, chunk):
        table = table_ref[:, start:start + chunk].astype(jnp.bfloat16)
        left = jnp.dot(pick_a, table, preferred_element_type=jnp.float32)
        right = jnp.dot(pick_b, table, preferred_element_type=jnp.float32)
        psi_ref[:, start:start + chunk] = (left * right).astype(jnp.bfloat16)
    blocks = terms // TILE
    part_rows = fold_ref.shape[0] // 2
    cell = cell_ref[0]
    for block in range(blocks):
        rows = psi_ref[pl.ds(pl.multiple_of(block * TILE + cell * part_rows, part_rows), part_rows), :]
        reach = (block + 1) * TILE
        value = lax.dot_general(
            rows, psi_ref[0:reach, :], (((1,), (1,)), ((), ())), preferred_element_type=jnp.float32
        )
        half, at = fold_place(block, blocks)
        fold_ref[half * part_rows:(half + 1) * part_rows, at:at + reach] = value


def fold_place(block, blocks):
    low = min(block, blocks - 1 - block)
    return low, 0 if block == low else (low + 1) * TILE


def design(points, term_index, cell, n_cell):
    params, samples = points.shape
    terms = term_index.shape[0]
    blocks = terms // TILE
    rows = 2 * TILE // n_cell
    return pl.pallas_call(
        functools.partial(design_kernel, 512),
        out_shape=(
            jax.ShapeDtypeStruct((terms, samples), jnp.bfloat16),
            jax.ShapeDtypeStruct((rows, (blocks + 1) * TILE), jnp.float32),
        ),
        in_specs=[SMEM, VMEM, VMEM],
        out_specs=(VMEM, VMEM),
        scratch_shapes=[
            pltpu.VMEM((256, samples), jnp.float32),
        ],
        compiler_params=BIG,
        name="design",
    )(cell.reshape(1), term_index.T, points)


def cross_kernel(low_ref, psi_ref, yields_ref, kept_ref, sent_ref):
    rows = kept_ref.shape[0]
    for ref, which in ((sent_ref, low_ref[0] ^ 1), (kept_ref, low_ref[0])):
        part = psi_ref[pl.ds(pl.multiple_of(which * rows, rows), rows), :]
        ref[...] = jnp.dot(part, yields_ref[...], preferred_element_type=jnp.float32)


def cross_halves(psi, yields, low):
    half = jax.ShapeDtypeStruct((psi.shape[0] // 2, yields.shape[1]), jnp.float32)
    return pl.pallas_call(
        cross_kernel,
        out_shape=(half, half),
        in_specs=[SMEM, VMEM, VMEM],
        out_specs=(VMEM, VMEM),
        compiler_params=SMALL,
        name="cross_halves",
    )(low.reshape(1), psi, yields)


def lane_of(values, at):
    lanes = jnp.full(values.shape, at, jnp.int32)
    return jnp.take_along_axis(values, lanes, axis=1, mode="promise_in_bounds")


def row_of(values, at):
    return jnp.broadcast_to(values[at:at + 1, :], values.shape)


def stacked_outer(left, right):
    a, b = split3(left), split3(right)
    left = jnp.concatenate([a[0], a[0], a[1], a[1], a[0], a[2]], axis=0).astype(jnp.bfloat16)
    right = jnp.concatenate([b[0], b[1], b[0], b[1], b[2], b[0]], axis=0).astype(jnp.bfloat16)
    return lax.dot_general(left, right, (((0,), (0,)), ((), ())), preferred_element_type=jnp.float32)


def sweep_tile(bands):
    bands = list(bands)
    shape = bands[0].shape
    subs = lax.broadcasted_iota(jnp.int32, shape, 0)
    lanes = lax.broadcasted_iota(jnp.int32, shape, 1)
    for at in range(len(bands)):
        base = 8 * at
        own = bands[at]
        inside = (lanes >= base) & (lanes < base + 8)
        columns = [lane_of(own, base + k) for k in range(8)]
        fresh = jnp.where(inside, jnp.where(lanes == subs + base, -1.0, 0.0), own)
        for p in range(0, 8, 2):
            q = p + 1
            a, b, d = row_of(columns[p], p), row_of(columns[p], q), row_of(columns[q], q)
            det = a * d - b * b
            first = d * columns[p] - b * columns[q]
            second = a * columns[q] - b * columns[p]
            first = jnp.where(subs == p, det - d, jnp.where(subs == q, b, first))
            second = jnp.where(subs == p, b, jnp.where(subs == q, det - a, second))
            inverse = 1.0 / det
            for k in range(q + 1, 8):
                less = first * row_of(columns[k], p) + second * row_of(columns[k], q)
                columns[k] = columns[k] - less * inverse
            less = first * row_of(fresh, p) + second * row_of(fresh, q)
            fresh = fresh - less * inverse
        delta = stacked_outer(own, fresh)
        following = ((at + 1) % len(bands), (at + 2) % len(bands))
        for other in range(len(bands)):
            value = jnp.where(inside, 0.0, bands[other])
            if other in following:
                terms = [lane_of(bands[other], base + k) * row_of(fresh, k) for k in range(8)]
                while len(terms) > 1:
                    terms = [terms[k] + terms[k + 1] for k in range(0, len(terms), 2)]
                value = value - terms[0]
            else:
                value = value - delta[8 * other:8 * other + 8]
            bands[other] = value
        bands[at] = fresh
    return bands


def stacked_dot(left, right):
    a = [part.astype(jnp.bfloat16) for part in split3(left)]
    b = [part.astype(jnp.bfloat16) for part in split3(right)]
    left = jnp.concatenate([a[0], a[0], a[1], a[1], a[0], a[2]], axis=1)
    right = jnp.concatenate([b[0], b[1], b[0], b[1], b[2], b[0]], axis=0)
    return jnp.dot(left, right, preferred_element_type=jnp.float32)


def sweep_block(gram, out_ref, minus, block):
    terms = out_ref.shape[0]
    band = slice(block * TILE, (block + 1) * TILE)
    whole = slice(0, terms)
    fresh = -stacked_dot(minus, gram(band, whole))
    parts = [minus if at == block * TILE else fresh[:, at:at + TILE] for at in range(0, terms, TILE)]
    fresh = jnp.concatenate(parts, axis=1)
    change = stacked_dot(gram(whole, band), fresh)
    inside = (lax.broadcasted_iota(jnp.int32, (TILE, terms), 1) // TILE) == block
    for at in range(0, terms, TILE):
        rows = slice(at, at + TILE)
        if at == block * TILE:
            out_ref[rows, :] = fresh
        else:
            out_ref[rows, :] = jnp.where(inside, 0.0, gram(rows, whole)) - change[rows, :]


def sweep(tile):
    return jnp.concatenate(sweep_tile([tile[at:at + 8, :] for at in range(0, TILE, 8)]), axis=0)


def first_kernel(where_ref, *refs):
    out_ref, scale_ref, gram_ref, fold_ref = refs[-4:]
    terms = out_ref.shape[0]
    blocks = terms // TILE
    for step, ref in enumerate(refs[:-4]):
        piece = ref.shape[0] // 2
        eighth = ref.shape[0] // 8
        for at in range(8):
            row = ((at & 1) * 4 + (at & 2) + (at >> 2)) * eighth
            fold_ref[row:row + eighth, :] = ref[at * eighth:(at + 1) * eighth, :]
        start = pl.multiple_of((where_ref[0] ^ step) * piece, piece)
        for block in range(blocks):
            half, lane = fold_place(block, blocks)
            reach = (block + 1) * TILE
            gram_ref[pl.ds(start + block * TILE, piece), 0:reach] = (
                fold_ref[half * piece:(half + 1) * piece, lane:lane + reach]
            )
    diagonal = lax.broadcasted_iota(jnp.int32, (TILE, TILE), 0) == lax.broadcasted_iota(jnp.int32, (TILE, TILE), 1)
    bands = [slice(block * TILE, (block + 1) * TILE) for block in range(blocks)]
    across, down = [], []
    for band in bands:
        only = jnp.where(diagonal, gram_ref[band, band], 0.0)
        down.append(lax.rsqrt(jnp.sum(only, axis=1, keepdims=True)))
        across.append(lax.rsqrt(jnp.sum(only, axis=0, keepdims=True)))
    tiles = {}
    for i, band in enumerate(bands):
        scale_ref[band, :] = down[i]
        for j in range(i + 1):
            tiles[i, j] = gram_ref[band, bands[j]] * down[i] * across[j]
    minus = sweep(tiles[0, 0])
    for i, band in enumerate(bands):
        for j in range(i + 1):
            gram_ref[band, bands[j]] = tiles[i, j]
            if j < i:
                gram_ref[bands[j], band] = tiles[i, j].T
    sweep_block(lambda rows, lanes: gram_ref[rows, lanes], out_ref, minus, 0)


def next_kernel(block, in_ref, out_ref):
    band = slice(block * TILE, (block + 1) * TILE)
    sweep_block(lambda rows, lanes: in_ref[rows, lanes], out_ref, sweep(in_ref[band, band]), block)


STEP_COST = pl.CostEstimate(flops=10**9, bytes_accessed=2**20, transcendentals=512)


def first_block(where, pieces, terms):
    return pl.pallas_call(
        first_kernel,
        out_shape=(
            jax.ShapeDtypeStruct((terms, terms), jnp.float32),
            jax.ShapeDtypeStruct((terms, 1), jnp.float32),
        ),
        in_specs=[SMEM] + [VMEM] * len(pieces),
        out_specs=(VMEM, VMEM),
        scratch_shapes=[pltpu.VMEM((terms, terms), jnp.float32), pltpu.VMEM(pieces[0].shape, jnp.float32)],
        compiler_params=BIG,
        cost_estimate=STEP_COST,
        name="block_0",
    )(where, *pieces)


def next_block(gram, block):
    return pl.pallas_call(
        functools.partial(next_kernel, block),
        out_shape=jax.ShapeDtypeStruct(gram.shape, jnp.float32),
        in_specs=[VMEM],
        out_specs=VMEM,
        compiler_params=BIG,
        cost_estimate=STEP_COST,
        name="block_%d" % block,
    )(gram)


def solve_kernel(samples, steps, rows, finish, where_ref, group_ref, inverse_ref, scale_ref, *refs):
    count = len(steps)
    pieces = refs[:2]
    others = refs[2:-(count + finish + 1)]
    cross_ref = refs[-1]
    shares = refs[-(count + finish + 1):-(finish + 1)]
    steps_back = [0, 1, 4, 5, 2, 3, 6, 7]
    for ref in pieces:
        for at in range(0, ref.shape[0], rows):
            place = (where_ref[0] ^ steps_back.pop(0)) * rows
            cross_ref[pl.ds(pl.multiple_of(place, rows), rows), :] = ref[at:at + rows, :]
    terms, cells = cross_ref.shape
    scaled = scale_ref[...] * cross_ref[...]
    size = jnp.sqrt(jnp.float32(samples))
    share = shares[0].shape[0]
    for step, ref in zip(steps, shares):
        band = pl.ds(pl.multiple_of((where_ref[1] ^ step) * share, share), share)
        value = jnp.dot(inverse_ref[band, :], scaled, precision=HIGH, preferred_element_type=jnp.float32)
        ref[...] = -scale_ref[band, :] * value * size
    if not finish:
        return
    sobol_ref = refs[-2]
    totals, labels = [], []
    for step, ref in enumerate(shares + others):
        owner = where_ref[1] ^ step
        value = ref[...] / size
        squares = value * value
        row = lax.broadcasted_iota(jnp.int32, squares.shape, 0) + owner * share
        squares = jnp.where(row >= 1, squares, 0.0)
        for at in range(0, share, BLOCK):
            totals.append(jnp.sum(squares[at:at + BLOCK], axis=0, keepdims=True))
            labels.append(group_ref[owner * (share // BLOCK) + at // BLOCK])
    total = functools.reduce(jnp.add, totals)
    for group in range(GROUPS):
        part = jnp.zeros_like(total)
        for label, value in zip(labels, totals):
            part = part + jnp.where(label == group, value, 0.0)
        sobol_ref[group:group + 1, :] = part / total


def solve(where, inverse, scale, pieces, rows, block_group, samples, n_cell, steps, others=()):
    terms = inverse.shape[0]
    cells = pieces[0].shape[1]
    finish = len(others) > 0
    out = (jax.ShapeDtypeStruct((terms // n_cell, cells), jnp.float32),) * len(steps)
    if finish:
        out += (jax.ShapeDtypeStruct((GROUPS, cells), jnp.float32),)
    return pl.pallas_call(
        functools.partial(solve_kernel, samples, steps, rows, finish),
        out_shape=out,
        in_specs=[SMEM, SMEM] + [VMEM] * (2 + len(pieces) + len(others)),
        out_specs=(VMEM,) * len(out),
        scratch_shapes=[pltpu.VMEM((terms, cells), jnp.float32)],
        compiler_params=BIG,
        cost_estimate=pl.CostEstimate(flops=(5 if finish else 1) * 10**9, bytes_accessed=2**20, transcendentals=0),
        name="solve_near" if finish else "solve_far",
    )(where, block_group, inverse, scale, *pieces, *others)


def join_kernel(where_ref, *refs):
    out_ref = refs[-1]
    for step, ref in enumerate(refs[:-1]):
        wide = ref.shape[1]
        out_ref[:, pl.ds(pl.multiple_of((where_ref[0] ^ step) * wide, wide), wide)] = ref[...]


def join_columns(where, shares):
    rows, wide = shares[0].shape
    return pl.pallas_call(
        join_kernel,
        out_shape=jax.ShapeDtypeStruct((rows, wide * len(shares)), jnp.float32),
        in_specs=[SMEM] + [VMEM] * len(shares),
        out_specs=VMEM,
        compiler_params=SMALL,
        name="join_columns",
    )(where, *shares)


def swap(values, axis, step):
    size = lax.axis_size(axis)
    return lax.ppermute(values, axis, [(at, at ^ step) for at in range(size)])


def pick(values, at):
    return lax.dynamic_index_in_dim(values, at, axis=0, keepdims=False)


def halve(values, me, bit):
    halves = values.reshape(2, values.shape[0] // 2, values.shape[1])
    mine = (me >> bit) & 1
    return pick(halves, mine) + swap(pick(halves, mine ^ 1), "samp", 1 << bit)


def join(values, step):
    return jnp.concatenate([values, swap(values, "samp", step)], axis=0)


def add_rest(values):
    step = 8
    while step < lax.axis_size("samp"):
        values = values + swap(values, "samp", step)
        step *= 2
    return values


def on_device(points, yields, term_index, block_group):
    n_samp = lax.axis_size("samp")
    n_cell = lax.axis_size("cell")
    me, cell = lax.axis_index("samp"), lax.axis_index("cell")
    blocks = term_index.shape[0] // TILE
    psi, fold = design(points, term_index, cell, n_cell)
    spot = ((me & 1) << 2) | (me & 2) | ((me >> 2) & 1)
    fold = halve(fold, me, 0)
    kept, sent = cross_halves(psi, yields, me & 1)
    fold, kept, sent = lax.optimization_barrier((fold, kept, sent))
    part = kept + swap(sent, "samp", 1)
    fold = add_rest(halve(halve(fold, me, 1), me, 2))
    fold, part = lax.optimization_barrier((fold, part))
    part = halve(part, me, 1)
    copies = jnp.broadcast_to(fold[None], (n_samp,) + fold.shape)
    fold = lax.all_to_all(copies, "samp", split_axis=0, concat_axis=0)[:8].reshape(-1, fold.shape[1])
    fold, part = lax.optimization_barrier((fold, part))
    part = add_rest(halve(part, me, 2))
    rows = part.shape[0]
    held, order = [fold], [0]
    step = n_cell // 2
    while step:
        held = held + [swap(value, "cell", step) for value in held]
        order = order + [value ^ step for value in order]
        step //= 2
    held, part = lax.optimization_barrier((held, part))
    gram, scale = first_block(cell.reshape(1), [held[order.index(at)] for at in range(n_cell)], term_index.shape[0])
    for block in range(1, blocks):
        if block <= 2:
            part = join(part, (4, 1)[block - 1])
            gram, part = lax.optimization_barrier((gram, part))
        gram = next_block(gram, block)
    pieces = [part, swap(part, "samp", 2)]
    where = jnp.stack([spot, cell])
    given = (where, gram, scale, pieces, rows, block_group, points.shape[1] * n_samp, n_cell)
    far = solve(*given, tuple(range(1, n_cell)))
    came = [swap(value, "cell", 1 + at) for at, value in enumerate(far)]
    near, sobol = solve(*given, (0,), far)
    shares = [near] + came
    return (join_columns(cell.reshape(1), shares), sobol)


def solution(mesh):
    placed = (P(None, "samp"), P("samp", "cell"), P(), P())
    return jax.shard_map(
        on_device,
        mesh=mesh,
        in_specs=placed,
        out_specs=(P("cell", None), P(None, "cell")),
        check_vma=False,
    )
```

```python
import functools

import jax
import jax.numpy as jnp
from jax import lax
from jax.experimental import pallas as pl
from jax.experimental.pallas import tpu as pltpu
from jax.sharding import PartitionSpec as P

BLOCK = 64
GROUPS = 8
TILE = 128
VMEM = pl.BlockSpec(memory_space=pltpu.VMEM)
SMEM = pl.BlockSpec(memory_space=pltpu.SMEM)
BIG = pltpu.CompilerParams(vmem_limit_bytes=16 * 2**20)
SMALL = pltpu.CompilerParams(vmem_limit_bytes=8 * 2**20)


def split3(values):
    top = values.astype(jnp.bfloat16).astype(jnp.float32)
    rest = values - top
    middle = rest.astype(jnp.bfloat16).astype(jnp.float32)
    return top, middle, rest - middle


def picks(column, params, width):
    span = 3 * params
    degree = column % 4
    place = (degree - 1) * params + column // 4
    at = lax.broadcasted_iota(jnp.int32, (width, column.shape[1]), 0)
    hit = (at == place) | (at == place + span) | (at == place + 2 * span)
    hit = (hit & (degree > 0)) | ((at == 3 * span) & (degree == 0))
    return hit.astype(jnp.float32).T.astype(jnp.bfloat16)


def design_kernel(chunk, cell_ref, index_ref, points_ref, psi_ref, fold_ref, table_ref):
    params, samples = points_ref.shape
    terms = index_ref.shape[1]
    width = table_ref.shape[0]
    span = 3 * params
    xs = points_ref[...]
    first = 1.7320508075688772 * xs
    second = 2.23606797749979 * (1.5 * xs * xs - 0.5)
    third = 2.6457513110645907 * (2.5 * xs * xs * xs - 1.5 * xs)
    for at, rows in enumerate((first, second, third)):
        for part, values in enumerate(split3(rows)):
            table_ref[pl.ds(part * span + at * params, params), :] = values
    table_ref[pl.ds(3 * span, width - 3 * span), :] = jnp.ones((width - 3 * span, samples), jnp.float32)
    pick_a = picks(index_ref[0:1, :], params, width)
    pick_b = picks(index_ref[1:2, :], params, width)
    for start in range(0, samples, chunk):
        table = table_ref[:, start:start + chunk].astype(jnp.bfloat16)
        left = jnp.dot(pick_a, table, preferred_element_type=jnp.float32)
        right = jnp.dot(pick_b, table, preferred_element_type=jnp.float32)
        psi_ref[:, start:start + chunk] = (left * right).astype(jnp.bfloat16)
    blocks = terms // TILE
    part_rows = fold_ref.shape[0] // 2
    cell = cell_ref[0]
    for block in range(blocks):
        rows = psi_ref[pl.ds(pl.multiple_of(block * TILE + cell * part_rows, part_rows), part_rows), :]
        reach = (block + 1) * TILE
        value = lax.dot_general(
            rows, psi_ref[0:reach, :], (((1,), (1,)), ((), ())), preferred_element_type=jnp.float32
        )
        half, at = fold_place(block, blocks)
        fold_ref[half * part_rows:(half + 1) * part_rows, at:at + reach] = value


def fold_place(block, blocks):
    low = min(block, blocks - 1 - block)
    return low, 0 if block == low else (low + 1) * TILE


def design(points, term_index, cell, n_cell):
    params, samples = points.shape
    terms = term_index.shape[0]
    blocks = terms // TILE
    rows = 2 * TILE // n_cell
    return pl.pallas_call(
        functools.partial(design_kernel, 512),
        out_shape=(
            jax.ShapeDtypeStruct((terms, samples), jnp.bfloat16),
            jax.ShapeDtypeStruct((rows, (blocks + 1) * TILE), jnp.float32),
        ),
        in_specs=[SMEM, VMEM, VMEM],
        out_specs=(VMEM, VMEM),
        scratch_shapes=[
            pltpu.VMEM((256, samples), jnp.float32),
        ],
        compiler_params=BIG,
        name="design",
    )(cell.reshape(1), term_index.T, points)


def cross_kernel(low_ref, psi_ref, yields_ref, kept_ref, sent_ref):
    rows = kept_ref.shape[0]
    for ref, which in ((sent_ref, low_ref[0] ^ 1), (kept_ref, low_ref[0])):
        part = psi_ref[pl.ds(pl.multiple_of(which * rows, rows), rows), :]
        ref[...] = jnp.dot(part, yields_ref[...], preferred_element_type=jnp.float32)


def cross_halves(psi, yields, low):
    half = jax.ShapeDtypeStruct((psi.shape[0] // 2, yields.shape[1]), jnp.float32)
    return pl.pallas_call(
        cross_kernel,
        out_shape=(half, half),
        in_specs=[SMEM, VMEM, VMEM],
        out_specs=(VMEM, VMEM),
        compiler_params=SMALL,
        name="cross_halves",
    )(low.reshape(1), psi, yields)


def lane_of(values, at):
    lanes = jnp.full(values.shape, at, jnp.int32)
    return jnp.take_along_axis(values, lanes, axis=1, mode="promise_in_bounds")


def row_of(values, at):
    return jnp.broadcast_to(values[at:at + 1, :], values.shape)


def stacked_outer(left, right):
    a, b = split3(left), split3(right)
    left = jnp.concatenate([a[0], a[0], a[1], a[1], a[0], a[2]], axis=0).astype(jnp.bfloat16)
    right = jnp.concatenate([b[0], b[1], b[0], b[1], b[2], b[0]], axis=0).astype(jnp.bfloat16)
    return lax.dot_general(left, right, (((0,), (0,)), ((), ())), preferred_element_type=jnp.float32)


def sweep_tile(bands):
    bands = list(bands)
    shape = bands[0].shape
    subs = lax.broadcasted_iota(jnp.int32, shape, 0)
    lanes = lax.broadcasted_iota(jnp.int32, shape, 1)
    for at in range(len(bands)):
        base = 8 * at
        own = bands[at]
        inside = (lanes >= base) & (lanes < base + 8)
        columns = [lane_of(own, base + k) for k in range(8)]
        fresh = jnp.where(inside, jnp.where(lanes == subs + base, -1.0, 0.0), own)
        for p in range(0, 8, 2):
            q = p + 1
            a, b, d = row_of(columns[p], p), row_of(columns[p], q), row_of(columns[q], q)
            det = a * d - b * b
            first = d * columns[p] - b * columns[q]
            second = a * columns[q] - b * columns[p]
            first = jnp.where(subs == p, det - d, jnp.where(subs == q, b, first))
            second = jnp.where(subs == p, b, jnp.where(subs == q, det - a, second))
            inverse = 1.0 / det
            for k in range(q + 1, 8):
                less = first * row_of(columns[k], p) + second * row_of(columns[k], q)
                columns[k] = columns[k] - less * inverse
            less = first * row_of(fresh, p) + second * row_of(fresh, q)
            fresh = fresh - less * inverse
        delta = stacked_outer(own, fresh)
        following = (at + 1) % len(bands)
        for other in range(len(bands)):
            value = jnp.where(inside, 0.0, bands[other])
            if other == following:
                terms = [lane_of(bands[other], base + k) * row_of(fresh, k) for k in range(8)]
                while len(terms) > 1:
                    terms = [terms[k] + terms[k + 1] for k in range(0, len(terms), 2)]
                value = value - terms[0]
            else:
                value = value - delta[8 * other:8 * other + 8]
            bands[other] = value
        bands[at] = fresh
    return bands


def stacked_dot(left, right):
    a = [part.astype(jnp.bfloat16) for part in split3(left)]
    b = [part.astype(jnp.bfloat16) for part in split3(right)]
    left = jnp.concatenate([a[0], a[0], a[1], a[1], a[0], a[2]], axis=1)
    right = jnp.concatenate([b[0], b[1], b[0], b[1], b[2], b[0]], axis=0)
    return jnp.dot(left, right, preferred_element_type=jnp.float32)


def sweep_block(gram, out_ref, minus, block):
    terms = out_ref.shape[0]
    band = slice(block * TILE, (block + 1) * TILE)
    whole = slice(0, terms)
    fresh = -stacked_dot(minus, gram(band, whole))
    parts = [minus if at == block * TILE else fresh[:, at:at + TILE] for at in range(0, terms, TILE)]
    fresh = jnp.concatenate(parts, axis=1)
    starts = [at for at in range(0, terms, TILE) if at != block * TILE]
    change = stacked_dot(jnp.concatenate([gram(slice(at, at + TILE), band) for at in starts], axis=0), fresh)
    inside = (lax.broadcasted_iota(jnp.int32, (TILE, terms), 1) // TILE) == block
    out_ref[band, :] = fresh
    for place, at in enumerate(starts):
        rows = slice(at, at + TILE)
        out_ref[rows, :] = jnp.where(inside, 0.0, gram(rows, whole)) - change[place * TILE:(place + 1) * TILE, :]


def sweep(tile):
    return jnp.concatenate(sweep_tile([tile[at:at + 8, :] for at in range(0, TILE, 8)]), axis=0)


def first_kernel(where_ref, *refs):
    out_ref, scale_ref, gram_ref, fold_ref = refs[-4:]
    terms = out_ref.shape[0]
    blocks = terms // TILE
    for step, ref in enumerate(refs[:-4]):
        piece = ref.shape[0] // 2
        eighth = ref.shape[0] // 8
        for at in range(8):
            row = ((at & 1) * 4 + (at & 2) + (at >> 2)) * eighth
            fold_ref[row:row + eighth, :] = ref[at * eighth:(at + 1) * eighth, :]
        start = pl.multiple_of((where_ref[0] ^ step) * piece, piece)
        for block in range(blocks):
            half, lane = fold_place(block, blocks)
            reach = (block + 1) * TILE
            gram_ref[pl.ds(start + block * TILE, piece), 0:reach] = (
                fold_ref[half * piece:(half + 1) * piece, lane:lane + reach]
            )
    diagonal = lax.broadcasted_iota(jnp.int32, (TILE, TILE), 0) == lax.broadcasted_iota(jnp.int32, (TILE, TILE), 1)
    bands = [slice(block * TILE, (block + 1) * TILE) for block in range(blocks)]
    across, down = [], []
    for band in bands:
        only = jnp.where(diagonal, gram_ref[band, band], 0.0)
        down.append(lax.rsqrt(jnp.sum(only, axis=1, keepdims=True)))
        across.append(lax.rsqrt(jnp.sum(only, axis=0, keepdims=True)))
    tiles = {}
    for i, band in enumerate(bands):
        scale_ref[band, :] = down[i]
        for j in range(i + 1):
            tiles[i, j] = gram_ref[band, bands[j]] * down[i] * across[j]
    minus = sweep(tiles[0, 0])
    for i, band in enumerate(bands):
        for j in range(i + 1):
            gram_ref[band, bands[j]] = tiles[i, j]
            if j < i:
                gram_ref[bands[j], band] = tiles[i, j].T
    sweep_block(lambda rows, lanes: gram_ref[rows, lanes], out_ref, minus, 0)


def next_kernel(block, in_ref, out_ref):
    band = slice(block * TILE, (block + 1) * TILE)
    sweep_block(lambda rows, lanes: in_ref[rows, lanes], out_ref, sweep(in_ref[band, band]), block)


STEP_COST = pl.CostEstimate(flops=10**9, bytes_accessed=2**20, transcendentals=512)


def first_block(where, pieces, terms):
    return pl.pallas_call(
        first_kernel,
        out_shape=(
            jax.ShapeDtypeStruct((terms, terms), jnp.float32),
            jax.ShapeDtypeStruct((terms, 1), jnp.float32),
        ),
        in_specs=[SMEM] + [VMEM] * len(pieces),
        out_specs=(VMEM, VMEM),
        scratch_shapes=[pltpu.VMEM((terms, terms), jnp.float32), pltpu.VMEM(pieces[0].shape, jnp.float32)],
        compiler_params=BIG,
        cost_estimate=STEP_COST,
        name="block_0",
    )(where, *pieces)


def next_block(gram, block):
    return pl.pallas_call(
        functools.partial(next_kernel, block),
        out_shape=jax.ShapeDtypeStruct(gram.shape, jnp.float32),
        in_specs=[VMEM],
        out_specs=VMEM,
        compiler_params=BIG,
        cost_estimate=STEP_COST,
        name="block_%d" % block,
    )(gram)


def solve_kernel(samples, steps, rows, finish, where_ref, group_ref, inverse_ref, scale_ref, *refs):
    count = len(steps)
    pieces = refs[:2]
    others = refs[2:-(count + finish + 1)]
    cross_ref = refs[-1]
    shares = refs[-(count + finish + 1):-(finish + 1)]
    steps_back = [0, 1, 4, 5, 2, 3, 6, 7]
    for ref in pieces:
        for at in range(0, ref.shape[0], rows):
            place = (where_ref[0] ^ steps_back.pop(0)) * rows
            cross_ref[pl.ds(pl.multiple_of(place, rows), rows), :] = ref[at:at + rows, :]
    terms, cells = cross_ref.shape
    scaled = scale_ref[...] * cross_ref[...]
    size = jnp.sqrt(jnp.float32(samples))
    share = shares[0].shape[0]
    bands = [pl.ds(pl.multiple_of((where_ref[1] ^ step) * share, share), share) for step in steps]
    values = stacked_dot(jnp.concatenate([inverse_ref[band, :] for band in bands], axis=0), scaled)
    for at, (band, ref) in enumerate(zip(bands, shares)):
        ref[...] = -scale_ref[band, :] * values[at * share:(at + 1) * share, :] * size
    if not finish:
        return
    sobol_ref = refs[-2]
    totals, labels = [], []
    for step, ref in enumerate(shares + others):
        owner = where_ref[1] ^ step
        value = ref[...] / size
        squares = value * value
        row = lax.broadcasted_iota(jnp.int32, squares.shape, 0) + owner * share
        squares = jnp.where(row >= 1, squares, 0.0)
        for at in range(0, share, BLOCK):
            totals.append(jnp.sum(squares[at:at + BLOCK], axis=0, keepdims=True))
            labels.append(group_ref[owner * (share // BLOCK) + at // BLOCK])
    total = functools.reduce(jnp.add, totals)
    for group in range(GROUPS):
        part = jnp.zeros_like(total)
        for label, value in zip(labels, totals):
            part = part + jnp.where(label == group, value, 0.0)
        sobol_ref[group:group + 1, :] = part / total


def solve(where, inverse, scale, pieces, rows, block_group, samples, n_cell, steps, others=()):
    terms = inverse.shape[0]
    cells = pieces[0].shape[1]
    finish = len(others) > 0
    out = (jax.ShapeDtypeStruct((terms // n_cell, cells), jnp.float32),) * len(steps)
    if finish:
        out += (jax.ShapeDtypeStruct((GROUPS, cells), jnp.float32),)
    return pl.pallas_call(
        functools.partial(solve_kernel, samples, steps, rows, finish),
        out_shape=out,
        in_specs=[SMEM, SMEM] + [VMEM] * (2 + len(pieces) + len(others)),
        out_specs=(VMEM,) * len(out),
        scratch_shapes=[pltpu.VMEM((terms, cells), jnp.float32)],
        compiler_params=BIG,
        cost_estimate=pl.CostEstimate(flops=(5 if finish else 1) * 10**9, bytes_accessed=2**20, transcendentals=0),
        name="solve_near" if finish else "solve_far",
    )(where, block_group, inverse, scale, *pieces, *others)


def join_kernel(where_ref, *refs):
    out_ref = refs[-1]
    for step, ref in enumerate(refs[:-1]):
        wide = ref.shape[1]
        out_ref[:, pl.ds(pl.multiple_of((where_ref[0] ^ step) * wide, wide), wide)] = ref[...]


def join_columns(where, shares):
    rows, wide = shares[0].shape
    return pl.pallas_call(
        join_kernel,
        out_shape=jax.ShapeDtypeStruct((rows, wide * len(shares)), jnp.float32),
        in_specs=[SMEM] + [VMEM] * len(shares),
        out_specs=VMEM,
        compiler_params=SMALL,
        name="join_columns",
    )(where, *shares)


def swap(values, axis, step):
    size = lax.axis_size(axis)
    return lax.ppermute(values, axis, [(at, at ^ step) for at in range(size)])


def pick(values, at):
    return lax.dynamic_index_in_dim(values, at, axis=0, keepdims=False)


def halve(values, me, bit):
    halves = values.reshape(2, values.shape[0] // 2, values.shape[1])
    mine = (me >> bit) & 1
    return pick(halves, mine) + swap(pick(halves, mine ^ 1), "samp", 1 << bit)


def join(values, step):
    return jnp.concatenate([values, swap(values, "samp", step)], axis=0)


def add_rest(values):
    step = 8
    while step < lax.axis_size("samp"):
        values = values + swap(values, "samp", step)
        step *= 2
    return values


def on_device(points, yields, term_index, block_group):
    n_samp = lax.axis_size("samp")
    n_cell = lax.axis_size("cell")
    me, cell = lax.axis_index("samp"), lax.axis_index("cell")
    blocks = term_index.shape[0] // TILE
    psi, fold = design(points, term_index, cell, n_cell)
    spot = ((me & 1) << 2) | (me & 2) | ((me >> 2) & 1)
    fold = halve(fold, me, 0)
    kept, sent = cross_halves(psi, yields, me & 1)
    fold, kept, sent = lax.optimization_barrier((fold, kept, sent))
    part = kept + swap(sent, "samp", 1)
    fold = add_rest(halve(halve(fold, me, 1), me, 2))
    fold, part = lax.optimization_barrier((fold, part))
    part = halve(part, me, 1)
    copies = jnp.broadcast_to(fold[None], (n_samp,) + fold.shape)
    fold = lax.all_to_all(copies, "samp", split_axis=0, concat_axis=0)[:8].reshape(-1, fold.shape[1])
    fold, part = lax.optimization_barrier((fold, part))
    part = add_rest(halve(part, me, 2))
    rows = part.shape[0]
    held, order = [fold], [0]
    step = n_cell // 2
    while step:
        held = held + [swap(value, "cell", step) for value in held]
        order = order + [value ^ step for value in order]
        step //= 2
    held, part = lax.optimization_barrier((held, part))
    gram, scale = first_block(cell.reshape(1), [held[order.index(at)] for at in range(n_cell)], term_index.shape[0])
    for block in range(1, blocks):
        if block <= 2:
            part = join(part, (4, 1)[block - 1])
            gram, part = lax.optimization_barrier((gram, part))
        gram = next_block(gram, block)
    pieces = [part, swap(part, "samp", 2)]
    where = jnp.stack([spot, cell])
    given = (where, gram, scale, pieces, rows, block_group, points.shape[1] * n_samp, n_cell)
    far = solve(*given, tuple(range(1, n_cell)))
    came = [swap(value, "cell", 1 + at) for at, value in enumerate(far)]
    near, sobol = solve(*given, (0,), far)
    shares = [near] + came
    return (join_columns(cell.reshape(1), shares), sobol)


def solution(mesh):
    placed = (P(None, "samp"), P("samp", "cell"), P(), P())
    return jax.shard_map(
        on_device,
        mesh=mesh,
        in_specs=placed,
        out_specs=(P("cell", None), P(None, "cell")),
        check_vma=False,
    )
```

```python
import functools

import jax
import jax.numpy as jnp
from jax import lax
from jax.experimental import pallas as pl
from jax.experimental.pallas import tpu as pltpu
from jax.sharding import PartitionSpec as P

BLOCK = 64
GROUPS = 8
TILE = 128
VMEM = pl.BlockSpec(memory_space=pltpu.VMEM)
SMEM = pl.BlockSpec(memory_space=pltpu.SMEM)
BIG = pltpu.CompilerParams(vmem_limit_bytes=16 * 2**20)
SMALL = pltpu.CompilerParams(vmem_limit_bytes=8 * 2**20)


def split3(values):
    top = values.astype(jnp.bfloat16).astype(jnp.float32)
    rest = values - top
    middle = rest.astype(jnp.bfloat16).astype(jnp.float32)
    return top, middle, rest - middle


def picks(column, params, width):
    span = 3 * params
    degree = column % 4
    place = (degree - 1) * params + column // 4
    at = lax.broadcasted_iota(jnp.int32, (width, column.shape[1]), 0)
    hit = (at == place) | (at == place + span) | (at == place + 2 * span)
    hit = (hit & (degree > 0)) | ((at == 3 * span) & (degree == 0))
    return hit.astype(jnp.float32).T.astype(jnp.bfloat16)


def design_kernel(chunk, cell_ref, index_ref, points_ref, psi_ref, fold_ref, table_ref):
    params, samples = points_ref.shape
    terms = index_ref.shape[1]
    width = table_ref.shape[0]
    span = 3 * params
    xs = points_ref[...]
    first = 1.7320508075688772 * xs
    second = 2.23606797749979 * (1.5 * xs * xs - 0.5)
    third = 2.6457513110645907 * (2.5 * xs * xs * xs - 1.5 * xs)
    for at, rows in enumerate((first, second, third)):
        for part, values in enumerate(split3(rows)):
            table_ref[pl.ds(part * span + at * params, params), :] = values
    table_ref[pl.ds(3 * span, width - 3 * span), :] = jnp.ones((width - 3 * span, samples), jnp.float32)
    pick_a = picks(index_ref[0:1, :], params, width)
    pick_b = picks(index_ref[1:2, :], params, width)
    for start in range(0, samples, chunk):
        table = table_ref[:, start:start + chunk].astype(jnp.bfloat16)
        left = jnp.dot(pick_a, table, preferred_element_type=jnp.float32)
        right = jnp.dot(pick_b, table, preferred_element_type=jnp.float32)
        psi_ref[:, start:start + chunk] = (left * right).astype(jnp.bfloat16)
    blocks = terms // TILE
    part_rows = fold_ref.shape[0] // 2
    cell = cell_ref[0]
    rows = jnp.concatenate([
        psi_ref[pl.ds(pl.multiple_of(block * TILE + cell * part_rows, part_rows), part_rows), :]
        for block in range(blocks)
    ], axis=0)
    value = lax.dot_general(
        psi_ref[...], rows, (((1,), (1,)), ((), ())), preferred_element_type=jnp.float32
    ).T
    for block in range(blocks):
        reach = (block + 1) * TILE
        half, at = fold_place(block, blocks)
        fold_ref[half * part_rows:(half + 1) * part_rows, at:at + reach] = (
            value[block * part_rows:(block + 1) * part_rows, 0:reach]
        )


def fold_place(block, blocks):
    low = min(block, blocks - 1 - block)
    return low, 0 if block == low else (low + 1) * TILE


def design(points, term_index, cell, n_cell):
    params, samples = points.shape
    terms = term_index.shape[0]
    blocks = terms // TILE
    rows = 2 * TILE // n_cell
    return pl.pallas_call(
        functools.partial(design_kernel, 512),
        out_shape=(
            jax.ShapeDtypeStruct((terms, samples), jnp.bfloat16),
            jax.ShapeDtypeStruct((rows, (blocks + 1) * TILE), jnp.float32),
        ),
        in_specs=[SMEM, VMEM, VMEM],
        out_specs=(VMEM, VMEM),
        scratch_shapes=[
            pltpu.VMEM((256, samples), jnp.float32),
        ],
        compiler_params=BIG,
        name="design",
    )(cell.reshape(1), term_index.T, points)


def cross_kernel(low_ref, psi_ref, yields_ref, kept_ref, sent_ref):
    rows = kept_ref.shape[0]
    for ref, which in ((sent_ref, low_ref[0] ^ 1), (kept_ref, low_ref[0])):
        part = psi_ref[pl.ds(pl.multiple_of(which * rows, rows), rows), :]
        ref[...] = jnp.dot(part, yields_ref[...], preferred_element_type=jnp.float32)


def cross_halves(psi, yields, low):
    half = jax.ShapeDtypeStruct((psi.shape[0] // 2, yields.shape[1]), jnp.float32)
    return pl.pallas_call(
        cross_kernel,
        out_shape=(half, half),
        in_specs=[SMEM, VMEM, VMEM],
        out_specs=(VMEM, VMEM),
        compiler_params=SMALL,
        name="cross_halves",
    )(low.reshape(1), psi, yields)


def lane_of(values, at):
    lanes = jnp.full(values.shape, at, jnp.int32)
    return jnp.take_along_axis(values, lanes, axis=1, mode="promise_in_bounds")


def row_of(values, at):
    return jnp.broadcast_to(values[at:at + 1, :], values.shape)


def stacked_outer(left, right):
    a, b = split3(left), split3(right)
    left = jnp.concatenate([a[0], a[0], a[1], a[1], a[0], a[2]], axis=0).astype(jnp.bfloat16)
    right = jnp.concatenate([b[0], b[1], b[0], b[1], b[2], b[0]], axis=0).astype(jnp.bfloat16)
    return lax.dot_general(left, right, (((0,), (0,)), ((), ())), preferred_element_type=jnp.float32)


def sweep_tile(bands):
    bands = list(bands)
    shape = bands[0].shape
    subs = lax.broadcasted_iota(jnp.int32, shape, 0)
    lanes = lax.broadcasted_iota(jnp.int32, shape, 1)
    for at in range(len(bands)):
        base = 8 * at
        own = bands[at]
        inside = (lanes >= base) & (lanes < base + 8)
        columns = [lane_of(own, base + k) for k in range(8)]
        fresh = jnp.where(inside, jnp.where(lanes == subs + base, -1.0, 0.0), own)
        for p in range(0, 8, 2):
            q = p + 1
            a, b, d = row_of(columns[p], p), row_of(columns[p], q), row_of(columns[q], q)
            det = a * d - b * b
            first = d * columns[p] - b * columns[q]
            second = a * columns[q] - b * columns[p]
            first = jnp.where(subs == p, det - d, jnp.where(subs == q, b, first))
            second = jnp.where(subs == p, b, jnp.where(subs == q, det - a, second))
            inverse = 1.0 / det
            for k in range(q + 1, 8):
                less = first * row_of(columns[k], p) + second * row_of(columns[k], q)
                columns[k] = columns[k] - less * inverse
            less = first * row_of(fresh, p) + second * row_of(fresh, q)
            fresh = fresh - less * inverse
        delta = stacked_outer(own, fresh)
        following = (at + 1) % len(bands)
        for other in range(len(bands)):
            value = jnp.where(inside, 0.0, bands[other])
            if other == following:
                terms = [lane_of(bands[other], base + k) * row_of(fresh, k) for k in range(8)]
                while len(terms) > 1:
                    terms = [terms[k] + terms[k + 1] for k in range(0, len(terms), 2)]
                value = value - terms[0]
            else:
                value = value - delta[8 * other:8 * other + 8]
            bands[other] = value
        bands[at] = fresh
    return bands


def stacked_dot(left, right):
    a = [part.astype(jnp.bfloat16) for part in split3(left)]
    b = [part.astype(jnp.bfloat16) for part in split3(right)]
    left = jnp.concatenate([a[0], a[0], a[1], a[1], a[0], a[2]], axis=1)
    right = jnp.concatenate([b[0], b[1], b[0], b[1], b[2], b[0]], axis=0)
    return jnp.dot(left, right, preferred_element_type=jnp.float32)


def sweep_block(gram, out_ref, minus, block):
    terms = out_ref.shape[0]
    band = slice(block * TILE, (block + 1) * TILE)
    whole = slice(0, terms)
    fresh = -stacked_dot(minus, gram(band, whole))
    parts = [minus if at == block * TILE else fresh[:, at:at + TILE] for at in range(0, terms, TILE)]
    fresh = jnp.concatenate(parts, axis=1)
    starts = [at for at in range(0, terms, TILE) if at != block * TILE]
    change = stacked_dot(jnp.concatenate([gram(slice(at, at + TILE), band) for at in starts], axis=0), fresh)
    inside = (lax.broadcasted_iota(jnp.int32, (TILE, terms), 1) // TILE) == block
    out_ref[band, :] = fresh
    for place, at in enumerate(starts):
        rows = slice(at, at + TILE)
        out_ref[rows, :] = jnp.where(inside, 0.0, gram(rows, whole)) - change[place * TILE:(place + 1) * TILE, :]


def sweep(tile):
    return jnp.concatenate(sweep_tile([tile[at:at + 8, :] for at in range(0, TILE, 8)]), axis=0)


def first_kernel(where_ref, *refs):
    out_ref, scale_ref, gram_ref, fold_ref = refs[-4:]
    terms = out_ref.shape[0]
    blocks = terms // TILE
    for step, ref in enumerate(refs[:-4]):
        piece = ref.shape[0] // 2
        eighth = ref.shape[0] // 8
        for at in range(8):
            row = ((at & 1) * 4 + (at & 2) + (at >> 2)) * eighth
            fold_ref[row:row + eighth, :] = ref[at * eighth:(at + 1) * eighth, :]
        start = pl.multiple_of((where_ref[0] ^ step) * piece, piece)
        for block in range(blocks):
            half, lane = fold_place(block, blocks)
            reach = (block + 1) * TILE
            gram_ref[pl.ds(start + block * TILE, piece), 0:reach] = (
                fold_ref[half * piece:(half + 1) * piece, lane:lane + reach]
            )
    diagonal = lax.broadcasted_iota(jnp.int32, (TILE, TILE), 0) == lax.broadcasted_iota(jnp.int32, (TILE, TILE), 1)
    bands = [slice(block * TILE, (block + 1) * TILE) for block in range(blocks)]
    across, down = [], []
    for band in bands:
        only = jnp.where(diagonal, gram_ref[band, band], 0.0)
        down.append(lax.rsqrt(jnp.sum(only, axis=1, keepdims=True)))
        across.append(lax.rsqrt(jnp.sum(only, axis=0, keepdims=True)))
    tiles = {}
    for i, band in enumerate(bands):
        scale_ref[band, :] = down[i]
        for j in range(i + 1):
            tiles[i, j] = gram_ref[band, bands[j]] * down[i] * across[j]
    minus = sweep(tiles[0, 0])
    for i, band in enumerate(bands):
        for j in range(i + 1):
            gram_ref[band, bands[j]] = tiles[i, j]
            if j < i:
                gram_ref[bands[j], band] = tiles[i, j].T
    sweep_block(lambda rows, lanes: gram_ref[rows, lanes], out_ref, minus, 0)


def next_kernel(block, in_ref, out_ref):
    band = slice(block * TILE, (block + 1) * TILE)
    sweep_block(lambda rows, lanes: in_ref[rows, lanes], out_ref, sweep(in_ref[band, band]), block)


STEP_COST = pl.CostEstimate(flops=10**9, bytes_accessed=2**20, transcendentals=512)


def first_block(where, pieces, terms):
    return pl.pallas_call(
        first_kernel,
        out_shape=(
            jax.ShapeDtypeStruct((terms, terms), jnp.float32),
            jax.ShapeDtypeStruct((terms, 1), jnp.float32),
        ),
        in_specs=[SMEM] + [VMEM] * len(pieces),
        out_specs=(VMEM, VMEM),
        scratch_shapes=[pltpu.VMEM((terms, terms), jnp.float32), pltpu.VMEM(pieces[0].shape, jnp.float32)],
        compiler_params=BIG,
        cost_estimate=STEP_COST,
        name="block_0",
    )(where, *pieces)


def next_block(gram, block):
    return pl.pallas_call(
        functools.partial(next_kernel, block),
        out_shape=jax.ShapeDtypeStruct(gram.shape, jnp.float32),
        in_specs=[VMEM],
        out_specs=VMEM,
        compiler_params=BIG,
        cost_estimate=STEP_COST,
        name="block_%d" % block,
    )(gram)


def solve_kernel(samples, steps, rows, finish, where_ref, group_ref, inverse_ref, scale_ref, *refs):
    count = len(steps)
    pieces = refs[:2]
    others = refs[2:-(count + finish + 1)]
    cross_ref = refs[-1]
    shares = refs[-(count + finish + 1):-(finish + 1)]
    steps_back = [0, 1, 4, 5, 2, 3, 6, 7]
    for ref in pieces:
        for at in range(0, ref.shape[0], rows):
            place = (where_ref[0] ^ steps_back.pop(0)) * rows
            cross_ref[pl.ds(pl.multiple_of(place, rows), rows), :] = ref[at:at + rows, :]
    terms, cells = cross_ref.shape
    scaled = scale_ref[...] * cross_ref[...]
    size = jnp.sqrt(jnp.float32(samples))
    share = shares[0].shape[0]
    bands = [pl.ds(pl.multiple_of((where_ref[1] ^ step) * share, share), share) for step in steps]
    values = stacked_dot(jnp.concatenate([inverse_ref[band, :] for band in bands], axis=0), scaled)
    for at, (band, ref) in enumerate(zip(bands, shares)):
        ref[...] = -scale_ref[band, :] * values[at * share:(at + 1) * share, :] * size
    if not finish:
        return
    sobol_ref = refs[-2]
    totals, labels = [], []
    for step, ref in enumerate(shares + others):
        owner = where_ref[1] ^ step
        value = ref[...] / size
        squares = value * value
        row = lax.broadcasted_iota(jnp.int32, squares.shape, 0) + owner * share
        squares = jnp.where(row >= 1, squares, 0.0)
        for at in range(0, share, BLOCK):
            totals.append(jnp.sum(squares[at:at + BLOCK], axis=0, keepdims=True))
            labels.append(group_ref[owner * (share // BLOCK) + at // BLOCK])
    total = functools.reduce(jnp.add, totals)
    for group in range(GROUPS):
        part = jnp.zeros_like(total)
        for label, value in zip(labels, totals):
            part = part + jnp.where(label == group, value, 0.0)
        sobol_ref[group:group + 1, :] = part / total


def solve(where, inverse, scale, pieces, rows, block_group, samples, n_cell, steps, others=()):
    terms = inverse.shape[0]
    cells = pieces[0].shape[1]
    finish = len(others) > 0
    out = (jax.ShapeDtypeStruct((terms // n_cell, cells), jnp.float32),) * len(steps)
    if finish:
        out += (jax.ShapeDtypeStruct((GROUPS, cells), jnp.float32),)
    return pl.pallas_call(
        functools.partial(solve_kernel, samples, steps, rows, finish),
        out_shape=out,
        in_specs=[SMEM, SMEM] + [VMEM] * (2 + len(pieces) + len(others)),
        out_specs=(VMEM,) * len(out),
        scratch_shapes=[pltpu.VMEM((terms, cells), jnp.float32)],
        compiler_params=BIG,
        cost_estimate=pl.CostEstimate(flops=(5 if finish else 1) * 10**9, bytes_accessed=2**20, transcendentals=0),
        name="solve_near" if finish else "solve_far",
    )(where, block_group, inverse, scale, *pieces, *others)


def join_kernel(where_ref, *refs):
    out_ref = refs[-1]
    for step, ref in enumerate(refs[:-1]):
        wide = ref.shape[1]
        out_ref[:, pl.ds(pl.multiple_of((where_ref[0] ^ step) * wide, wide), wide)] = ref[...]


def join_columns(where, shares):
    rows, wide = shares[0].shape
    return pl.pallas_call(
        join_kernel,
        out_shape=jax.ShapeDtypeStruct((rows, wide * len(shares)), jnp.float32),
        in_specs=[SMEM] + [VMEM] * len(shares),
        out_specs=VMEM,
        compiler_params=SMALL,
        name="join_columns",
    )(where, *shares)


def swap(values, axis, step):
    size = lax.axis_size(axis)
    return lax.ppermute(values, axis, [(at, at ^ step) for at in range(size)])


def pick(values, at):
    return lax.dynamic_index_in_dim(values, at, axis=0, keepdims=False)


def halve(values, me, bit):
    halves = values.reshape(2, values.shape[0] // 2, values.shape[1])
    mine = (me >> bit) & 1
    return pick(halves, mine) + swap(pick(halves, mine ^ 1), "samp", 1 << bit)


def join(values, step):
    return jnp.concatenate([values, swap(values, "samp", step)], axis=0)


def add_rest(values):
    step = 8
    while step < lax.axis_size("samp"):
        values = values + swap(values, "samp", step)
        step *= 2
    return values


def on_device(points, yields, term_index, block_group):
    n_samp = lax.axis_size("samp")
    n_cell = lax.axis_size("cell")
    me, cell = lax.axis_index("samp"), lax.axis_index("cell")
    blocks = term_index.shape[0] // TILE
    psi, fold = design(points, term_index, cell, n_cell)
    spot = ((me & 1) << 2) | (me & 2) | ((me >> 2) & 1)
    fold = halve(fold, me, 0)
    kept, sent = cross_halves(psi, yields, me & 1)
    fold, kept, sent = lax.optimization_barrier((fold, kept, sent))
    part = kept + swap(sent, "samp", 1)
    fold = add_rest(halve(halve(fold, me, 1), me, 2))
    fold, part = lax.optimization_barrier((fold, part))
    part = halve(part, me, 1)
    copies = jnp.broadcast_to(fold[None], (n_samp,) + fold.shape)
    fold = lax.all_to_all(copies, "samp", split_axis=0, concat_axis=0)[:8].reshape(-1, fold.shape[1])
    fold, part = lax.optimization_barrier((fold, part))
    part = add_rest(halve(part, me, 2))
    rows = part.shape[0]
    held, order = [fold], [0]
    step = n_cell // 2
    while step:
        held = held + [swap(value, "cell", step) for value in held]
        order = order + [value ^ step for value in order]
        step //= 2
    held, part = lax.optimization_barrier((held, part))
    gram, scale = first_block(cell.reshape(1), [held[order.index(at)] for at in range(n_cell)], term_index.shape[0])
    for block in range(1, blocks):
        if block <= 2:
            part = join(part, (4, 1)[block - 1])
            gram, part = lax.optimization_barrier((gram, part))
        gram = next_block(gram, block)
    pieces = [part, swap(part, "samp", 2)]
    where = jnp.stack([spot, cell])
    given = (where, gram, scale, pieces, rows, block_group, points.shape[1] * n_samp, n_cell)
    far = solve(*given, tuple(range(1, n_cell)))
    came = [swap(value, "cell", 1 + at) for at, value in enumerate(far)]
    near, sobol = solve(*given, (0,), far)
    shares = [near] + came
    return (join_columns(cell.reshape(1), shares), sobol)


def solution(mesh):
    placed = (P(None, "samp"), P("samp", "cell"), P(), P())
    return jax.shard_map(
        on_device,
        mesh=mesh,
        in_specs=placed,
        out_specs=(P("cell", None), P(None, "cell")),
        check_vma=False,
    )
```

```python
import functools

import jax
import jax.numpy as jnp
from jax import lax
from jax.experimental import pallas as pl
from jax.experimental.pallas import tpu as pltpu
from jax.sharding import PartitionSpec as P

BLOCK = 64
GROUPS = 8
TILE = 128
VMEM = pl.BlockSpec(memory_space=pltpu.VMEM)
SMEM = pl.BlockSpec(memory_space=pltpu.SMEM)
BIG = pltpu.CompilerParams(vmem_limit_bytes=16 * 2**20)
SMALL = pltpu.CompilerParams(vmem_limit_bytes=8 * 2**20)


def split3(values):
    top = values.astype(jnp.bfloat16).astype(jnp.float32)
    rest = values - top
    middle = rest.astype(jnp.bfloat16).astype(jnp.float32)
    return top, middle, rest - middle


def picks(column, params, width):
    span = 3 * params
    degree = column % 4
    place = (degree - 1) * params + column // 4
    at = lax.broadcasted_iota(jnp.int32, (width, column.shape[1]), 0)
    hit = (at == place) | (at == place + span) | (at == place + 2 * span)
    hit = (hit & (degree > 0)) | ((at == 3 * span) & (degree == 0))
    return hit.astype(jnp.float32).T.astype(jnp.bfloat16)


def design_kernel(chunk, cell_ref, index_ref, points_ref, psi_ref, fold_ref, table_ref):
    params, samples = points_ref.shape
    terms = index_ref.shape[1]
    width = table_ref.shape[0]
    span = 3 * params
    xs = points_ref[...]
    first = 1.7320508075688772 * xs
    second = 2.23606797749979 * (1.5 * xs * xs - 0.5)
    third = 2.6457513110645907 * (2.5 * xs * xs * xs - 1.5 * xs)
    for at, rows in enumerate((first, second, third)):
        for part, values in enumerate(split3(rows)):
            table_ref[pl.ds(part * span + at * params, params), :] = values
    table_ref[pl.ds(3 * span, width - 3 * span), :] = jnp.ones((width - 3 * span, samples), jnp.float32)
    pick_a = picks(index_ref[0:1, :], params, width)
    pick_b = picks(index_ref[1:2, :], params, width)
    for start in range(0, samples, chunk):
        table = table_ref[:, start:start + chunk].astype(jnp.bfloat16)
        left = jnp.dot(pick_a, table, preferred_element_type=jnp.float32)
        right = jnp.dot(pick_b, table, preferred_element_type=jnp.float32)
        psi_ref[:, start:start + chunk] = (left * right).astype(jnp.bfloat16)
    blocks = terms // TILE
    part_rows = fold_ref.shape[0] // 2
    cell = cell_ref[0]
    rows = jnp.concatenate([
        psi_ref[pl.ds(pl.multiple_of(block * TILE + cell * part_rows, part_rows), part_rows), :]
        for block in range(blocks)
    ], axis=0)
    value = lax.dot_general(
        rows, psi_ref[...], (((1,), (1,)), ((), ())), preferred_element_type=jnp.float32
    )
    for block in range(blocks):
        reach = (block + 1) * TILE
        half, at = fold_place(block, blocks)
        fold_ref[half * part_rows:(half + 1) * part_rows, at:at + reach] = (
            value[block * part_rows:(block + 1) * part_rows, 0:reach]
        )


def fold_place(block, blocks):
    low = min(block, blocks - 1 - block)
    return low, 0 if block == low else (low + 1) * TILE


def design(points, term_index, cell, n_cell):
    params, samples = points.shape
    terms = term_index.shape[0]
    blocks = terms // TILE
    rows = 2 * TILE // n_cell
    return pl.pallas_call(
        functools.partial(design_kernel, 512),
        out_shape=(
            jax.ShapeDtypeStruct((terms, samples), jnp.bfloat16),
            jax.ShapeDtypeStruct((rows, (blocks + 1) * TILE), jnp.float32),
        ),
        in_specs=[SMEM, VMEM, VMEM],
        out_specs=(VMEM, VMEM),
        scratch_shapes=[
            pltpu.VMEM((256, samples), jnp.float32),
        ],
        compiler_params=BIG,
        name="design",
    )(cell.reshape(1), term_index.T, points)


def cross_kernel(low_ref, psi_ref, yields_ref, kept_ref, sent_ref):
    rows = kept_ref.shape[0]
    for ref, which in ((sent_ref, low_ref[0] ^ 1), (kept_ref, low_ref[0])):
        part = psi_ref[pl.ds(pl.multiple_of(which * rows, rows), rows), :]
        ref[...] = jnp.dot(part, yields_ref[...], preferred_element_type=jnp.float32)


def cross_halves(psi, yields, low):
    half = jax.ShapeDtypeStruct((psi.shape[0] // 2, yields.shape[1]), jnp.float32)
    return pl.pallas_call(
        cross_kernel,
        out_shape=(half, half),
        in_specs=[SMEM, VMEM, VMEM],
        out_specs=(VMEM, VMEM),
        compiler_params=SMALL,
        name="cross_halves",
    )(low.reshape(1), psi, yields)


def lane_of(values, at):
    lanes = jnp.full(values.shape, at, jnp.int32)
    return jnp.take_along_axis(values, lanes, axis=1, mode="promise_in_bounds")


def row_of(values, at):
    return jnp.broadcast_to(values[at:at + 1, :], values.shape)


def stacked_outer(left, right):
    a, b = split3(left), split3(right)
    left = jnp.concatenate([a[0], a[0], a[1], a[1], a[0], a[2]], axis=0).astype(jnp.bfloat16)
    right = jnp.concatenate([b[0], b[1], b[0], b[1], b[2], b[0]], axis=0).astype(jnp.bfloat16)
    return lax.dot_general(left, right, (((0,), (0,)), ((), ())), preferred_element_type=jnp.float32)


def sweep_tile(bands):
    bands = list(bands)
    shape = bands[0].shape
    subs = lax.broadcasted_iota(jnp.int32, shape, 0)
    lanes = lax.broadcasted_iota(jnp.int32, shape, 1)
    for at in range(len(bands)):
        base = 8 * at
        own = bands[at]
        inside = (lanes >= base) & (lanes < base + 8)
        columns = [lane_of(own, base + k) for k in range(8)]
        fresh = jnp.where(inside, jnp.where(lanes == subs + base, -1.0, 0.0), own)
        for p in range(0, 8, 2):
            q = p + 1
            a, b, d = row_of(columns[p], p), row_of(columns[p], q), row_of(columns[q], q)
            det = a * d - b * b
            first = d * columns[p] - b * columns[q]
            second = a * columns[q] - b * columns[p]
            first = jnp.where(subs == p, det - d, jnp.where(subs == q, b, first))
            second = jnp.where(subs == p, b, jnp.where(subs == q, det - a, second))
            inverse = 1.0 / det
            for k in range(q + 1, 8):
                less = first * row_of(columns[k], p) + second * row_of(columns[k], q)
                columns[k] = columns[k] - less * inverse
            less = first * row_of(fresh, p) + second * row_of(fresh, q)
            fresh = fresh - less * inverse
        delta = stacked_outer(own, fresh)
        following = (at + 1) % len(bands)
        for other in range(len(bands)):
            value = jnp.where(inside, 0.0, bands[other])
            if other == following:
                terms = [lane_of(bands[other], base + k) * row_of(fresh, k) for k in range(8)]
                while len(terms) > 1:
                    terms = [terms[k] + terms[k + 1] for k in range(0, len(terms), 2)]
                value = value - terms[0]
            else:
                value = value - delta[8 * other:8 * other + 8]
            bands[other] = value
        bands[at] = fresh
    return bands


def stacked_dot(left, right):
    a = [part.astype(jnp.bfloat16) for part in split3(left)]
    b = [part.astype(jnp.bfloat16) for part in split3(right)]
    left = jnp.concatenate([a[0], a[0], a[1], a[1], a[0], a[2]], axis=1)
    right = jnp.concatenate([b[0], b[1], b[0], b[1], b[2], b[0]], axis=0)
    return jnp.dot(left, right, preferred_element_type=jnp.float32)


def sweep_block(gram, out_ref, minus, block):
    terms = out_ref.shape[0]
    band = slice(block * TILE, (block + 1) * TILE)
    whole = slice(0, terms)
    fresh = -stacked_dot(minus, gram(band, whole))
    parts = [minus if at == block * TILE else fresh[:, at:at + TILE] for at in range(0, terms, TILE)]
    fresh = jnp.concatenate(parts, axis=1)
    starts = [at for at in range(0, terms, TILE) if at != block * TILE]
    change = stacked_dot(jnp.concatenate([gram(slice(at, at + TILE), band) for at in starts], axis=0), fresh)
    inside = (lax.broadcasted_iota(jnp.int32, (TILE, terms), 1) // TILE) == block
    out_ref[band, :] = fresh
    for place, at in enumerate(starts):
        rows = slice(at, at + TILE)
        out_ref[rows, :] = jnp.where(inside, 0.0, gram(rows, whole)) - change[place * TILE:(place + 1) * TILE, :]


def sweep(tile):
    return jnp.concatenate(sweep_tile([tile[at:at + 8, :] for at in range(0, TILE, 8)]), axis=0)


def first_kernel(where_ref, *refs):
    out_ref, scale_ref, gram_ref, fold_ref = refs[-4:]
    terms = out_ref.shape[0]
    blocks = terms // TILE
    for step, ref in enumerate(refs[:-4]):
        piece = ref.shape[0] // 2
        eighth = ref.shape[0] // 8
        for at in range(8):
            row = ((at & 1) * 4 + (at & 2) + (at >> 2)) * eighth
            fold_ref[row:row + eighth, :] = ref[at * eighth:(at + 1) * eighth, :]
        start = pl.multiple_of((where_ref[0] ^ step) * piece, piece)
        for block in range(blocks):
            half, lane = fold_place(block, blocks)
            reach = (block + 1) * TILE
            gram_ref[pl.ds(start + block * TILE, piece), 0:reach] = (
                fold_ref[half * piece:(half + 1) * piece, lane:lane + reach]
            )
    diagonal = lax.broadcasted_iota(jnp.int32, (TILE, TILE), 0) == lax.broadcasted_iota(jnp.int32, (TILE, TILE), 1)
    bands = [slice(block * TILE, (block + 1) * TILE) for block in range(blocks)]
    across, down = [], []
    for band in bands:
        only = jnp.where(diagonal, gram_ref[band, band], 0.0)
        down.append(lax.rsqrt(jnp.sum(only, axis=1, keepdims=True)))
        across.append(lax.rsqrt(jnp.sum(only, axis=0, keepdims=True)))
    tiles = {}
    for i, band in enumerate(bands):
        scale_ref[band, :] = down[i]
        for j in range(i + 1):
            tiles[i, j] = gram_ref[band, bands[j]] * down[i] * across[j]
    minus = sweep(tiles[0, 0])
    for i, band in enumerate(bands):
        for j in range(i + 1):
            gram_ref[band, bands[j]] = tiles[i, j]
            if j < i:
                gram_ref[bands[j], band] = tiles[i, j].T
    sweep_block(lambda rows, lanes: gram_ref[rows, lanes], out_ref, minus, 0)


def next_kernel(block, in_ref, out_ref):
    band = slice(block * TILE, (block + 1) * TILE)
    sweep_block(lambda rows, lanes: in_ref[rows, lanes], out_ref, sweep(in_ref[band, band]), block)


STEP_COST = pl.CostEstimate(flops=10**9, bytes_accessed=2**20, transcendentals=512)


def first_block(where, pieces, terms):
    return pl.pallas_call(
        first_kernel,
        out_shape=(
            jax.ShapeDtypeStruct((terms, terms), jnp.float32),
            jax.ShapeDtypeStruct((terms, 1), jnp.float32),
        ),
        in_specs=[SMEM] + [VMEM] * len(pieces),
        out_specs=(VMEM, VMEM),
        scratch_shapes=[pltpu.VMEM((terms, terms), jnp.float32), pltpu.VMEM(pieces[0].shape, jnp.float32)],
        compiler_params=BIG,
        cost_estimate=STEP_COST,
        name="block_0",
    )(where, *pieces)


def next_block(gram, block):
    return pl.pallas_call(
        functools.partial(next_kernel, block),
        out_shape=jax.ShapeDtypeStruct(gram.shape, jnp.float32),
        in_specs=[VMEM],
        out_specs=VMEM,
        compiler_params=BIG,
        cost_estimate=STEP_COST,
        name="block_%d" % block,
    )(gram)


def solve_kernel(samples, steps, rows, finish, where_ref, group_ref, inverse_ref, scale_ref, *refs):
    count = len(steps)
    pieces = refs[:2]
    others = refs[2:-(count + finish + 1)]
    cross_ref = refs[-1]
    shares = refs[-(count + finish + 1):-(finish + 1)]
    steps_back = [0, 1, 4, 5, 2, 3, 6, 7]
    for ref in pieces:
        for at in range(0, ref.shape[0], rows):
            place = (where_ref[0] ^ steps_back.pop(0)) * rows
            cross_ref[pl.ds(pl.multiple_of(place, rows), rows), :] = ref[at:at + rows, :]
    terms, cells = cross_ref.shape
    scaled = scale_ref[...] * cross_ref[...]
    size = jnp.sqrt(jnp.float32(samples))
    share = shares[0].shape[0]
    bands = [pl.ds(pl.multiple_of((where_ref[1] ^ step) * share, share), share) for step in steps]
    values = stacked_dot(jnp.concatenate([inverse_ref[band, :] for band in bands], axis=0), scaled)
    for at, (band, ref) in enumerate(zip(bands, shares)):
        ref[...] = -scale_ref[band, :] * values[at * share:(at + 1) * share, :] * size
    if not finish:
        return
    sobol_ref = refs[-2]
    totals, labels = [], []
    for step, ref in enumerate(shares + others):
        owner = where_ref[1] ^ step
        value = ref[...] / size
        squares = value * value
        row = lax.broadcasted_iota(jnp.int32, squares.shape, 0) + owner * share
        squares = jnp.where(row >= 1, squares, 0.0)
        for at in range(0, share, BLOCK):
            totals.append(jnp.sum(squares[at:at + BLOCK], axis=0, keepdims=True))
            labels.append(group_ref[owner * (share // BLOCK) + at // BLOCK])
    total = functools.reduce(jnp.add, totals)
    for group in range(GROUPS):
        part = jnp.zeros_like(total)
        for label, value in zip(labels, totals):
            part = part + jnp.where(label == group, value, 0.0)
        sobol_ref[group:group + 1, :] = part / total


def solve(where, inverse, scale, pieces, rows, block_group, samples, n_cell, steps, others=()):
    terms = inverse.shape[0]
    cells = pieces[0].shape[1]
    finish = len(others) > 0
    out = (jax.ShapeDtypeStruct((terms // n_cell, cells), jnp.float32),) * len(steps)
    if finish:
        out += (jax.ShapeDtypeStruct((GROUPS, cells), jnp.float32),)
    return pl.pallas_call(
        functools.partial(solve_kernel, samples, steps, rows, finish),
        out_shape=out,
        in_specs=[SMEM, SMEM] + [VMEM] * (2 + len(pieces) + len(others)),
        out_specs=(VMEM,) * len(out),
        scratch_shapes=[pltpu.VMEM((terms, cells), jnp.float32)],
        compiler_params=BIG,
        cost_estimate=pl.CostEstimate(flops=(5 if finish else 1) * 10**9, bytes_accessed=2**20, transcendentals=0),
        name="solve_near" if finish else "solve_far",
    )(where, block_group, inverse, scale, *pieces, *others)


def join_kernel(where_ref, *refs):
    out_ref = refs[-1]
    for step, ref in enumerate(refs[:-1]):
        wide = ref.shape[1]
        out_ref[:, pl.ds(pl.multiple_of((where_ref[0] ^ step) * wide, wide), wide)] = ref[...]


def join_columns(where, shares):
    rows, wide = shares[0].shape
    return pl.pallas_call(
        join_kernel,
        out_shape=jax.ShapeDtypeStruct((rows, wide * len(shares)), jnp.float32),
        in_specs=[SMEM] + [VMEM] * len(shares),
        out_specs=VMEM,
        compiler_params=SMALL,
        name="join_columns",
    )(where, *shares)


def swap(values, axis, step):
    size = lax.axis_size(axis)
    return lax.ppermute(values, axis, [(at, at ^ step) for at in range(size)])


def pick(values, at):
    return lax.dynamic_index_in_dim(values, at, axis=0, keepdims=False)


def halve(values, me, bit):
    halves = values.reshape(2, values.shape[0] // 2, values.shape[1])
    mine = (me >> bit) & 1
    return pick(halves, mine) + swap(pick(halves, mine ^ 1), "samp", 1 << bit)


def join(values, step):
    return jnp.concatenate([values, swap(values, "samp", step)], axis=0)


def add_rest(values):
    step = 8
    while step < lax.axis_size("samp"):
        values = values + swap(values, "samp", step)
        step *= 2
    return values


def on_device(points, yields, term_index, block_group):
    n_samp = lax.axis_size("samp")
    n_cell = lax.axis_size("cell")
    me, cell = lax.axis_index("samp"), lax.axis_index("cell")
    blocks = term_index.shape[0] // TILE
    psi, fold = design(points, term_index, cell, n_cell)
    spot = ((me & 1) << 2) | (me & 2) | ((me >> 2) & 1)
    fold = halve(fold, me, 0)
    kept, sent = cross_halves(psi, yields, me & 1)
    fold, kept, sent = lax.optimization_barrier((fold, kept, sent))
    part = kept + swap(sent, "samp", 1)
    fold = add_rest(halve(halve(fold, me, 1), me, 2))
    fold, part = lax.optimization_barrier((fold, part))
    part = halve(part, me, 1)
    copies = jnp.broadcast_to(fold[None], (n_samp,) + fold.shape)
    fold = lax.all_to_all(copies, "samp", split_axis=0, concat_axis=0)[:8].reshape(-1, fold.shape[1])
    fold, part = lax.optimization_barrier((fold, part))
    part = add_rest(halve(part, me, 2))
    rows = part.shape[0]
    held, order = [fold], [0]
    step = n_cell // 2
    while step:
        held = held + [swap(value, "cell", step) for value in held]
        order = order + [value ^ step for value in order]
        step //= 2
    held, part = lax.optimization_barrier((held, part))
    gram, scale = first_block(cell.reshape(1), [held[order.index(at)] for at in range(n_cell)], term_index.shape[0])
    for block in range(1, blocks):
        if block <= 2:
            part = join(part, (4, 1)[block - 1])
            gram, part = lax.optimization_barrier((gram, part))
        gram = next_block(gram, block)
    pieces = [part, swap(part, "samp", 2)]
    where = jnp.stack([spot, cell])
    given = (where, gram, scale, pieces, rows, block_group, points.shape[1] * n_samp, n_cell)
    far = solve(*given, tuple(range(1, n_cell)))
    came = [swap(value, "cell", 1 + at) for at, value in enumerate(far)]
    near, sobol = solve(*given, (0,), far)
    shares = [near] + came
    return (join_columns(cell.reshape(1), shares), sobol)


def solution(mesh):
    placed = (P(None, "samp"), P("samp", "cell"), P(), P())
    return jax.shard_map(
        on_device,
        mesh=mesh,
        in_specs=placed,
        out_specs=(P("cell", None), P(None, "cell")),
        check_vma=False,
    )
```
